32 devices in a mesh: dp: 16 (over z, y, x), mp: 2 (over core).
Axes of the slice: x: 2, y: 2, z: 4, core: 2. Of those that a mesh axis runs over, the one named last changes fastest.
Arguments:
- tokens: bfloat16 [2, 4096, 1024], P(None, 'dp', 'mp'), may hold values from -6 to 6
- class_ids: int32 [2, 16], replicated, may hold values from 0 to 999
- final_scale: int32 [2, 16, 16], P(None, 'dp'), may hold values from -1 to 6, as said below
- row_slots: int32 [2, 16, 256], P(None, 'dp'), may hold values from 0 to 255, as said below
- class_table: bfloat16 [1000, 1024], P(None, 'dp'), may hold values from -6 to 6
- ada_weight: bfloat16 [1024, 6, 1024], P('dp'), may hold values from -0.1875 to 0.1875
- ada_bias: float32 [6, 1024], P(None, 'mp'), may hold values from -1.75 to 1.75
- qkv_weight: bfloat16 [1024, 3, 1024], P(None, None, 'mp'), may hold values from -0.1875 to 0.1875
- qv_bias: float32 [2, 1024], P(None, 'mp'), may hold values from -0.875 to 0.875
- log_scale: float32 [16], P('mp'), may hold values from 2 to 3
- proj_weight: bfloat16 [1024, 1024], P('mp'), may hold values from -0.75 to 0.75
- proj_bias: float32 [1024], P('mp'), may hold values from -1.25 to 1.25
- fc1_weight: bfloat16 [1024, 4096], P(None, 'mp'), may hold values from -0.1875 to 0.1875
- fc1_bias: float32 [4096], P('mp'), may hold values from -1.75 to 1.75
- fc2_weight: bfloat16 [4096, 1024], P('mp'), may hold values from -0.09375 to 0.09375
- fc2_bias: float32 [1024], P('mp'), may hold values from -1.25 to 1.25
- out_grad: bfloat16 [2, 4096, 1024], P(None, 'dp', 'mp'), may hold values from -6 to 6
Outputs:
- output: bfloat16 [2, 4096, 1024], P(None, 'dp', 'mp')
- tokens_grad: bfloat16 [2, 4096, 1024], P(None, 'dp', 'mp')
- class_table_grad: float32 [1000, 1024], P(None, 'dp')
- ada_weight_grad: float32 [1024, 6, 1024], P('dp')
- ada_bias_grad: float32 [6, 1024], replicated
- qkv_weight_grad: float32 [1024, 3, 1024], P('dp', None, 'mp')
- qv_bias_grad: float32 [2, 1024], P(None, 'mp')
- log_scale_grad: float32 [16], P('mp')
- proj_weight_grad: float32 [1024, 1024], P('mp', 'dp')
- proj_bias_grad: float32 [1024], P('mp')
- fc1_weight_grad: float32 [1024, 4096], P('dp', 'mp')
- fc1_bias_grad: float32 [4096], P('mp')
- fc2_weight_grad: float32 [4096, 1024], P('mp', 'dp')
- fc2_bias_grad: float32 [1024], P('mp')
The draws below stay inside these ranges and needn't reach their ends.
Inputs may be any that keep to these rules, and one draw needn't show every extreme that they name: `final_scale`: items fill positions from 0 in order, lengths sum to at most 256; the first item of each row has index 4 or more; -1 marks an empty place and only empty places follow it; in each micro-batch some row's first item has index 6. `row_slots`: each row's entries are a permutation of its positions; slots 0, 128 and 255 hold positions 0, 1 and 2.
All inputs are finite; a program needn't handle non-finite values.
Results may differ from the reference program's by a relative error of at most 0.025.
Values may be sent and summed in bfloat16 or wider, within the bound.
No kernel may reach another device: no remote copies, remote signals or barrier semaphores. Data moves between devices by JAX's collectives and lax.ppermute only.
A program may use at most 192 MiB of HBM per device.

```python
import math
import jax
import jax.numpy as jnp
from jax import lax

D = 1024
HEADS = 16
HEAD_DIM = 64
FF = 4096
CLASSES = 1000
ROW = 256
MICRO = 2
SCALES = 7
ITEMS = 16
GROUPS = 16
ROWS = 16
TOKENS = 4096
N_DP = 16


scale_ends = (1, 5, 14, 30, 55, 91, 155, 255, 424, 680)


def draw_final_scale(key, part):
    key = jax.random.fold_in(key, 11)
    first_key, row_key, rest_key = jax.random.split(key, 3)
    leading = jax.random.randint(first_key, (MICRO, ROWS, 1), SCALES - 3, SCALES)
    chosen = jax.random.randint(row_key, (MICRO, 1, 1), 0, ROWS)
    row_ids = jnp.arange(ROWS, dtype=jnp.int32)[None, :, None]
    leading = jnp.where(row_ids == chosen, SCALES - 1, leading)
    others = jax.random.randint(rest_key, (MICRO, ROWS, ITEMS - 1), 0, SCALES)
    picked = jnp.concatenate([leading, others], axis=2).astype(jnp.int32)
    length_table = jnp.asarray(scale_ends, dtype=jnp.int32)
    matches = picked[..., None] == jnp.arange(len(scale_ends), dtype=jnp.int32)[None, None, None, :]
    lengths = jnp.sum(jnp.where(matches, length_table, 0), axis=3)
    filled = jnp.cumsum(lengths, axis=2)
    return jnp.where(filled <= ROW, picked, -1).astype(jnp.int32)


def draw_row_slots(key, part):
    key = jax.random.fold_in(key, 23)
    row_total = MICRO * ROWS
    row_keys = jax.random.split(key, row_total)
    shuffled = jax.vmap(lambda single: jax.random.permutation(single, ROW - 3))(row_keys) + 3
    middle = ROW // 2
    fixed_zero = jnp.zeros((row_total, 1), jnp.int32)
    slots = jnp.concatenate([fixed_zero, shuffled[:, :middle - 1], fixed_zero + 1, shuffled[:, middle - 1:], fixed_zero + 2], axis=1)
    return slots.reshape(MICRO, ROWS, ROW).astype(jnp.int32)


def place_ends(values, stream_key, smallest, top_value):
    longest = values.shape.index(max(values.shape))
    spots = []
    for shift in (0, 1):
        where = [jax.random.randint(jax.random.fold_in(stream_key, axis), (), 0, length) for axis, length in enumerate(values.shape)]
        where[longest] = (where[longest] + shift) % values.shape[longest]
        spots.append(tuple(where))
    return values.at[spots[0]].set(smallest).at[spots[1]].set(top_value)


def level_of(rng, shape, cuts, least, largest):
    factor_of, own = 1.0, jax.random.fold_in(rng, 6)
    for dim, shards_of in cuts:
        draws = jnp.exp(jax.random.uniform(jax.random.fold_in(own, dim), (shards_of,), jnp.float32, least / len(cuts), largest / len(cuts)))
        factor_of = factor_of * jnp.repeat(draws, shape[dim] // shards_of).reshape([-1 if axis == dim else 1 for axis in range(len(shape))])
    return factor_of


def noise(stream_key, shape, width, most, cuts=(), kind=jnp.bfloat16):
    factor_of = level_of(stream_key, shape, cuts, -0.22, 0.18) if cuts else 1.0
    values = jax.random.normal(stream_key, shape, jnp.float32) * width * factor_of
    return jnp.minimum(jnp.maximum(values, -most), most).astype(kind)


def setup_inputs(seed: int = 0) -> dict:
    keys = jax.random.split(jax.random.key(seed), 18)
    return {
        "tokens": noise(keys[0], (MICRO, TOKENS, D), 1.0, 6.0, ((1, 16), (2, 2))),
        "class_ids": place_ends(jax.random.randint(keys[1], (MICRO, GROUPS), 0, CLASSES), jax.random.fold_in(keys[1], 1), 0, CLASSES - 1).astype(jnp.int32),
        "final_scale": draw_final_scale(jax.random.fold_in(keys[17], 71), 0),
        "row_slots": draw_row_slots(jax.random.fold_in(keys[17], 71), 0),
        "class_table": noise(keys[4], (CLASSES, D), 1.0, 6.0, ((1, 16),)),
        "ada_weight": noise(keys[5], (D, 6, D), D ** -0.5, 0.1875, ((0, 16),)),
        "ada_bias": noise(keys[6], (6, D), 0.3, 1.75, ((1, 2),), jnp.float32),
        "qkv_weight": noise(keys[7], (D, 3, D), D ** -0.5, 0.1875, ((2, 2),)),
        "qv_bias": noise(keys[8], (2, D), 0.15, 0.875, ((1, 2),), jnp.float32),
        "log_scale": jnp.clip(2.0 + 1.0 * jax.random.uniform(keys[9], (HEADS,), jnp.float32) ** level_of(keys[9], (HEADS,), ((0, 2),), -0.2, 0.2), 2.0, 3.0),
        "proj_weight": noise(keys[10], (D, D), (D // 16) ** -0.5, 0.75, ((0, 2),)),
        "proj_bias": noise(keys[11], (D,), 0.2, 1.25, ((0, 2),), jnp.float32),
        "fc1_weight": noise(keys[12], (D, FF), D ** -0.5, 0.1875, ((1, 2),)),
        "fc1_bias": noise(keys[13], (FF,), 0.3, 1.75, ((0, 2),), jnp.float32),
        "fc2_weight": noise(keys[14], (FF, D), FF ** -0.5, 0.09375, ((0, 2),)),
        "fc2_bias": noise(keys[15], (D,), 0.2, 1.25, ((0, 2),), jnp.float32),
        "out_grad": noise(keys[16], (MICRO, TOKENS, D), 1.0, 6.0, ((1, 16), (2, 2))),
    }


scale_ends = (1, 5, 14, 30, 55, 91, 155, 255, 424, 680)
norm_eps = 1e-06
unit_eps = 1e-06
masked_score = -1e+30
highest = lax.Precision.HIGHEST

@jax.custom_vjp
def low(v):
    return lax.optimization_barrier(v.astype(jnp.bfloat16)).astype(jnp.float32)

@jax.custom_vjp
def low_back(v):
    return v

def low_keep(v):
    return (low(v), None)

def low_pass(kept, grad):
    return (grad,)

def back_keep(v):
    return (v, None)

def back_low(kept, grad):
    return (low(grad),)
low.defvjp(low_keep, low_pass)
low_back.defvjp(back_keep, back_low)

def slot_layout(final_row, slots_row):
    ends_table = jnp.asarray(scale_ends, dtype=jnp.int32)
    levels_count = ends_table.shape[0]
    chosen = final_row[:, None] == jnp.arange(levels_count, dtype=jnp.int32)[None, :]
    lengths = lax.optimization_barrier(jnp.sum(jnp.where(chosen, ends_table[None, :], 0), axis=1)).astype(jnp.int32)
    item_ends = jnp.cumsum(lengths).astype(jnp.int32)
    places = jnp.arange(slots_row.shape[0], dtype=jnp.int32)
    passed = places[:, None] >= item_ends[None, :]
    segment = lax.optimization_barrier(jnp.sum(passed, axis=1)).astype(jnp.int32)
    item_start = lax.optimization_barrier(jnp.sum(jnp.where(passed, lengths[None, :], 0), axis=1)).astype(jnp.int32)
    offset = places - item_start
    level_id = lax.optimization_barrier(jnp.sum(offset[:, None] >= ends_table[None, :], axis=1)).astype(jnp.int32)
    level_id = jnp.where(segment == final_row.shape[0], 0, level_id).astype(jnp.int32)
    return (jnp.take(segment, slots_row, axis=0), jnp.take(level_id, slots_row, axis=0))

def layer_normal(values):
    mean_value = lax.optimization_barrier(jnp.mean(values, axis=-1, keepdims=True))
    spread = lax.optimization_barrier(jnp.mean(values * values, axis=-1, keepdims=True)) - mean_value * mean_value
    return (values - mean_value) * lax.rsqrt(spread + norm_eps)

def attend_group(queries, key_heads, value_heads, segments, levels):
    row_len = segments.shape[1]
    block_rows = min(512, row_len)
    block_count = row_len // block_rows

    def one_block(block_index):
        first_row = block_index * block_rows
        query_block = lax.dynamic_slice_in_dim(queries, first_row, block_rows, 1)
        seg_block = lax.dynamic_slice_in_dim(segments, first_row, block_rows, 1)
        level_block = lax.dynamic_slice_in_dim(levels, first_row, block_rows, 1)
        scores = jnp.einsum('rqhd,rkhd->rhqk', query_block, key_heads, precision=highest)
        scores = low_back(scores)
        allowed = (seg_block[:, None, :, None] == segments[:, None, None, :]) & (levels[:, None, None, :] <= level_block[:, None, :, None])
        masked = jnp.where(allowed, scores, masked_score)
        row_peak = lax.optimization_barrier(jnp.max(masked, axis=-1, keepdims=True))
        raised = jnp.exp(masked - row_peak)
        weights = low(raised / lax.optimization_barrier(jnp.sum(raised, axis=-1, keepdims=True)))
        return jnp.einsum('rhqk,rkhd->rqhd', weights, value_heads, precision=highest)
    blocks = lax.map(jax.checkpoint(one_block), jnp.arange(block_count, dtype=jnp.int32))
    return jnp.moveaxis(blocks, 0, 1).reshape(queries.shape)

def group_block(x_group, seg_group, level_group, mods, weights):
    qkv_mat, qkv_shift, log_scale, proj_mat, proj_shift, fc1_mat, fc1_shift, fc2_mat, fc2_shift = weights
    gamma_one, gamma_two = (mods[:, None, 0], mods[:, None, 1])
    scale_one, scale_two = (mods[:, None, 2], mods[:, None, 3])
    shift_one, shift_two = (mods[:, None, 4], mods[:, None, 5])
    group_rows, row_len = (x_group.shape[0], x_group.shape[1])
    first_in = low(layer_normal(x_group) * (1.0 + scale_one) + shift_one)
    projected = jnp.einsum('rld,dte->rlte', first_in, qkv_mat, precision=highest) + qkv_shift
    projected = low_back(projected)
    queries = projected[:, :, 0].reshape(group_rows, row_len, HEADS, HEAD_DIM)
    key_heads = projected[:, :, 1].reshape(group_rows, row_len, HEADS, HEAD_DIM)
    value_heads = projected[:, :, 2].reshape(group_rows, row_len, HEADS, HEAD_DIM)
    queries = queries * lax.rsqrt(lax.optimization_barrier(jnp.sum(queries * queries, axis=-1, keepdims=True)) + unit_eps) * jnp.exp(log_scale)[:, None]
    key_heads = key_heads * lax.rsqrt(lax.optimization_barrier(jnp.sum(key_heads * key_heads, axis=-1, keepdims=True)) + unit_eps)
    queries = low_back(low(queries))
    key_heads = low_back(low(key_heads))
    value_heads = low_back(low(value_heads))
    mixed_rows = attend_group(queries, key_heads, value_heads, seg_group, level_group)
    mixed_rows = low_back(low(mixed_rows)).reshape(group_rows, row_len, D)
    attention_out = low_back(jnp.einsum('rld,de->rle', mixed_rows, proj_mat, precision=highest) + proj_shift)
    middle = x_group + gamma_one * attention_out
    second_in = low(layer_normal(middle) * (1.0 + scale_two) + shift_two)
    hidden_pre = low_back(jnp.einsum('rld,df->rlf', second_in, fc1_mat, precision=highest) + fc1_shift)
    hidden_act = low(jax.nn.gelu(hidden_pre, approximate=True))
    branch_out = low_back(jnp.einsum('rlf,fd->rld', hidden_act, fc2_mat, precision=highest) + fc2_shift)
    return middle + gamma_two * branch_out

def to_rows(array):
    share = ROW // N_DP
    micro_count = array.shape[0]
    shaped = array.reshape(micro_count, N_DP, N_DP, share, D)
    return jnp.transpose(shaped, (0, 2, 1, 3, 4)).reshape(micro_count, N_DP, ROW, D)

def to_groups(array):
    share = ROW // N_DP
    micro_count = array.shape[0]
    shaped = array.reshape(micro_count, N_DP, N_DP, share, D)
    return jnp.transpose(shaped, (0, 2, 1, 3, 4)).reshape(micro_count, N_DP * ROW, D)

def forward(tokens_f, table_f, ada_mat, ada_shift, qkv_mat, qv_shift, log_scale, proj_mat, proj_shift, fc1_mat, fc1_shift, fc2_mat, fc2_shift, class_ids, segments, levels):
    condition = jnp.take(table_f, class_ids, axis=0)
    lifted = low(jax.nn.silu(condition))
    ada = jnp.einsum('mgi,isd->mgsd', lifted, ada_mat, precision=highest) + ada_shift
    qkv_shift = jnp.stack([qv_shift[0], jnp.zeros_like(qv_shift[0]), qv_shift[1]])
    weights = (qkv_mat, qkv_shift, log_scale, proj_mat, proj_shift, fc1_mat, fc1_shift, fc2_mat, fc2_shift)
    rows_in = to_rows(tokens_f)
    group_rows = math.gcd(N_DP, max(1, 4096 // ROW))
    results = []
    for batch_index in range(MICRO):
        mods_shaped = ada[batch_index].reshape(N_DP // group_rows, group_rows, 6, D)
        x_shaped = rows_in[batch_index].reshape(N_DP // group_rows, group_rows, ROW, D)
        seg_shaped = segments[batch_index].reshape(N_DP // group_rows, group_rows, ROW)
        level_shaped = levels[batch_index].reshape(N_DP // group_rows, group_rows, ROW)

        def scan_step(carried, pieces):
            return (carried, jax.checkpoint(group_block)(pieces[0], pieces[1], pieces[2], pieces[3], weights))
        _, stacked = lax.scan(scan_step, jnp.zeros((), jnp.float32), (x_shaped, seg_shaped, level_shaped, mods_shaped))
        results.append(stacked.reshape(N_DP, ROW, D))
    return to_groups(jnp.stack(results))

def reference(tokens, class_ids, final_scale, row_slots, class_table, ada_weight, ada_bias, qkv_weight, qv_bias, log_scale, proj_weight, proj_bias, fc1_weight, fc1_bias, fc2_weight, fc2_bias, out_grad):
    seg_flat, level_flat = jax.vmap(slot_layout)(final_scale.reshape(MICRO * N_DP, ITEMS), row_slots.reshape(MICRO * N_DP, ROW))
    segments = seg_flat.reshape(MICRO, N_DP, ROW)
    levels = level_flat.reshape(MICRO, N_DP, ROW)
    floats = (tokens.astype(jnp.float32), class_table.astype(jnp.float32), ada_weight.astype(jnp.float32), ada_bias, qkv_weight.astype(jnp.float32), qv_bias, log_scale, proj_weight.astype(jnp.float32), proj_bias, fc1_weight.astype(jnp.float32), fc1_bias, fc2_weight.astype(jnp.float32), fc2_bias)

    def wrapped(*inputs):
        return forward(*inputs, class_ids, segments, levels)
    result, pullback = jax.vjp(wrapped, *floats)
    grads = pullback(out_grad.astype(jnp.float32))
    return (result.astype(jnp.bfloat16), grads[0].astype(jnp.bfloat16), grads[1], grads[2], grads[3], grads[4], grads[5], grads[6], grads[7], grads[8], grads[9], grads[10], grads[11], grads[12])
```

```python
import functools

import jax
import jax.numpy as jnp
from jax import lax
from jax.experimental import pallas as pl
from jax.experimental.pallas import tpu as pltpu
from jax.sharding import PartitionSpec as P

HEAD_DIM = 64
LANES = 128
scale_ends = (1, 5, 14, 30, 55, 91, 155, 255, 424, 680)
norm_eps = 1e-06
unit_eps = 1e-06
bf16 = jnp.bfloat16
f32 = jnp.float32
gelu_c = 0.7978845608028654
gelu_a = 0.044715


def slot_layout(final_row, slots_row):
    ends_table = jnp.asarray(scale_ends, dtype=jnp.int32)
    chosen = final_row[:, None] == jnp.arange(len(scale_ends), dtype=jnp.int32)[None, :]
    lengths = jnp.sum(jnp.where(chosen, ends_table[None, :], 0), axis=1)
    items = final_row.shape[0]
    before = jnp.arange(items)[:, None] <= jnp.arange(items)[None, :]
    item_ends = jnp.sum(jnp.where(before, lengths[:, None], 0), axis=0)
    passed = slots_row[:, None] >= item_ends[None, :]
    segment = jnp.sum(passed.astype(jnp.int32), axis=1)
    item_start = jnp.sum(jnp.where(passed, lengths[None, :], 0), axis=1)
    offset = slots_row - item_start
    level = jnp.sum((offset[:, None] >= ends_table[None, :]).astype(jnp.int32), axis=1)
    return segment, jnp.where(segment == items, 0, level)


def dot(a, b):
    return jnp.dot(a, b, preferred_element_type=f32)


def dot_nt(a, b):
    return lax.dot_general(a, b, (((1,), (1,)), ((), ())), preferred_element_type=f32)


def dot_tn(a, b):
    return lax.dot_general(a, b, (((0,), (0,)), ((), ())), preferred_element_type=f32)


def half_sums(values, first):
    low = jnp.sum(jnp.where(first, values, 0.0), axis=1, keepdims=True)
    high = jnp.sum(jnp.where(first, 0.0, values), axis=1, keepdims=True)
    return jnp.where(first, low, high)


def attend_kernel(qkv_ref, bias_ref, mult_ref, mask_ref, q_out, k_out, v_out, p_out, mixed_out):
    rows, width = mixed_out.shape
    first = lax.broadcasted_iota(jnp.int32, (rows, LANES), 1) < HEAD_DIM
    mask = mask_ref[...]
    for pair in range(width // LANES):
        cols = slice(pair * LANES, (pair + 1) * LANES)

        def part(index):
            at = slice(index * width + pair * LANES, index * width + (pair + 1) * LANES)
            return qkv_ref[:, at] + bias_ref[:, at]

        queries, keys = part(0), part(1)
        query_unit = queries * lax.rsqrt(half_sums(queries * queries, first) + unit_eps)
        key_unit = keys * lax.rsqrt(half_sums(keys * keys, first) + unit_eps)
        q_low = (query_unit * mult_ref[:, cols]).astype(bf16)
        k_low = key_unit.astype(bf16)
        v_low = part(2).astype(bf16)
        q_out[:, cols] = q_low
        k_out[:, cols] = k_low
        v_out[:, cols] = v_low
        mixed = []
        for head in range(2):
            own = first if head == 0 else jnp.logical_not(first)
            scores = dot_nt(jnp.where(own, q_low, jnp.zeros_like(q_low)), k_low)
            raised = jnp.exp(scores) * mask
            weights = (raised / jnp.sum(raised, axis=1, keepdims=True)).astype(bf16)
            p_out[2 * pair + head] = weights
            mixed.append(dot(weights, v_low))
        mixed_out[:, cols] = jnp.where(first, mixed[0], mixed[1]).astype(bf16)


def attend_back_kernel(
    qkv_ref, bias_ref, mult_ref, q_ref, k_ref, v_ref, p_ref, grad_ref, qkv_out, scale_out
):
    rows, width = grad_ref.shape
    first = lax.broadcasted_iota(jnp.int32, (rows, LANES), 1) < HEAD_DIM
    for pair in range(width // LANES):
        cols = slice(pair * LANES, (pair + 1) * LANES)
        grad = grad_ref[:, cols]
        q_low, k_low, v_low = q_ref[:, cols], k_ref[:, cols], v_ref[:, cols]
        parts = []
        for head in range(2):
            own = first if head == 0 else jnp.logical_not(first)
            probs_low = p_ref[2 * pair + head]
            probs = probs_low.astype(f32)
            prob_grad = dot_nt(jnp.where(own, grad, jnp.zeros_like(grad)), v_low)
            centred = jnp.sum(prob_grad * probs, axis=1, keepdims=True)
            score_grad = (probs * (prob_grad - centred)).astype(bf16)
            parts.append(
                (dot(score_grad, k_low), dot_tn(score_grad, q_low), dot_tn(probs_low, grad))
            )
        query_grad, key_grad, value_grad = [
            jnp.where(first, low, high).astype(bf16) for low, high in zip(*parts)
        ]
        query_grad = query_grad.astype(f32)
        key_grad = key_grad.astype(f32)

        def part(index):
            at = slice(index * width + pair * LANES, index * width + (pair + 1) * LANES)
            return qkv_ref[:, at] + bias_ref[:, at]

        queries, keys = part(0), part(1)
        query_scale = lax.rsqrt(half_sums(queries * queries, first) + unit_eps)
        key_scale = lax.rsqrt(half_sums(keys * keys, first) + unit_eps)
        query_unit = queries * query_scale
        key_unit = keys * key_scale
        unit_grad = query_grad * mult_ref[:, cols]
        cross = unit_grad * query_unit
        scale_out[:, cols] = jnp.sum(cross, axis=0, keepdims=True)
        query_pre = query_scale * (unit_grad - query_unit * half_sums(cross, first))
        key_pre = key_scale * (key_grad - key_unit * half_sums(key_grad * key_unit, first))
        qkv_out[:, cols] = query_pre.astype(bf16)
        qkv_out[:, width + pair * LANES : width + (pair + 1) * LANES] = key_pre.astype(bf16)
        qkv_out[:, 2 * width + pair * LANES : 2 * width + (pair + 1) * LANES] = value_grad


def attend(qkv, bias, mult, mask):
    rows, width = qkv.shape[0], qkv.shape[1] // 3
    heads = width // HEAD_DIM
    wide = jax.ShapeDtypeStruct((rows, width), bf16)
    return pl.pallas_call(
        attend_kernel,
        out_shape=(wide, wide, wide, jax.ShapeDtypeStruct((heads, rows, rows), bf16), wide),
        compiler_params=pltpu.CompilerParams(vmem_limit_bytes=32 * 2**20),
        cost_estimate=pl.CostEstimate(
            flops=8 * heads * rows * rows * HEAD_DIM,
            bytes_accessed=16 * rows * width,
            transcendentals=heads * rows * rows,
        ),
    )(qkv, bias, mult, mask)


def attend_back(qkv, bias, mult, kept, grad):
    rows, width = grad.shape
    heads = width // HEAD_DIM
    return pl.pallas_call(
        attend_back_kernel,
        out_shape=(
            jax.ShapeDtypeStruct((rows, 3 * width), bf16),
            jax.ShapeDtypeStruct((1, width), f32),
        ),
        compiler_params=pltpu.CompilerParams(vmem_limit_bytes=32 * 2**20),
        cost_estimate=pl.CostEstimate(
            flops=20 * heads * rows * rows * HEAD_DIM,
            bytes_accessed=16 * rows * width,
            transcendentals=0,
        ),
    )(qkv, bias, mult, *kept, grad)


def normalize(values):
    mean = jnp.mean(values, axis=1, keepdims=True)
    spread = jnp.mean(values * values, axis=1, keepdims=True) - mean * mean
    scale = lax.rsqrt(spread + norm_eps)
    return (values - mean) * scale, scale


def norm_back(grad, normed, scale):
    return scale * (
        grad
        - jnp.mean(grad, axis=1, keepdims=True)
        - normed * jnp.mean(grad * normed, axis=1, keepdims=True)
    )


def gelu_parts(pre):
    square = pre * pre
    tanh = jnp.tanh(gelu_c * (pre + gelu_a * pre * square))
    value = 0.5 * pre * (1.0 + tanh)
    slope = 0.5 * (1.0 + tanh) + 0.5 * pre * (1.0 - tanh * tanh) * gelu_c * (
        1.0 + 3.0 * gelu_a * square
    )
    return value, slope


def shards(
    tokens,
    class_ids,
    final_scale,
    row_slots,
    class_table,
    ada_weight,
    ada_bias,
    qkv_weight,
    qv_bias,
    log_scale,
    proj_weight,
    proj_bias,
    fc1_weight,
    fc1_bias,
    fc2_weight,
    fc2_bias,
    out_grad,
):
    groups = lax.axis_size("dp")
    bits = groups.bit_length() - 1
    here = lax.axis_index("dp")
    core = lax.axis_index("mp")
    micro, row_len, half = tokens.shape
    width = 2 * half
    share = row_len // groups
    heads = log_scale.shape[0]
    hidden = fc1_weight.shape[1]

    def swap(values):
        return lax.ppermute(values, "mp", [(0, 1), (1, 0)])

    def flip(values, bit):
        return lax.ppermute(values, "dp", [(i, i ^ (1 << bit)) for i in range(groups)])

    def in_order(own, other, axis):
        return jnp.where(
            core == 0,
            jnp.concatenate([own, other], axis),
            jnp.concatenate([other, own], axis),
        )

    qkv_own = qkv_weight.reshape(width, 3 * half)
    small = jnp.concatenate(
        [ada_bias.reshape(-1), qv_bias.reshape(-1), log_scale, proj_bias, fc1_bias, fc2_bias]
    )
    small_sizes = [6 * half, 2 * half, heads, half, hidden, half]

    def unpack(flat):
        starts = [sum(small_sizes[:i]) for i in range(7)]
        return [flat[starts[i] : starts[i + 1]] for i in range(6)]

    own_small, oth_small = unpack(small), unpack(swap(small))
    qkv_w = (qkv_own, swap(qkv_own))
    proj_w = (proj_weight, swap(proj_weight))
    fc1_w = (fc1_weight, swap(fc1_weight))
    fc2_w = (fc2_weight, swap(fc2_weight))
    ada_shift = in_order(own_small[0].reshape(6, half), oth_small[0].reshape(6, half), 1)
    proj_shift = in_order(own_small[3], oth_small[3], 0)
    fc2_shift = in_order(own_small[5], oth_small[5], 0)
    fc1_shift = (own_small[4], oth_small[4])
    qkv_shift = [
        jnp.concatenate([part[1][:half], jnp.zeros((half,), f32), part[1][half:]])[None]
        for part in (own_small, oth_small)
    ]
    head_mult = [
        jnp.repeat(jnp.exp(part[2]), HEAD_DIM)[None] for part in (own_small, oth_small)
    ]

    class_picks = (
        class_ids.reshape(-1)[:, None] == jnp.arange(class_table.shape[0], dtype=jnp.int32)[None, :]
    )
    condition = dot(class_picks.astype(bf16), class_table)
    lifted = jax.nn.silu(condition).astype(bf16)
    ada_half = lax.dynamic_slice_in_dim(ada_weight, core * half, half, 2)
    ada_terms = dot(lifted, ada_half.reshape(ada_half.shape[0], 6 * half)).astype(bf16)

    def by_target(values):
        return values.reshape(micro, groups, -1, half).swapaxes(0, 1).reshape(2 * groups, -1, half)

    def exchange(values):
        return lax.all_to_all(values, ("dp", "mp"), split_axis=0, concat_axis=0, tiled=True)

    def to_row(values):
        return (
            values.reshape(groups, 2, share, half).transpose(0, 2, 1, 3).reshape(row_len, width)
        )

    arrived = exchange(jnp.concatenate([by_target(tokens), by_target(ada_terms)], axis=1))
    resident = to_row(arrived[:, :share]).astype(f32)
    ada = (
        jnp.sum(arrived[:, share:].reshape(groups, 2, 6, half).astype(f32), axis=0)
        .transpose(1, 0, 2)
        .reshape(6, width)
        + ada_shift
    )
    gamma_one, gamma_two, scale_one, scale_two, shift_one, shift_two = [
        ada[index][None] for index in range(6)
    ]
    grad_out = to_row(exchange(by_target(out_grad))).astype(f32)

    segments, levels = slot_layout(
        lax.dynamic_index_in_dim(final_scale[:, 0], core, 0, keepdims=False),
        lax.dynamic_index_in_dim(row_slots[:, 0], core, 0, keepdims=False),
    )
    mask = (
        (segments[:, None] == segments[None, :]) & (levels[None, :] <= levels[:, None])
    ).astype(f32)

    normed_one, spread_one = normalize(resident)
    first_in = (normed_one * (1.0 + scale_one) + shift_one).astype(bf16)
    qkv = [dot(first_in, weight) for weight in qkv_w]
    attended = [
        attend(qkv[i], qkv_shift[i], head_mult[i], mask) for i in range(2)
    ]
    mixed = [part[4] for part in attended]
    attention_out = dot(mixed[0], proj_w[0]) + dot(mixed[1], proj_w[1]) + proj_shift[None]
    middle = resident + gamma_one * attention_out
    normed_two, spread_two = normalize(middle)
    second_in = (normed_two * (1.0 + scale_two) + shift_two).astype(bf16)
    pre = [dot(second_in, fc1_w[i]) + fc1_shift[i][None] for i in range(2)]
    gelus = [gelu_parts(values) for values in pre]
    act = [values[0].astype(bf16) for values in gelus]

    def paired(own, sent):
        return jnp.concatenate([own, swap(sent)], axis=0)

    def as_bits(grad):
        return grad.astype(bf16).reshape((2,) * bits + (width // groups, grad.shape[1]))

    def stage(part, left, bit, kind=bf16):
        axis = left.index(bit)
        mine = (here >> bit) & 1
        kept = lax.dynamic_index_in_dim(part, mine, axis, keepdims=False)
        sent = lax.dynamic_index_in_dim(part, 1 - mine, axis, keepdims=False)
        total = kept.astype(f32) + flip(sent, bit).astype(f32)
        return total.astype(kind), [b for b in left if b != bit]

    def scatter_sum(grad):
        parts = as_bits(grad)
        middle_col = grad.shape[1] // 2
        done = []
        for piece, order in ((parts[..., :middle_col], (0, 1)), (parts[..., middle_col:], (1, 0))):
            left = list(range(bits - 1, -1, -1))
            for bit in order:
                piece, left = stage(piece, left, bit)
            done.append(piece)
        total = jnp.concatenate(done, axis=-1)
        for bit in range(2, bits):
            total, left = stage(total, left, bit, f32 if bit == bits - 1 else bf16)
        return total

    grad_branch = (gamma_two * grad_out).astype(bf16)
    branch_pair = paired(grad_branch, grad_branch)
    act_pair = paired(act[0], act[1])
    fc2_sum = scatter_sum(dot_tn(branch_pair, act_pair))

    branch = dot(act[0], fc2_w[0]) + dot(act[1], fc2_w[1]) + fc2_shift[None]
    output = (middle + gamma_two * branch).astype(bf16)

    grad_gamma_two = jnp.sum(grad_out * branch, axis=0)
    grad_pre = [
        (dot_nt(grad_branch, fc2_w[i]) * gelus[i][1]).astype(bf16) for i in range(2)
    ]
    second_pair = paired(second_in, second_in)
    pre_pair = paired(grad_pre[0], grad_pre[1])
    fc1_sum = scatter_sum(dot_tn(second_pair, pre_pair))
    grad_second = dot_nt(grad_pre[0], fc1_w[0]) + dot_nt(grad_pre[1], fc1_w[1])
    grad_scale_two = jnp.sum(grad_second * normed_two, axis=0)
    grad_shift_two = jnp.sum(grad_second, axis=0)
    grad_middle = grad_out + norm_back(grad_second * (1.0 + scale_two), normed_two, spread_two)
    grad_gamma_one = jnp.sum(grad_middle * attention_out, axis=0)
    grad_attention = (gamma_one * grad_middle).astype(bf16)
    grad_mixed = [dot_nt(grad_attention, weight).astype(bf16) for weight in proj_w]
    back = [
        attend_back(qkv[i], qkv_shift[i], head_mult[i], attended[i][:4], grad_mixed[i])
        for i in range(2)
    ]
    grad_qkv = [part[0] for part in back]
    attention_pair = paired(grad_attention, grad_attention)
    mixed_pair = paired(mixed[0], mixed[1])
    first_pair = paired(first_in, first_in)
    qkv_pair = paired(grad_qkv[0], grad_qkv[1])
    qkv_sum = scatter_sum(
        jnp.concatenate([dot_tn(first_pair, qkv_pair), dot_tn(attention_pair, mixed_pair)], axis=1)
    )
    grad_first = dot_nt(grad_qkv[0], qkv_w[0]) + dot_nt(grad_qkv[1], qkv_w[1])
    grad_scale_one = jnp.sum(grad_first * normed_one, axis=0)
    grad_shift_one = jnp.sum(grad_first, axis=0)
    tokens_grad = (
        grad_middle + norm_back(grad_first * (1.0 + scale_one), normed_one, spread_one)
    ).astype(bf16)

    row_grads = jnp.stack(
        [
            grad_gamma_one,
            grad_gamma_two,
            grad_scale_one,
            grad_scale_two,
            grad_shift_one,
            grad_shift_two,
        ]
    ).astype(bf16)
    scale_terms = [jnp.sum(part[1].reshape(heads, HEAD_DIM), axis=1) for part in back]
    scale_sum = scale_terms[0] + swap(scale_terms[1])
    own_cols = core * half

    def own_half(values):
        return lax.dynamic_slice_in_dim(values, own_cols, half, 1)

    bias_sum = jnp.concatenate(
        [
            jnp.sum(qkv_pair[:, :half].astype(f32), axis=0),
            jnp.sum(qkv_pair[:, 2 * half :].astype(f32), axis=0),
            jnp.sum(own_half(attention_pair).astype(f32), axis=0),
            jnp.sum(pre_pair.astype(f32), axis=0),
            jnp.sum(own_half(branch_pair).astype(f32), axis=0),
            scale_sum,
        ]
    )
    gathered = row_grads.reshape(1, 6 * width)
    for bit in range(bits):
        rounded = bias_sum.astype(bf16)
        came = flip(jnp.concatenate([gathered.reshape(-1), rounded]), bit)
        count = gathered.size
        theirs = came[:count].reshape(gathered.shape)
        mine = (here >> bit) & 1
        gathered = jnp.where(
            mine == 0,
            jnp.concatenate([gathered, theirs], 0),
            jnp.concatenate([theirs, gathered], 0),
        )
        bias_sum = rounded.astype(f32) + came[count:].astype(f32)
    gathered = in_order(gathered, swap(gathered), 0)

    ada_weight_grad = dot_tn(lifted, gathered).reshape(ada_weight.shape)
    ada_bias_grad = jnp.sum(gathered.astype(f32), axis=0).reshape(6, width)
    grad_lifted = dot_nt(gathered, ada_weight.reshape(ada_weight.shape[0], 6 * width))
    _, silu_pull = jax.vjp(jax.nn.silu, condition)
    table_grad = lax.dot_general(
        class_picks.astype(f32),
        silu_pull(grad_lifted)[0],
        (((0,), (0,)), ((), ())),
        precision=lax.Precision.HIGHEST,
    )

    def to_target(values):
        return (
            values.reshape(groups, share, 2, half).transpose(0, 2, 1, 3).reshape(-1, share, half)
        )

    returned = exchange(jnp.concatenate([to_target(output), to_target(tokens_grad)], axis=1))

    def from_rows(values):
        return values.reshape(groups, 2, share, half).swapaxes(0, 1).reshape(2, row_len, half)

    ends = [half, 2 * half, 3 * half, 3 * half + hidden, 4 * half + hidden]
    return (
        from_rows(returned[:, :share]),
        from_rows(returned[:, share:]),
        table_grad,
        ada_weight_grad,
        ada_bias_grad,
        qkv_sum[:, : 3 * half].reshape(-1, 3, half),
        bias_sum[: ends[1]].reshape(2, half),
        bias_sum[ends[4] :],
        qkv_sum[:, 3 * half :].T,
        bias_sum[ends[1] : ends[2]],
        fc1_sum,
        bias_sum[ends[2] : ends[3]],
        fc2_sum.T,
        bias_sum[ends[3] : ends[4]],
    )


def solution(mesh):
    placed = (
        P(None, "dp", "mp"),
        P(),
        P(None, "dp", None),
        P(None, "dp", None),
        P(None, "dp"),
        P("dp", None, None),
        P(None, "mp"),
        P(None, None, "mp"),
        P(None, "mp"),
        P("mp"),
        P("mp", None),
        P("mp"),
        P(None, "mp"),
        P("mp"),
        P("mp", None),
        P("mp"),
        P(None, "dp", "mp"),
    )
    return jax.shard_map(
        shards,
        mesh=mesh,
        in_specs=placed,
        out_specs=(
            P(None, "dp", "mp"),
            P(None, "dp", "mp"),
            P(None, "dp"),
            P("dp", None, None),
            P(),
            P("dp", None, "mp"),
            P(None, "mp"),
            P("mp"),
            P("mp", "dp"),
            P("mp"),
            P("dp", "mp"),
            P("mp"),
            P("mp", "dp"),
            P("mp"),
        ),
        check_vma=False,
    )
```

```python
import functools

import jax
import jax.numpy as jnp
from jax import lax
from jax.experimental import pallas as pl
from jax.experimental.pallas import tpu as pltpu
from jax.sharding import PartitionSpec as P

HEAD_DIM = 64
LANES = 128
scale_ends = (1, 5, 14, 30, 55, 91, 155, 255, 424, 680)
norm_eps = 1e-06
unit_eps = 1e-06
bf16 = jnp.bfloat16
f32 = jnp.float32
gelu_c = 0.7978845608028654
gelu_a = 0.044715


def slot_layout(final_row, slots_row):
    ends_table = jnp.asarray(scale_ends, dtype=jnp.int32)
    chosen = final_row[:, None] == jnp.arange(len(scale_ends), dtype=jnp.int32)[None, :]
    lengths = jnp.sum(jnp.where(chosen, ends_table[None, :], 0), axis=1)
    items = final_row.shape[0]
    before = jnp.arange(items)[:, None] <= jnp.arange(items)[None, :]
    item_ends = jnp.sum(jnp.where(before, lengths[:, None], 0), axis=0)
    passed = slots_row[:, None] >= item_ends[None, :]
    segment = jnp.sum(passed.astype(jnp.int32), axis=1)
    item_start = jnp.sum(jnp.where(passed, lengths[None, :], 0), axis=1)
    offset = slots_row - item_start
    level = jnp.sum((offset[:, None] >= ends_table[None, :]).astype(jnp.int32), axis=1)
    return segment, jnp.where(segment == items, 0, level)


def dot(a, b):
    return jnp.dot(a, b, preferred_element_type=f32)


def dot_nt(a, b):
    return lax.dot_general(a, b, (((1,), (1,)), ((), ())), preferred_element_type=f32)


def dot_tn(a, b):
    return lax.dot_general(a, b, (((0,), (0,)), ((), ())), preferred_element_type=f32)


def half_sums(values, first):
    low = jnp.sum(jnp.where(first, values, 0.0), axis=1, keepdims=True)
    high = jnp.sum(jnp.where(first, 0.0, values), axis=1, keepdims=True)
    return jnp.where(first, low, high)


def head_parts(queries, keys, mult, first):
    query_scale = lax.rsqrt(half_sums(queries * queries, first) + unit_eps)
    key_scale = lax.rsqrt(half_sums(keys * keys, first) + unit_eps)
    return queries * query_scale * mult, keys * key_scale, query_scale, key_scale


def start_copies(pairs, sems):
    copies = [pltpu.make_async_copy(src, dst, sems.at[i]) for i, (src, dst) in enumerate(pairs)]
    for copy in copies:
        copy.start()
    return copies


def wait_all(copies):
    for copy in copies:
        copy.wait()


def tiles(size, most):
    tile = min(most, size)
    return [slice(start, start + tile) for start in range(0, size, tile)]


def forward_kernel(
    x_ref, mods, qkv_bias, mult, mask_ref, proj_bias, fc1_bias, *refs
):
    weights, outs, held, rest = split_refs(refs, [10, 17, 17])
    qkv_w, proj_w, fc1_w, qkv_s, in_sems, out_sems = rest
    copies = start_copies(
        [(weights[i], qkv_w.at[i // 3, i % 3]) for i in range(6)]
        + [(weights[6 + i], proj_w.at[i]) for i in range(2)]
        + [(weights[8 + i], fc1_w.at[i]) for i in range(2)],
        in_sems,
    )
    leaving = []

    def leave(index, *at):
        src, dst = held[index], outs[index]
        if at:
            src, dst = src.at[at], dst.at[at]
        copy = pltpu.make_async_copy(src, dst, out_sems.at[len(leaving)])
        copy.start()
        leaving.append(copy)

    h1, qn_out, kn_out, v_out, rq_out, rk_out, p_out, mixed0, mixed1, attn_out = held[:10]
    middle_out, h2_out, act0, act1a, act1b, slope0, slope1 = held[10:]
    rows, width = x_ref.shape
    half = width // 2
    x = x_ref[...].astype(f32)
    h1[...] = (normalize(x)[0] * (1.0 + mods[2:3, :]) + mods[4:5, :]).astype(bf16)
    leave(0)
    first = lax.broadcasted_iota(jnp.int32, (rows, LANES), 1) < HEAD_DIM
    mask = mask_ref[...]
    heads = half // HEAD_DIM
    for side, mixed_out in enumerate((mixed0, mixed1)):
        for part in range(3):
            copies[3 * side + part].wait()
            at = slice(part * half, (part + 1) * half)
            qkv_s[:, at] = dot(h1[...], qkv_w[side, part]) + qkv_bias[side : side + 1, at]
        for pair in range(half // LANES):
            at = slice(pair * LANES, (pair + 1) * LANES)
            qn, kn, query_scale, key_scale = head_parts(
                qkv_s[:, at],
                qkv_s[:, half + pair * LANES : half + (pair + 1) * LANES],
                mult[side : side + 1, at],
                first,
            )
            q_low, k_low = qn.astype(bf16), kn.astype(bf16)
            v_low = qkv_s[:, 2 * half + pair * LANES : 2 * half + (pair + 1) * LANES].astype(bf16)
            qn_out[side, :, at] = q_low
            kn_out[side, :, at] = k_low
            v_out[side, :, at] = v_low
            rq_out[side, :, at] = query_scale
            rk_out[side, :, at] = key_scale
            mixed = []
            for head in range(2):
                own = first if head == 0 else jnp.logical_not(first)
                scores = dot_nt(jnp.where(own, k_low, jnp.zeros_like(k_low)), q_low)
                raised = jnp.exp(scores) * mask
                weight = raised * (1.0 / jnp.sum(raised, axis=0, keepdims=True))
                p_out[side * heads + 2 * pair + head] = weight
                mixed.append(dot_tn(weight.astype(bf16), v_low))
            mixed_out[:, at] = jnp.where(first, mixed[0], mixed[1]).astype(bf16)
        leave(7 + side)
        for index in range(1, 6):
            leave(index, side)
        leave(6, pl.ds(side * heads, heads))
    copies[6].wait()
    copies[7].wait()
    attn_out[...] = dot(mixed0[...], proj_w[0]) + dot(mixed1[...], proj_w[1]) + proj_bias[...]
    leave(9)
    middle = x + mods[0:1, :] * attn_out[...]
    middle_out[...] = middle
    leave(10)
    h2_out[...] = (normalize(middle)[0] * (1.0 + mods[3:4, :]) + mods[5:6, :]).astype(bf16)
    leave(11)

    def expand(side, act, slope, first_col):
        for to in tiles(act.shape[1], 512):
            at = slice(first_col + to.start, first_col + to.stop)
            pre = dot(h2_out[...], fc1_w[side, :, at]) + fc1_bias[side : side + 1, at]
            value, rise = gelu_parts(pre)
            act[:, to] = value.astype(bf16)
            slope[:, at] = rise.astype(bf16)

    copies[9].wait()
    expand(1, act1a, slope1, 0)
    leave(13)
    expand(1, act1b, slope1, act1a.shape[1])
    leave(14)
    leave(16)
    copies[8].wait()
    expand(0, act0, slope0, 0)
    leave(12)
    leave(15)
    wait_all(leaving)


def hidden_back_kernel(grad_ref, *refs):
    ins, outs, held, rest = split_refs(refs, [4, 3, 3])
    slope_s, fc2_w, in_sems, out_sems = rest
    slope0, slope1, fc2_0, fc2_1 = ins
    pre0, pre1a, pre1b = held
    cut = pre1a.shape[1]
    pairs = []
    for side in (1, 0):
        fc2, slope = (fc2_0, slope0) if side == 0 else (fc2_1, slope1)
        for at in (slice(0, cut), slice(cut, 2 * cut)):
            pairs.append((fc2.at[at, :], fc2_w.at[side, at, :]))
            pairs.append((slope.at[:, at], slope_s.at[side, :, at]))
    copies = start_copies(pairs, in_sems)
    leaving = []
    for side, pre, at, first_col in (
        (1, pre1a, slice(0, cut), 0),
        (1, pre1b, slice(cut, 2 * cut), 0),
        (0, pre0, slice(0, cut), 0),
        (0, pre0, slice(cut, 2 * cut), cut),
    ):
        step = 2 * (1 - side) + at.start // cut
        copies[2 * step].wait()
        copies[2 * step + 1].wait()
        for to in tiles(cut, 512):
            cols = slice(at.start + to.start, at.start + to.stop)
            grad = dot_nt(grad_ref[...], fc2_w[side, cols, :])
            pre[:, first_col + to.start : first_col + to.stop] = (
                grad * slope_s[side, :, cols].astype(f32)
            ).astype(bf16)
        if step < 2 or step == 3:
            index = {0: 1, 1: 2, 3: 0}[step]
            leaving += start_copies([(held[index], outs[index])], out_sems.at[pl.ds(index, 1)])
    wait_all(leaving)


def row_back_kernel(mods, mult, *refs):
    ins, outs, held, got, rest = split_refs(refs, [16, 6, 6, 16])
    h2_s, mixed_s, in_sems, out_sems = rest
    copies = start_copies(list(zip(ins, got)), in_sems)
    leaving = []

    def leave(index):
        copy = pltpu.make_async_copy(held[index], outs[index], out_sems.at[index])
        copy.start()
        leaving.append(copy)

    pre0, fc1_0, pre1a, pre1b, fc1_1, middle_ref, grad_out_ref, attn_ref = got[:8]
    proj_0, proj_1, qn_ref, kn_ref, v_ref, p_ref, rq_ref, rk_ref = got[8:]
    middle_grad, attn_grad, qkv_grad0, qkv1a, qkv1b, small = held
    rows, width = middle_ref.shape
    half = width // 2
    heads = half // HEAD_DIM
    copies[0].wait()
    copies[1].wait()
    for at in tiles(width, 512):
        h2_s[:, at] = dot_nt(pre0[...], fc1_0[at, :])
    wait_all(copies[2:5])
    for at in tiles(width, 512):
        total = h2_s[:, at]
        for index, pre in enumerate((pre1a, pre1b)):
            cut = pre.shape[1]
            total = total + dot_nt(pre[...], fc1_1[at, index * cut : (index + 1) * cut])
        h2_s[:, at] = total
    wait_all(copies[5:8])
    normed, spread = normalize(middle_ref[...])
    grad = h2_s[...]
    small[0:1, :] = jnp.sum(grad * normed, axis=0, keepdims=True)
    small[1:2, :] = jnp.sum(grad, axis=0, keepdims=True)
    total = grad_out_ref[...].astype(f32) + norm_back(
        grad * (1.0 + mods[3:4, :]), normed, spread
    )
    middle_grad[...] = total
    leave(0)
    small[2:3, :] = jnp.sum(total * attn_ref[...], axis=0, keepdims=True)
    attn_grad[...] = (mods[0:1, :] * total).astype(bf16)
    leave(1)
    first = lax.broadcasted_iota(jnp.int32, (rows, LANES), 1) < HEAD_DIM
    cut = qkv1a.shape[1]

    def put(side, start, values):
        if side == 0:
            qkv_grad0[:, start : start + LANES] = values
        else:
            index, to = start // cut, start % cut
            (qkv1a, qkv1b)[index][:, to : to + LANES] = values

    wait_all(copies[8:])
    for side in (1, 0):
        mixed_s[...] = dot_nt(attn_grad[...], (proj_0, proj_1)[side][...]).astype(bf16)
        for pair in range(half // LANES):
            at = slice(pair * LANES, (pair + 1) * LANES)
            mixed = mixed_s[:, at]
            q_low, k_low, v_low = qn_ref[side, :, at], kn_ref[side, :, at], v_ref[side, :, at]
            parts = []
            for head in range(2):
                own = first if head == 0 else jnp.logical_not(first)
                probs = p_ref[side * heads + 2 * pair + head]
                prob_grad = dot_nt(jnp.where(own, v_low, jnp.zeros_like(v_low)), mixed)
                centred = jnp.sum(prob_grad * probs, axis=0, keepdims=True)
                score_grad = (probs * (prob_grad - centred)).astype(bf16)
                parts.append(
                    (dot_tn(score_grad, k_low), dot(score_grad, q_low), dot(probs.astype(bf16), mixed))
                )
            query_grad, key_grad, value_grad = [
                jnp.where(first, low, high).astype(bf16) for low, high in zip(*parts)
            ]
            scaled = mult[side : side + 1, at]
            query_unit = q_low.astype(f32) * (1.0 / scaled)
            key_unit = k_low.astype(f32)
            unit_grad = query_grad.astype(f32) * scaled
            key_grad = key_grad.astype(f32)
            cross = unit_grad * query_unit
            small[3:4, side * half + pair * LANES : side * half + (pair + 1) * LANES] = jnp.sum(
                cross, axis=0, keepdims=True
            )
            query_pre = rq_ref[side, :, at] * (unit_grad - query_unit * half_sums(cross, first))
            key_pre = rk_ref[side, :, at] * (
                key_grad - key_unit * half_sums(key_grad * key_unit, first)
            )
            put(side, pair * LANES, query_pre.astype(bf16))
            put(side, half + pair * LANES, key_pre.astype(bf16))
            put(side, 2 * half + pair * LANES, value_grad)
        for index in (3, 4) if side == 1 else (2, 5):
            leave(index)
    wait_all(leaving)


def branch_kernel(mods, fc2_bias, *refs):
    ins, outs, got, rest = split_refs(refs, [7, 2, 7])
    output, mod_out = outs
    (in_sems,) = rest
    copies = start_copies(list(zip(ins, got)), in_sems)
    act0, fc2_0, act1a, act1b, fc2_1, grad_out_ref, middle_ref = got
    wait_all(copies)
    cut = act1a.shape[1]
    for at in tiles(middle_ref.shape[1], 512):
        value = (
            dot(act0[...], fc2_0[:, at])
            + dot(act1a[...], fc2_1[:cut, at])
            + dot(act1b[...], fc2_1[cut:, at])
            + fc2_bias[:, at]
        )
        output[:, at] = (middle_ref[:, at] + mods[1:2, at] * value).astype(bf16)
        mod_out[0:1, at] = jnp.sum(grad_out_ref[:, at].astype(f32) * value, axis=0, keepdims=True)


def input_back_kernel(mods, *refs):
    ins, outs, got, rest = split_refs(refs, [11, 2, 11])
    tokens_grad, mod_out = outs
    sum_s, in_sems = rest
    copies = start_copies(list(zip(ins, got)), in_sems)
    qkv_grad0, qkv1a, qkv1b, x_ref, middle_grad = got[:5]
    weights = got[5:]
    wait_all(copies)
    width = x_ref.shape[1]
    half, cut = width // 2, qkv1a.shape[1]
    normed, spread = normalize(x_ref[...].astype(f32))
    for at in tiles(width, 512):
        total = jnp.zeros((x_ref.shape[0], at.stop - at.start), f32)
        for part in range(3):
            total = total + dot_nt(
                qkv_grad0[:, part * half : (part + 1) * half], weights[part][at, :]
            )
        for start in range(0, 3 * half, half // 2):
            piece = (qkv1a, qkv1b)[start // cut][:, start % cut : start % cut + half // 2]
            inner = start % half
            total = total + dot_nt(piece, weights[3 + start // half][at, inner : inner + half // 2])
        sum_s[:, at] = total
    grad = sum_s[...]
    mod_out[0:1, :] = jnp.sum(grad * normed, axis=0, keepdims=True)
    mod_out[1:2, :] = jnp.sum(grad, axis=0, keepdims=True)
    tokens_grad[...] = (
        middle_grad[...] + norm_back(grad * (1.0 + mods[2:3, :]), normed, spread)
    ).astype(bf16)


def column_tiles(rights, flow):
    start = 0
    for source, (near, *pieces) in enumerate(rights):
        quarter, cut = near.shape[1] // 4, pieces[0].shape[1]
        for step in range(2):
            at = (2 * flow + step) * quarter
            to = start + step * quarter
            far = pieces[at // cut][:, at % cut : at % cut + quarter]
            both = jnp.concatenate([near[:, at : at + quarter], far], axis=0)
            yield source, both, slice(at, at + quarter), slice(to, to + quarter)
        start += 2 * quarter


def split_refs(refs, counts):
    out = []
    for count in counts:
        out.append(refs[:count])
        refs = refs[count:]
    return out + [refs]


def grad_kernel(pieces, bit_ref, *refs):
    sources = len(pieces)
    *ins, outs = split_refs(refs, [3 + count for count in pieces])
    left_sums, right_sums = outs[:sources], outs[sources : 2 * sources]
    left_t = outs[2 * sources : 3 * sources]
    sent_a, sent_b, picked = outs[3 * sources :]
    moved, part, columns = sent_a.shape
    tokens, half = ins[0][0].shape[0], ins[0][0].shape[1] // 2
    depth = 2 * tokens
    ones = jnp.ones((8, depth), bf16)
    for source in range(sources):
        for side in range(2):
            cols = slice(side * half, (side + 1) * half)
            near, far = ins[source][0][:, cols], ins[source][1][:, cols]
            rows = slice(side * moved, (side + 1) * moved)
            left_sums[source][:, cols] = dot(ones, jnp.concatenate([near, far], axis=0))[0:1]
            left_t[source][rows, :, :tokens] = near.T.reshape(moved, part, tokens)
            left_t[source][rows, :, tokens:] = far.T.reshape(moved, part, tokens)
    rights = [refs[2:] for refs in ins]
    for flow, sent in enumerate((sent_a, sent_b)):
        away = 1 - bit_ref[flow]
        for source in range(sources):
            for row in range(moved):
                at = 2 * row + away if flow == 0 else (row // 2) * 4 + row % 2 + 2 * away
                picked[source, row] = left_t[source][at]
        for source, right, at, to in column_tiles(rights, flow):
            left = picked[source].reshape(moved * part, depth)
            sent[:, :, to] = dot(left, right).astype(bf16).reshape(moved, part, -1)
            right_sums[source][:, at] = dot(ones, right)[0:1]


def second_kernel(pieces, bit_ref, *refs):
    sources = len(pieces)
    left_t, *rights, ends = split_refs(refs, [sources] + [1 + count for count in pieces])
    came_a, came_b, sent_a, sent_b, own, picked = ends
    moved, part, columns = sent_a.shape
    depth = left_t[0].shape[2]
    for flow, (came, sent) in enumerate(((came_a, sent_a), (came_b, sent_b))):
        mine, away = bit_ref[flow], 1 - bit_ref[1 - flow]
        for source in range(sources):
            for row in range(moved):
                if flow == 0:
                    base, other = 4 * row + mine, 2
                else:
                    base, other = 4 * row + 2 * mine, 1
                picked[source, row] = left_t[source][base + other * away]
                picked[source, moved + row] = left_t[source][base + other * (1 - away)]
        for source, right, at, to in column_tiles(rights, flow):
            left = picked[source].reshape(2 * moved * part, depth)
            block = dot(left, right).reshape(2 * moved, part, -1)
            kept = slice(flow * columns + to.start, flow * columns + to.stop)
            for row in range(moved):
                sent[row, :, to] = (block[row] + came[2 * row + away, :, to].astype(f32)).astype(
                    bf16
                )
                own[row, :, kept] = (
                    block[moved + row] + came[2 * row + 1 - away, :, to].astype(f32)
                ).astype(bf16)


def third_kernel(bit, bit_ref, own, *refs):
    came, (sent, kept) = refs[:-2], refs[-2:]
    mine = bit_ref[bit]
    start = 0
    for part in came:
        to = slice(start, start + part.shape[2])
        start += part.shape[2]
        for row in range(sent.shape[0]):
            away, near = 2 * row + 1 - mine, 2 * row + mine
            sent[row, :, to] = (own[away, :, to].astype(f32) + part[away].astype(f32)).astype(bf16)
            kept[row, :, to] = (own[near, :, to].astype(f32) + part[near].astype(f32)).astype(kept.dtype)


def local_call(kernel, limit, outs, scratch, kinds, *values, out_kind="v"):
    places = {
        "s": pl.BlockSpec(memory_space=pltpu.SMEM),
        "v": pl.BlockSpec(memory_space=pltpu.VMEM),
        "h": pl.BlockSpec(memory_space=pl.ANY),
    }
    return pl.pallas_call(
        kernel,
        out_shape=outs,
        in_specs=[places[kind] for kind in kinds],
        out_specs=[places[out_kind]] * len(outs),
        scratch_shapes=scratch,
        compiler_params=pltpu.CompilerParams(vmem_limit_bytes=limit * 2**20),
        cost_estimate=pl.CostEstimate(flops=1, bytes_accessed=1, transcendentals=0),
    )(*values)


def normalize(values):
    mean = jnp.mean(values, axis=1, keepdims=True)
    spread = jnp.mean(values * values, axis=1, keepdims=True) - mean * mean
    scale = lax.rsqrt(spread + norm_eps)
    return (values - mean) * scale, scale


def norm_back(grad, normed, scale):
    return scale * (
        grad
        - jnp.mean(grad, axis=1, keepdims=True)
        - normed * jnp.mean(grad * normed, axis=1, keepdims=True)
    )


def gelu_parts(pre):
    square = pre * pre
    tanh = jnp.tanh(pre * (gelu_c + gelu_c * gelu_a * square))
    gate = 0.5 + 0.5 * tanh
    slope = gate + pre * (0.5 - 0.5 * tanh * tanh) * (gelu_c + 3.0 * gelu_c * gelu_a * square)
    return pre * gate, slope


def shards(
    tokens,
    class_ids,
    final_scale,
    row_slots,
    class_table,
    ada_weight,
    ada_bias,
    qkv_weight,
    qv_bias,
    log_scale,
    proj_weight,
    proj_bias,
    fc1_weight,
    fc1_bias,
    fc2_weight,
    fc2_bias,
    out_grad,
):
    groups = lax.axis_size("dp")
    bits = groups.bit_length() - 1
    here = lax.axis_index("dp")
    core = lax.axis_index("mp")
    micro, row_len, half = tokens.shape
    width = 2 * half
    share = row_len // groups
    heads = log_scale.shape[0]
    hidden = fc1_weight.shape[1]

    def swap(values):
        return lax.ppermute(values, "mp", [(0, 1), (1, 0)])

    def flip(values, bit):
        return lax.ppermute(values, "dp", [(i, i ^ (1 << bit)) for i in range(groups)])

    def in_order(own, other, axis):
        return jnp.where(
            core == 0,
            jnp.concatenate([own, other], axis),
            jnp.concatenate([other, own], axis),
        )

    class_picks = (
        class_ids.reshape(-1)[:, None] == jnp.arange(class_table.shape[0], dtype=jnp.int32)[None, :]
    )
    condition = dot(class_picks.astype(bf16), class_table)
    lifted = jax.nn.silu(condition).astype(bf16)
    ada_half = lax.dynamic_slice_in_dim(ada_weight, core * half, half, 2)
    ada_terms = dot(lifted, ada_half.reshape(ada_half.shape[0], 6 * half)).astype(bf16)

    def by_target(values):
        return values.reshape(micro, groups, -1, half).swapaxes(0, 1).reshape(2 * groups, -1, half)

    def exchange(values):
        return lax.all_to_all(values, ("dp", "mp"), split_axis=0, concat_axis=0, tiled=True)

    def to_row(values):
        return (
            values.reshape(groups, 2, share, half).transpose(0, 2, 1, 3).reshape(row_len, width)
        )

    first_message = jnp.concatenate([by_target(tokens), by_target(ada_terms)], axis=1)
    arrived = exchange(first_message)

    def after(values, *earlier):
        return lax.optimization_barrier((values, earlier))[0]

    small = jnp.concatenate(
        [ada_bias.reshape(-1), qv_bias.reshape(-1), log_scale, proj_bias, fc1_bias, fc2_bias]
    )
    small_sizes = [6 * half, 2 * half, heads, half, hidden, half]

    def unpack(flat):
        starts = [sum(small_sizes[:i]) for i in range(7)]
        return [flat[starts[i] : starts[i + 1]] for i in range(6)]

    own_small, oth_small = unpack(small), unpack(swap(small))
    qkv_w = [qkv_weight[:, part] for part in range(3)]
    qkv_w += [swap(weight) for weight in qkv_w]
    proj_w = (proj_weight, swap(proj_weight))
    fc1_w = (fc1_weight, swap(fc1_weight))
    fc2_w = (fc2_weight, swap(fc2_weight))
    ada_shift = in_order(own_small[0].reshape(6, half), oth_small[0].reshape(6, half), 1)
    proj_shift = in_order(own_small[3], oth_small[3], 0)
    fc2_shift = in_order(own_small[5], oth_small[5], 0)
    fc1_shift = jnp.stack([own_small[4], oth_small[4]])
    qkv_shift = jnp.stack(
        [
            jnp.concatenate([part[1][:half], jnp.zeros((half,), f32), part[1][half:]])
            for part in (own_small, oth_small)
        ]
    )
    head_mult = jnp.stack([jnp.repeat(jnp.exp(part[2]), HEAD_DIM) for part in (own_small, oth_small)])

    segments, levels = slot_layout(
        lax.dynamic_index_in_dim(final_scale[:, 0], core, 0, keepdims=False),
        lax.dynamic_index_in_dim(row_slots[:, 0], core, 0, keepdims=False),
    )
    mask = (
        (segments[:, None] == segments[None, :]) & (levels[:, None] <= levels[None, :])
    ).astype(f32)

    resident = to_row(arrived[:, :share])
    grads_arrived = exchange(
        after(by_target(out_grad), arrived, qkv_shift, head_mult, mask, proj_shift, fc1_shift, fc2_shift)
    )
    mods = (
        jnp.sum(arrived[:, share:].reshape(groups, 2, 6, half).astype(f32), axis=0)
        .transpose(1, 0, 2)
        .reshape(6, width)
        + ada_shift
    )

    def array(*dims, kind=bf16):
        return jax.ShapeDtypeStruct(dims, kind)

    vmem, dma = pltpu.VMEM, pltpu.SemaphoreType.DMA

    def scratch(arrays):
        return [vmem(value.shape, value.dtype) for value in arrays]

    wide = array(2, row_len, half)
    wide32 = array(2, row_len, half, kind=f32)
    kept = [
        array(row_len, width),
        wide,
        wide,
        wide,
        wide32,
        wide32,
        array(2 * heads, row_len, row_len, kind=f32),
        array(row_len, half),
        array(row_len, half),
        array(row_len, width, kind=f32),
        array(row_len, width, kind=f32),
        array(row_len, width),
        array(row_len, hidden),
        array(row_len, hidden // 2),
        array(row_len, hidden // 2),
        array(row_len, hidden),
        array(row_len, hidden),
    ]
    h1, qn, kn, vn, rq, rk, probs, mixed0, mixed1, attn, middle, h2, act0, *more = local_call(
        forward_kernel,
        56,
        kept,
        scratch(kept)
        + [
            vmem((2, 3, width, half), bf16),
            vmem((2, half, width), bf16),
            vmem((2, width, hidden), bf16),
            vmem((row_len, 3 * half), f32),
            dma((10,)),
            dma((23,)),
        ],
        "vvvvvvv" + "h" * 10,
        resident,
        mods,
        qkv_shift,
        head_mult,
        mask,
        proj_shift[None],
        fc1_shift,
        *qkv_w,
        *proj_w,
        *fc1_w,
        out_kind="h",
    )
    act1, (slope0, slope1) = more[:2], more[2:]

    own_bits = jnp.stack([(here >> bit) & 1 for bit in range(bits)])
    part = width // groups

    def source(near_left, far_left, near_right, sent_right):
        return (near_left, far_left, near_right, *[swap(values) for values in sent_right])

    def scatter_start(*sources):
        count = len(sources)
        pieces = [len(source) - 3 for source in sources]
        columns = sum(source[2].shape[1] for source in sources) // 2
        outs = local_call(
            functools.partial(grad_kernel, pieces),
            56,
            [array(1, width, kind=f32)] * count
            + [array(1, source[2].shape[1], kind=f32) for source in sources]
            + [array(groups, part, 2 * row_len)] * count
            + [array(groups // 2, part, columns)] * 2,
            [vmem((count, groups // 2, part, 2 * row_len), bf16)],
            "s" + "v" * sum(3 + piece for piece in pieces),
            own_bits,
            *[value for source in sources for value in source],
        )
        left_sums, right_sums = outs[:count], outs[count : 2 * count]
        rest = list(outs[2 * count : 3 * count])
        rest += [value for source in sources for value in source[2:]]
        return left_sums, right_sums, (pieces, rest), tuple(outs[3 * count :])

    def travel(sent):
        return flip(sent[0], 0), flip(sent[1], 1)

    def scatter_second(started, came):
        pieces, rest = started
        count = len(pieces)
        columns = came[0].shape[2]
        sent_a, sent_b, own = local_call(
            functools.partial(second_kernel, pieces),
            56,
            [array(groups // 4, part, columns)] * 2
            + [array(groups // 4, part, 2 * columns)],
            [vmem((count, groups // 2, part, 2 * row_len), bf16)],
            "s" + "v" * (len(rest) + 2),
            own_bits,
            *rest,
            *came,
        )
        return own, (sent_a, sent_b)

    def scatter_more(bit, own, came):
        rows, _, columns = own.shape
        sent, own = local_call(
            functools.partial(third_kernel, bit),
            56,
            [
                array(rows // 2, part, columns),
                array(rows // 2, part, columns, kind=f32 if bit == bits - 1 else bf16),
            ],
            [],
            "sv" + "v" * len(came),
            own_bits,
            own,
            *came,
        )
        return own, sent

    def scatter_end(begin, own, came):
        for bit in range(begin, bits):
            own, sent = scatter_more(bit, own, came)
            came = (flip(sent, bit),)
        return own[0] + came[0][0].astype(f32)

    grad_out = to_row(after(grads_arrived, act0))
    grad_branch = (mods[1:2] * grad_out.astype(f32)).astype(bf16)
    fc2_left, _, fc2_rest, fc2_sent = scatter_start(
        source(grad_branch, swap(grad_branch), act0, act1)
    )
    h1_far, h2_far, mixed_far = swap(h1), swap(h2), swap(mixed1)
    fc2_came = travel(fc2_sent)

    pre_kept = [array(row_len, hidden)] + [array(row_len, hidden // 2)] * 2
    pre0, *pre1 = local_call(
        hidden_back_kernel,
        56,
        pre_kept,
        scratch(pre_kept)
        + [vmem((2, row_len, hidden), bf16), vmem((2, hidden, width), bf16), dma((8,)), dma((3,))],
        "vhhhh",
        after(grad_branch, fc2_sent, h1_far, h2_far, mixed_far),
        slope0,
        slope1,
        *fc2_w,
        out_kind="h",
    )
    _, fc1_right, fc1_rest, fc1_sent = scatter_start(
        source(h2, h2_far, pre0, pre1)
    )
    fc1_came = travel(fc1_sent)
    def to_target(values):
        return (
            values.reshape(groups, share, 2, half).transpose(0, 2, 1, 3).reshape(-1, share, half)
        )

    branch_ins = [after(act0, fc1_sent), fc2_w[0], *act1, fc2_w[1], grad_out, middle]
    output, branch_mods = local_call(
        branch_kernel,
        56,
        [array(row_len, width), array(1, width, kind=f32)],
        scratch(branch_ins) + [dma((7,))],
        "vv" + "h" * 7,
        mods,
        fc2_shift[None],
        *branch_ins,
    )
    output_back = exchange(to_target(output))
    fc2_own, fc2_sent = scatter_second(fc2_rest, after(fc2_came, fc1_sent, output))
    fc2_came = travel(fc2_sent[::-1])[::-1]
    row_ins = [
        after(pre0, fc2_sent),
        fc1_w[0],
        *pre1,
        fc1_w[1],
        middle,
        grad_out,
        attn,
        *proj_w,
        qn,
        kn,
        vn,
        probs,
        rq,
        rk,
    ]
    row_kept = [
        array(row_len, width, kind=f32),
        array(row_len, width),
        array(row_len, 3 * half),
        array(row_len, 3 * half // 2),
        array(row_len, 3 * half // 2),
        array(4, width, kind=f32),
    ]
    middle_grad, attn_grad, qkv_grad0, qkv1a, qkv1b, row_mods = local_call(
        row_back_kernel,
        56,
        row_kept,
        scratch(row_kept)
        + scratch(row_ins)
        + [vmem((row_len, width), f32), vmem((row_len, half), bf16), dma((16,)), dma((6,))],
        "vv" + "h" * 16,
        mods,
        head_mult,
        *row_ins,
        out_kind="h",
    )
    ready = after((qkv1a, qkv1b, attn_grad), fc2_came, fc1_came)
    attn_far = swap(ready[2])
    qkv_source = source(h1, h1_far, qkv_grad0, ready[:2])
    fc1_own, fc1_sent = scatter_second(fc1_rest, fc1_came)
    fc1_came = travel(fc1_sent[::-1])[::-1]
    fc2_own, fc2_sent = scatter_more(2, fc2_own, fc2_came)
    fc2_came = (flip(fc2_sent, 2),)
    qkv_left, qkv_right, qkv_rest, qkv_sent = scatter_start(
        after(qkv_source, fc1_sent, fc2_sent),
        (attn_grad, attn_far, mixed0, mixed_far),
    )
    qkv_came = travel(qkv_sent)
    fc2_own, fc2_sent = scatter_more(3, fc2_own, after(fc2_came, qkv_sent))
    fc2_came = (flip(fc2_sent, 3),)
    end_ins = [
        after(qkv_grad0, fc2_sent, output_back),
        qkv1a,
        qkv1b,
        resident,
        middle_grad,
        *qkv_w,
    ]
    tokens_grad, end_mods = local_call(
        input_back_kernel,
        56,
        [array(row_len, width), array(2, width, kind=f32)],
        scratch(end_ins) + [vmem((row_len, width), f32), dma((11,))],
        "v" + "h" * 11,
        mods,
        *end_ins,
    )

    row_grads = jnp.stack(
        [row_mods[2], branch_mods[0], end_mods[0], row_mods[0], end_mods[1], row_mods[1]]
    ).astype(bf16)
    scale_terms = jnp.sum(row_mods[3].reshape(2, heads, HEAD_DIM), axis=2)
    scale_sum = scale_terms[0] + swap(scale_terms[1])

    def own_half(values):
        return lax.dynamic_slice_in_dim(values, core * half, half, 0)

    bias_sum = jnp.concatenate(
        [
            qkv_right[0][0, :half],
            qkv_right[0][0, 2 * half :],
            own_half(qkv_left[1][0]),
            fc1_right[0][0],
            own_half(fc2_left[0][0]),
            scale_sum,
        ]
    )

    def double(gathered, bias_sum, bit):
        rounded = bias_sum.astype(bf16)
        count = gathered.size
        came = flip(jnp.concatenate([gathered.reshape(-1), rounded]), bit)
        theirs = came[:count].reshape(gathered.shape)
        mine = (here >> bit) & 1
        both = jnp.where(mine == 0, jnp.stack([gathered, theirs]), jnp.stack([theirs, gathered]))
        return both, rounded.astype(f32) + came[count:].astype(f32)

    gathered, bias_sum = double(row_grads.reshape(6 * width), bias_sum, 2)
    tokens_back = exchange(to_target(after(tokens_grad, row_grads)))
    qkv_own, qkv_sent = scatter_second(
        qkv_rest, after(qkv_came, fc1_came, fc2_came, gathered)
    )
    qkv_came = travel(qkv_sent[::-1])[::-1]
    fc1_own, fc1_sent = scatter_more(2, fc1_own, after(fc1_came, qkv_sent))
    fc1_came = (flip(fc1_sent, 2),)
    gathered = after(gathered, qkv_sent)
    for bit in range(2):
        gathered, bias_sum = double(gathered, bias_sum, bit)
    qkv_own, qkv_sent = scatter_more(2, qkv_own, after(qkv_came, fc1_came, gathered))
    qkv_came = (flip(qkv_sent, 2),)
    fc1_own, fc1_sent = scatter_more(3, fc1_own, after(fc1_came, qkv_sent))
    fc1_came = (flip(fc1_sent, 3),)
    gathered = after(gathered, fc1_sent)
    for bit in range(3, bits):
        gathered, bias_sum = double(gathered, bias_sum, bit)
    order = list(range(bits - 1, 2, -1)) + [1, 0, 2]
    gathered = gathered.transpose(
        *[order.index(bit) for bit in range(bits - 1, -1, -1)], bits
    ).reshape(groups, 6 * width)
    qkv_own, qkv_sent = scatter_more(3, qkv_own, after(qkv_came, fc1_came, gathered))
    qkv_came = (flip(qkv_sent, 3),)
    gathered = after(gathered, qkv_sent)
    gathered = in_order(gathered, swap(gathered), 0)
    fc2_sum = scatter_end(4, fc2_own, fc2_came)
    fc1_sum = scatter_end(4, fc1_own, fc1_came)
    qkv_sum = scatter_end(4, qkv_own, qkv_came)

    ada_weight_grad = dot_tn(lifted, gathered).reshape(ada_weight.shape)
    ada_bias_grad = jnp.sum(gathered.astype(f32), axis=0).reshape(6, width)
    grad_lifted = dot_nt(gathered, ada_weight.reshape(ada_weight.shape[0], 6 * width))
    _, silu_pull = jax.vjp(jax.nn.silu, condition)
    table_grad = lax.dot_general(
        class_picks.astype(f32),
        silu_pull(grad_lifted)[0],
        (((0,), (0,)), ((), ())),
        precision=lax.Precision.HIGHEST,
    )

    def from_rows(values):
        return values.reshape(groups, 2, share, half).swapaxes(0, 1).reshape(2, row_len, half)

    qkv_cols, proj_cols = 3 * half // 2, half // 2
    turn = qkv_cols + proj_cols
    qkv_own_sum = jnp.concatenate([qkv_sum[:, :qkv_cols], qkv_sum[:, turn : turn + qkv_cols]], 1)
    proj_sum = jnp.concatenate([qkv_sum[:, qkv_cols:turn], qkv_sum[:, turn + qkv_cols :]], 1)
    ends = [half, 2 * half, 3 * half, 3 * half + hidden, 4 * half + hidden]
    return (
        from_rows(output_back),
        from_rows(tokens_back),
        table_grad,
        ada_weight_grad,
        ada_bias_grad,
        qkv_own_sum.reshape(-1, 3, half),
        bias_sum[: ends[1]].reshape(2, half),
        bias_sum[ends[4] :],
        proj_sum.T,
        bias_sum[ends[1] : ends[2]],
        fc1_sum,
        bias_sum[ends[2] : ends[3]],
        fc2_sum.T,
        bias_sum[ends[3] : ends[4]],
    )


def solution(mesh):
    placed = (
        P(None, "dp", "mp"),
        P(),
        P(None, "dp", None),
        P(None, "dp", None),
        P(None, "dp"),
        P("dp", None, None),
        P(None, "mp"),
        P(None, None, "mp"),
        P(None, "mp"),
        P("mp"),
        P("mp", None),
        P("mp"),
        P(None, "mp"),
        P("mp"),
        P("mp", None),
        P("mp"),
        P(None, "dp", "mp"),
    )
    return jax.shard_map(
        shards,
        mesh=mesh,
        in_specs=placed,
        out_specs=(
            P(None, "dp", "mp"),
            P(None, "dp", "mp"),
            P(None, "dp"),
            P("dp", None, None),
            P(),
            P("dp", None, "mp"),
            P(None, "mp"),
            P("mp"),
            P("mp", "dp"),
            P("mp"),
            P("dp", "mp"),
            P("mp"),
            P("mp", "dp"),
            P("mp"),
        ),
        check_vma=False,
    )
```

```python
import functools

import jax
import jax.numpy as jnp
from jax import lax
from jax.experimental import pallas as pl
from jax.experimental.pallas import tpu as pltpu
from jax.sharding import PartitionSpec as P

HEAD_DIM = 64
LANES = 128
scale_ends = (1, 5, 14, 30, 55, 91, 155, 255, 424, 680)
norm_eps = 1e-06
unit_eps = 1e-06
bf16 = jnp.bfloat16
f32 = jnp.float32
gelu_c = 0.7978845608028654
gelu_a = 0.044715


def slot_layout(final_row, slots_row):
    ends_table = jnp.asarray(scale_ends, dtype=jnp.int32)
    chosen = final_row[:, None] == jnp.arange(len(scale_ends), dtype=jnp.int32)[None, :]
    lengths = jnp.sum(jnp.where(chosen, ends_table[None, :], 0), axis=1)
    items = final_row.shape[0]
    before = jnp.arange(items)[:, None] <= jnp.arange(items)[None, :]
    item_ends = jnp.sum(jnp.where(before, lengths[:, None], 0), axis=0)
    passed = slots_row[:, None] >= item_ends[None, :]
    segment = jnp.sum(passed.astype(jnp.int32), axis=1)
    item_start = jnp.sum(jnp.where(passed, lengths[None, :], 0), axis=1)
    offset = slots_row - item_start
    level = jnp.sum((offset[:, None] >= ends_table[None, :]).astype(jnp.int32), axis=1)
    return segment, jnp.where(segment == items, 0, level)


def dot(a, b):
    return jnp.dot(a, b, preferred_element_type=f32)


def dot_nt(a, b):
    return lax.dot_general(a, b, (((1,), (1,)), ((), ())), preferred_element_type=f32)


def dot_tn(a, b):
    return lax.dot_general(a, b, (((0,), (0,)), ((), ())), preferred_element_type=f32)


def half_sums(values, first):
    low = jnp.sum(jnp.where(first, values, 0.0), axis=1, keepdims=True)
    high = jnp.sum(jnp.where(first, 0.0, values), axis=1, keepdims=True)
    return jnp.where(first, low, high)


def head_parts(queries, keys, mult, first):
    query_scale = lax.rsqrt(half_sums(queries * queries, first) + unit_eps)
    key_scale = lax.rsqrt(half_sums(keys * keys, first) + unit_eps)
    return queries * query_scale * mult, keys * key_scale, query_scale, key_scale


def start_copies(pairs, sems):
    copies = [pltpu.make_async_copy(src, dst, sems.at[i]) for i, (src, dst) in enumerate(pairs)]
    for copy in copies:
        copy.start()
    return copies


def wait_all(copies):
    for copy in copies:
        copy.wait()


def tiles(size, most):
    tile = min(most, size)
    return [slice(start, start + tile) for start in range(0, size, tile)]


def forward_kernel(
    share, arrived, ada_ref, qkv_bias, mult, mask_ref, proj_bias, fc1_bias, *refs
):
    weights, outs, (x_ref, mods), held, rest = split_refs(refs, [10, 17, 2, 17])
    qkv_w, proj_w, fc1_w, qkv_s, in_sems, out_sems = rest
    copies = start_copies(
        [(weights[i], qkv_w.at[i // 3, i % 3]) for i in range(6)]
        + [(weights[6 + i], proj_w.at[i]) for i in range(2)]
        + [(weights[8 + i], fc1_w.at[i]) for i in range(2)],
        in_sems,
    )
    leaving = []

    def leave(index, *at):
        src, dst = held[index], outs[index]
        if at:
            src, dst = src.at[at], dst.at[at]
        copy = pltpu.make_async_copy(src, dst, out_sems.at[len(leaving)])
        copy.start()
        leaving.append(copy)

    h1, qn_out, kn_out, v_out, rq_out, rk_out, p_out, mixed0, mixed1, attn_out = held[:10]
    middle_out, h2_out, act0, act1a, act1b, slope0, slope1 = held[10:]
    rows, width = x_ref.shape
    half = width // 2
    if share:
        for side in range(2):
            cols = slice(side * half, (side + 1) * half)
            terms = jnp.zeros((8, half), f32)
            for group in range(rows // share):
                block = arrived.at[2 * group + side]
                x_ref[group * share : (group + 1) * share, cols] = block[:share, :]
                terms = terms + block[share : share + 8, :].astype(f32)
            mods[:, cols] = ada_ref[:, cols] + terms[:6]
            mods[2:3, cols] = mods[2:3, cols] + terms[6:7]
            mods[4:5, cols] = mods[4:5, cols] + terms[7:8]
    else:
        x_ref[...] = arrived[...]
        mods[...] = ada_ref[...]
    x = x_ref[...].astype(f32)
    h1[...] = (normalize(x)[0] * (1.0 + mods[2:3, :]) + mods[4:5, :]).astype(bf16)
    leave(0)
    first = lax.broadcasted_iota(jnp.int32, (rows, LANES), 1) < HEAD_DIM
    mask = mask_ref[...]
    heads = half // HEAD_DIM
    for side, mixed_out in enumerate((mixed0, mixed1)):
        for part in range(3):
            copies[3 * side + part].wait()
            at = slice(part * half, (part + 1) * half)
            qkv_s[:, at] = dot(h1[...], qkv_w[side, part]) + qkv_bias[side : side + 1, at]
        for pair in range(half // LANES):
            at = slice(pair * LANES, (pair + 1) * LANES)
            qn, kn, query_scale, key_scale = head_parts(
                qkv_s[:, at],
                qkv_s[:, half + pair * LANES : half + (pair + 1) * LANES],
                mult[side : side + 1, at],
                first,
            )
            q_low, k_low = qn.astype(bf16), kn.astype(bf16)
            v_low = qkv_s[:, 2 * half + pair * LANES : 2 * half + (pair + 1) * LANES].astype(bf16)
            qn_out[side, :, at] = q_low
            kn_out[side, :, at] = k_low
            v_out[side, :, at] = v_low
            rq_out[side, :, at] = query_scale
            rk_out[side, :, at] = key_scale
            mixed = []
            for head in range(2):
                own = first if head == 0 else jnp.logical_not(first)
                scores = dot_nt(jnp.where(own, k_low, jnp.zeros_like(k_low)), q_low)
                raised = jnp.exp(scores) * mask
                weight = raised * (1.0 / jnp.sum(raised, axis=0, keepdims=True))
                p_out[side * heads + 2 * pair + head] = weight
                mixed.append(dot_tn(weight.astype(bf16), v_low))
            mixed_out[:, at] = jnp.where(first, mixed[0], mixed[1]).astype(bf16)
        leave(7 + side)
        for index in range(1, 6):
            leave(index, side)
        leave(6, pl.ds(side * heads, heads))
    copies[6].wait()
    copies[7].wait()
    attn_out[...] = dot(mixed0[...], proj_w[0]) + dot(mixed1[...], proj_w[1]) + proj_bias[...]
    leave(9)
    middle = x + mods[0:1, :] * attn_out[...]
    middle_out[...] = middle
    leave(10)
    h2_out[...] = (normalize(middle)[0] * (1.0 + mods[3:4, :]) + mods[5:6, :]).astype(bf16)
    leave(11)

    def expand(side, act, slope, first_col):
        for to in tiles(act.shape[1], 512):
            at = slice(first_col + to.start, first_col + to.stop)
            pre = dot(h2_out[...], fc1_w[side, :, at]) + fc1_bias[side : side + 1, at]
            value, rise = gelu_parts(pre)
            act[:, to] = value.astype(bf16)
            slope[:, at] = rise.astype(bf16)

    copies[9].wait()
    expand(1, act1a, slope1, 0)
    leave(13)
    expand(1, act1b, slope1, act1a.shape[1])
    leave(14)
    leave(16)
    copies[8].wait()
    expand(0, act0, slope0, 0)
    leave(12)
    leave(15)
    wait_all(leaving)


def hidden_back_kernel(grad_ref, *refs):
    ins, outs, held, rest = split_refs(refs, [4, 3, 3])
    slope_s, fc2_w, in_sems, out_sems = rest
    slope0, slope1, fc2_0, fc2_1 = ins
    pre0, pre1a, pre1b = held
    cut = pre1a.shape[1]
    pairs = []
    for side in (1, 0):
        fc2, slope = (fc2_0, slope0) if side == 0 else (fc2_1, slope1)
        for at in (slice(0, cut), slice(cut, 2 * cut)):
            pairs.append((fc2.at[at, :], fc2_w.at[side, at, :]))
            pairs.append((slope.at[:, at], slope_s.at[side, :, at]))
    copies = start_copies(pairs, in_sems)
    leaving = []
    for side, pre, at, first_col in (
        (1, pre1a, slice(0, cut), 0),
        (1, pre1b, slice(cut, 2 * cut), 0),
        (0, pre0, slice(0, cut), 0),
        (0, pre0, slice(cut, 2 * cut), cut),
    ):
        step = 2 * (1 - side) + at.start // cut
        copies[2 * step].wait()
        copies[2 * step + 1].wait()
        for to in tiles(cut, 512):
            cols = slice(at.start + to.start, at.start + to.stop)
            grad = dot_nt(grad_ref[...], fc2_w[side, cols, :])
            pre[:, first_col + to.start : first_col + to.stop] = (
                grad * slope_s[side, :, cols].astype(f32)
            ).astype(bf16)
        if step < 2 or step == 3:
            index = {0: 1, 1: 2, 3: 0}[step]
            leaving += start_copies([(held[index], outs[index])], out_sems.at[pl.ds(index, 1)])
    wait_all(leaving)


def row_back_kernel(mods, mult, *refs):
    ins, outs, held, got, rest = split_refs(refs, [16, 6, 6, 16])
    h2_s, mixed_s, in_sems, out_sems = rest
    copies = start_copies(list(zip(ins, got)), in_sems)
    leaving = []

    def leave(index):
        copy = pltpu.make_async_copy(held[index], outs[index], out_sems.at[index])
        copy.start()
        leaving.append(copy)

    pre0, fc1_0, pre1a, pre1b, fc1_1, middle_ref, grad_out_ref, attn_ref = got[:8]
    proj_0, proj_1, qn_ref, kn_ref, v_ref, p_ref, rq_ref, rk_ref = got[8:]
    middle_grad, attn_grad, qkv_grad0, qkv1a, qkv1b, small = held
    rows, width = middle_ref.shape
    half = width // 2
    heads = half // HEAD_DIM
    copies[0].wait()
    copies[1].wait()
    for at in tiles(width, 512):
        h2_s[:, at] = dot_nt(pre0[...], fc1_0[at, :])
    wait_all(copies[2:5])
    for at in tiles(width, 512):
        total = h2_s[:, at]
        for index, pre in enumerate((pre1a, pre1b)):
            cut = pre.shape[1]
            total = total + dot_nt(pre[...], fc1_1[at, index * cut : (index + 1) * cut])
        h2_s[:, at] = total
    wait_all(copies[5:8])
    normed, spread = normalize(middle_ref[...])
    grad = h2_s[...]
    small[0:1, :] = jnp.sum(grad * normed, axis=0, keepdims=True)
    small[1:2, :] = jnp.sum(grad, axis=0, keepdims=True)
    total = grad_out_ref[...].astype(f32) + norm_back(
        grad * (1.0 + mods[3:4, :]), normed, spread
    )
    middle_grad[...] = total
    leave(0)
    small[2:3, :] = jnp.sum(total * attn_ref[...], axis=0, keepdims=True)
    attn_grad[...] = (mods[0:1, :] * total).astype(bf16)
    leave(1)
    first = lax.broadcasted_iota(jnp.int32, (rows, LANES), 1) < HEAD_DIM
    cut = qkv1a.shape[1]

    def put(side, start, values):
        if side == 0:
            qkv_grad0[:, start : start + LANES] = values
        else:
            index, to = start // cut, start % cut
            (qkv1a, qkv1b)[index][:, to : to + LANES] = values

    wait_all(copies[8:])
    for side in (1, 0):
        mixed_s[...] = dot_nt(attn_grad[...], (proj_0, proj_1)[side][...]).astype(bf16)
        for pair in range(half // LANES):
            at = slice(pair * LANES, (pair + 1) * LANES)
            mixed = mixed_s[:, at]
            q_low, k_low, v_low = qn_ref[side, :, at], kn_ref[side, :, at], v_ref[side, :, at]
            parts = []
            for head in range(2):
                own = first if head == 0 else jnp.logical_not(first)
                probs = p_ref[side * heads + 2 * pair + head]
                prob_grad = dot_nt(jnp.where(own, v_low, jnp.zeros_like(v_low)), mixed)
                centred = jnp.sum(prob_grad * probs, axis=0, keepdims=True)
                score_grad = (probs * (prob_grad - centred)).astype(bf16)
                parts.append(
                    (dot_tn(score_grad, k_low), dot(score_grad, q_low), dot(probs.astype(bf16), mixed))
                )
            query_grad, key_grad, value_grad = [
                jnp.where(first, low, high).astype(bf16) for low, high in zip(*parts)
            ]
            scaled = mult[side : side + 1, at]
            query_unit = q_low.astype(f32) * (1.0 / scaled)
            key_unit = k_low.astype(f32)
            unit_grad = query_grad.astype(f32) * scaled
            key_grad = key_grad.astype(f32)
            cross = unit_grad * query_unit
            small[3:4, side * half + pair * LANES : side * half + (pair + 1) * LANES] = jnp.sum(
                cross, axis=0, keepdims=True
            )
            query_pre = rq_ref[side, :, at] * (unit_grad - query_unit * half_sums(cross, first))
            key_pre = rk_ref[side, :, at] * (
                key_grad - key_unit * half_sums(key_grad * key_unit, first)
            )
            put(side, pair * LANES, query_pre.astype(bf16))
            put(side, half + pair * LANES, key_pre.astype(bf16))
            put(side, 2 * half + pair * LANES, value_grad)
        for index in (3, 4) if side == 1 else (2, 5):
            leave(index)
    wait_all(leaving)


def branch_kernel(mods, fc2_bias, *refs):
    ins, outs, got, rest = split_refs(refs, [7, 2, 7])
    output, mod_out = outs
    (in_sems,) = rest
    copies = start_copies(list(zip(ins, got)), in_sems)
    act0, fc2_0, act1a, act1b, fc2_1, grad_out_ref, middle_ref = got
    wait_all(copies)
    cut = act1a.shape[1]
    for at in tiles(middle_ref.shape[1], 512):
        value = (
            dot(act0[...], fc2_0[:, at])
            + dot(act1a[...], fc2_1[:cut, at])
            + dot(act1b[...], fc2_1[cut:, at])
            + fc2_bias[:, at]
        )
        output[:, at] = (middle_ref[:, at] + mods[1:2, at] * value).astype(bf16)
        mod_out[0:1, at] = jnp.sum(grad_out_ref[:, at].astype(f32) * value, axis=0, keepdims=True)


def input_back_kernel(mods, *refs):
    ins, outs, got, rest = split_refs(refs, [11, 2, 11])
    tokens_grad, mod_out = outs
    sum_s, in_sems = rest
    copies = start_copies(list(zip(ins, got)), in_sems)
    qkv_grad0, qkv1a, qkv1b, x_ref, middle_grad = got[:5]
    weights = got[5:]
    wait_all(copies)
    width = x_ref.shape[1]
    half, cut = width // 2, qkv1a.shape[1]
    normed, spread = normalize(x_ref[...].astype(f32))
    for at in tiles(width, 512):
        total = jnp.zeros((x_ref.shape[0], at.stop - at.start), f32)
        for part in range(3):
            total = total + dot_nt(
                qkv_grad0[:, part * half : (part + 1) * half], weights[part][at, :]
            )
        for start in range(0, 3 * half, half // 2):
            piece = (qkv1a, qkv1b)[start // cut][:, start % cut : start % cut + half // 2]
            inner = start % half
            total = total + dot_nt(piece, weights[3 + start // half][at, inner : inner + half // 2])
        sum_s[:, at] = total
    grad = sum_s[...]
    mod_out[0:1, :] = jnp.sum(grad * normed, axis=0, keepdims=True)
    mod_out[1:2, :] = jnp.sum(grad, axis=0, keepdims=True)
    tokens_grad[...] = (
        middle_grad[...] + norm_back(grad * (1.0 + mods[2:3, :]), normed, spread)
    ).astype(bf16)


def column_tiles(rights, flow):
    start = 0
    for source, (near, *pieces) in enumerate(rights):
        quarter, cut = near.shape[1] // 4, pieces[0].shape[1]
        for step in range(2):
            at = (2 * flow + step) * quarter
            to = start + step * quarter
            far = pieces[at // cut][:, at % cut : at % cut + quarter]
            both = jnp.concatenate([near[:, at : at + quarter], far], axis=0)
            yield source, both, slice(at, at + quarter), slice(to, to + quarter)
        start += 2 * quarter


def split_refs(refs, counts):
    out = []
    for count in counts:
        out.append(refs[:count])
        refs = refs[count:]
    return out + [refs]


def grad_kernel(pieces, bit_ref, *refs):
    sources = len(pieces)
    count = sum(pieces) + 3 * sources
    far, outs, got, held, rest = split_refs(refs, [count, 3 * sources + 2, count, sources + 2])
    *ins, _ = split_refs(got, [3 + count for count in pieces])
    picked, in_sems, out_sems = rest
    copies = start_copies(list(zip(far, got)), in_sems)
    waits = []
    for piece in pieces:
        waits.append(copies[: 3 + piece])
        copies = copies[3 + piece :]
    left_sums, right_sums = outs[:sources], outs[sources : 2 * sources]
    left_t, (sent_a, sent_b) = held[:sources], held[sources:]
    leaving = []

    def leave(index):
        copy = pltpu.make_async_copy(held[index], outs[2 * sources + index], out_sems.at[index])
        copy.start()
        leaving.append(copy)

    moved, part, columns = sent_a.shape
    tokens, half = ins[0][0].shape[0], ins[0][0].shape[1] // 2
    depth = 2 * tokens
    ones = jnp.ones((8, depth), bf16)
    for source in range(sources):
        wait_all(waits[source][:2])
        for side in range(2):
            cols = slice(side * half, (side + 1) * half)
            near, far = ins[source][0][:, cols], ins[source][1][:, cols]
            rows = slice(side * moved, (side + 1) * moved)
            left_sums[source][:, cols] = dot(ones, jnp.concatenate([near, far], axis=0))[0:1]
            left_t[source][rows, :, :tokens] = near.T.reshape(moved, part, tokens)
            left_t[source][rows, :, tokens:] = far.T.reshape(moved, part, tokens)
        leave(source)
    rights = [refs[2:] for refs in ins]
    for source in range(sources):
        wait_all(waits[source][2:])
    for flow, sent in enumerate((sent_a, sent_b)):
        away = 1 - bit_ref[flow]
        for source in range(sources):
            for row in range(moved):
                at = 2 * row + away if flow == 0 else (row // 2) * 4 + row % 2 + 2 * away
                picked[source, row] = left_t[source][at]
        for source, right, at, to in column_tiles(rights, flow):
            left = picked[source].reshape(moved * part, depth)
            sent[:, :, to] = dot(left, right).astype(bf16).reshape(moved, part, -1)
            right_sums[source][:, at] = dot(ones, right)[0:1]
        leave(sources + flow)
    wait_all(leaving)


def second_kernel(pieces, bit_ref, *refs):
    sources = len(pieces)
    count = 2 * sources + sum(pieces) + 2
    far, outs, got, held, rest = split_refs(refs, [count, 3, count, 3])
    left_t, *rights, (came_a, came_b) = split_refs(got, [sources] + [1 + count for count in pieces])
    sent_a, sent_b, own = held
    picked, in_sems, out_sems = rest
    copies = start_copies(list(zip(far, got)), in_sems)
    wait_all(copies[:-2])
    leaving = []
    moved, part, columns = sent_a.shape
    depth = left_t[0].shape[2]
    for flow, (came, sent) in enumerate(((came_a, sent_a), (came_b, sent_b))):
        copies[flow - 2].wait()
        mine, away = bit_ref[flow], 1 - bit_ref[1 - flow]
        for source in range(sources):
            for row in range(moved):
                if flow == 0:
                    base, other = 4 * row + mine, 2
                else:
                    base, other = 4 * row + 2 * mine, 1
                picked[source, row] = left_t[source][base + other * away]
                picked[source, moved + row] = left_t[source][base + other * (1 - away)]
        for source, right, at, to in column_tiles(rights, flow):
            left = picked[source].reshape(2 * moved * part, depth)
            block = dot(left, right).reshape(2 * moved, part, -1)
            kept = slice(flow * columns + to.start, flow * columns + to.stop)
            for row in range(moved):
                sent[row, :, to] = (block[row] + came[2 * row + away, :, to].astype(f32)).astype(
                    bf16
                )
                own[row, :, kept] = (
                    block[moved + row] + came[2 * row + 1 - away, :, to].astype(f32)
                ).astype(bf16)
        leaving += start_copies([(held[flow], outs[flow])], out_sems.at[pl.ds(flow, 1)])
    leaving += start_copies([(own, outs[2])], out_sems.at[pl.ds(2, 1)])
    wait_all(leaving)


def third_kernel(bit, bit_ref, own, *refs):
    came, (sent, kept) = refs[:-2], refs[-2:]
    mine = bit_ref[bit]
    start = 0
    for part in came:
        to = slice(start, start + part.shape[2])
        start += part.shape[2]
        for row in range(sent.shape[0]):
            away, near = 2 * row + 1 - mine, 2 * row + mine
            sent[row, :, to] = (own[away, :, to].astype(f32) + part[away].astype(f32)).astype(bf16)
            kept[row, :, to] = (own[near, :, to].astype(f32) + part[near].astype(f32)).astype(kept.dtype)


def local_call(kernel, limit, outs, scratch, kinds, *values, out_kind="v", flops=1):
    places = {
        "s": pl.BlockSpec(memory_space=pltpu.SMEM),
        "v": pl.BlockSpec(memory_space=pltpu.VMEM),
        "h": pl.BlockSpec(memory_space=pl.ANY),
    }
    return pl.pallas_call(
        kernel,
        out_shape=outs,
        in_specs=[places[kind] for kind in kinds],
        out_specs=[places[kind] for kind in (out_kind if len(out_kind) > 1 else out_kind * len(outs))],
        scratch_shapes=scratch,
        compiler_params=pltpu.CompilerParams(vmem_limit_bytes=limit * 2**20),
        cost_estimate=pl.CostEstimate(flops=flops, bytes_accessed=1, transcendentals=0),
    )(*values)


def normalize(values):
    mean = jnp.mean(values, axis=1, keepdims=True)
    spread = jnp.mean(values * values, axis=1, keepdims=True) - mean * mean
    scale = lax.rsqrt(spread + norm_eps)
    return (values - mean) * scale, scale


def norm_back(grad, normed, scale):
    return scale * (
        grad
        - jnp.mean(grad, axis=1, keepdims=True)
        - normed * jnp.mean(grad * normed, axis=1, keepdims=True)
    )


def gelu_parts(pre):
    square = pre * pre
    tanh = jnp.tanh(pre * (gelu_c + gelu_c * gelu_a * square))
    gate = 0.5 + 0.5 * tanh
    slope = gate + pre * (0.5 - 0.5 * tanh * tanh) * (gelu_c + 3.0 * gelu_c * gelu_a * square)
    return pre * gate, slope


def shards(
    tokens,
    class_ids,
    final_scale,
    row_slots,
    class_table,
    ada_weight,
    ada_bias,
    qkv_weight,
    qv_bias,
    log_scale,
    proj_weight,
    proj_bias,
    fc1_weight,
    fc1_bias,
    fc2_weight,
    fc2_bias,
    out_grad,
):
    groups = lax.axis_size("dp")
    bits = groups.bit_length() - 1
    here = lax.axis_index("dp")
    core = lax.axis_index("mp")
    micro, row_len, half = tokens.shape
    width = 2 * half
    share = row_len // groups
    heads = log_scale.shape[0]
    hidden = fc1_weight.shape[1]

    def swap(values):
        return lax.ppermute(values, "mp", [(0, 1), (1, 0)])

    def flip(values, bit):
        return lax.ppermute(values, "dp", [(i, i ^ (1 << bit)) for i in range(groups)])

    def in_order(own, other, axis):
        return jnp.where(
            core == 0,
            jnp.concatenate([own, other], axis),
            jnp.concatenate([other, own], axis),
        )

    class_picks = (
        class_ids.reshape(-1)[:, None] == jnp.arange(class_table.shape[0], dtype=jnp.int32)[None, :]
    )
    condition = dot(class_picks.astype(bf16), class_table)
    lifted = jax.nn.silu(condition).astype(bf16)
    ada_half = lax.dynamic_slice_in_dim(ada_weight, core * half, half, 2)
    ada_terms = dot(lifted, ada_half.reshape(ada_half.shape[0], 6 * half))
    ada_terms = ada_terms.reshape(micro, groups, 6, half)
    ada_round = lax.reduce_precision(ada_terms, 8, 7)
    ada_rest = jnp.stack([ada_terms[:, :, c] - ada_round[:, :, c] for c in (2, 4)], axis=2)
    ada_sent = jnp.concatenate([ada_round, ada_rest], axis=2).astype(bf16)

    def by_target(values):
        return values.reshape(micro, groups, -1, half).swapaxes(0, 1).reshape(2 * groups, -1, half)

    def exchange(values):
        return lax.all_to_all(values, ("dp", "mp"), split_axis=0, concat_axis=0, tiled=True)

    def to_row(values):
        return (
            values.reshape(groups, 2, share, half).transpose(0, 2, 1, 3).reshape(row_len, width)
        )

    first_message = jnp.concatenate([by_target(tokens), by_target(ada_sent)], axis=1)
    arrived = exchange(first_message)

    def after(values, *earlier):
        return lax.optimization_barrier((values, earlier))[0]

    small = jnp.concatenate(
        [ada_bias.reshape(-1), qv_bias.reshape(-1), log_scale, proj_bias, fc1_bias, fc2_bias]
    )
    small_sizes = [6 * half, 2 * half, heads, half, hidden, half]

    def unpack(flat):
        starts = [sum(small_sizes[:i]) for i in range(7)]
        return [flat[starts[i] : starts[i + 1]] for i in range(6)]

    own_small, oth_small = unpack(small), unpack(swap(small))
    qkv_w = [qkv_weight[:, part] for part in range(3)]
    qkv_w += [swap(weight) for weight in qkv_w]
    proj_w = (proj_weight, swap(proj_weight))
    fc1_w = (fc1_weight, swap(fc1_weight))
    fc2_w = (fc2_weight, swap(fc2_weight))
    ada_shift = in_order(own_small[0].reshape(6, half), oth_small[0].reshape(6, half), 1)
    proj_shift = in_order(own_small[3], oth_small[3], 0)
    fc2_shift = in_order(own_small[5], oth_small[5], 0)
    fc1_shift = jnp.stack([own_small[4], oth_small[4]])
    qkv_shift = jnp.stack(
        [
            jnp.concatenate([part[1][:half], jnp.zeros((half,), f32), part[1][half:]])
            for part in (own_small, oth_small)
        ]
    )
    head_mult = jnp.stack([jnp.repeat(jnp.exp(part[2]), HEAD_DIM) for part in (own_small, oth_small)])

    segments, levels = slot_layout(
        lax.dynamic_index_in_dim(final_scale[:, 0], core, 0, keepdims=False),
        lax.dynamic_index_in_dim(row_slots[:, 0], core, 0, keepdims=False),
    )
    mask = (
        (segments[:, None] == segments[None, :]) & (levels[:, None] <= levels[None, :])
    ).astype(f32)

    grads_arrived = exchange(
        after(by_target(out_grad), arrived, qkv_shift, head_mult, mask, proj_shift, fc1_shift, fc2_shift)
    )

    def array(*dims, kind=bf16):
        return jax.ShapeDtypeStruct(dims, kind)

    vmem, dma = pltpu.VMEM, pltpu.SemaphoreType.DMA

    def scratch(arrays):
        return [vmem(value.shape, value.dtype) for value in arrays]

    wide = array(2, row_len, half)
    wide32 = array(2, row_len, half, kind=f32)
    whole_tiles = share % 16 == 0
    if whole_tiles:
        row_in, ada_in = arrived, ada_shift
    else:
        row_in = to_row(arrived[:, :share])
        terms = jnp.sum(arrived[:, share:].reshape(groups, 2, 8, half).astype(f32), axis=0)
        terms = terms.transpose(1, 0, 2).reshape(8, width)
        ada_in = (ada_shift + terms[:6]).at[2].add(terms[6]).at[4].add(terms[7])
    kept = [
        array(row_len, width),
        wide,
        wide,
        wide,
        wide32,
        wide32,
        array(2 * heads, row_len, row_len, kind=f32),
        array(row_len, half),
        array(row_len, half),
        array(row_len, width, kind=f32),
        array(row_len, width, kind=f32),
        array(row_len, width),
        array(row_len, hidden),
        array(row_len, hidden // 2),
        array(row_len, hidden // 2),
        array(row_len, hidden),
        array(row_len, hidden),
    ]
    h1, qn, kn, vn, rq, rk, probs, mixed0, mixed1, attn, middle, h2, act0, *more = local_call(
        functools.partial(forward_kernel, share if whole_tiles else 0),
        56,
        kept + [array(row_len, width), array(6, width, kind=f32)],
        scratch(kept)
        + [
            vmem((2, 3, width, half), bf16),
            vmem((2, half, width), bf16),
            vmem((2, width, hidden), bf16),
            vmem((row_len, 3 * half), f32),
            dma((10,)),
            dma((23,)),
        ],
        "vvvvvvv" + "h" * 10,
        row_in,
        ada_in,
        qkv_shift,
        head_mult,
        mask,
        proj_shift[None],
        fc1_shift,
        *qkv_w,
        *proj_w,
        *fc1_w,
        out_kind="h" * len(kept) + "vv",
    )
    act1, (slope0, slope1, resident, mods) = more[:2], more[2:]

    own_bits = jnp.stack([(here >> bit) & 1 for bit in range(bits)])
    part = width // groups

    def source(near_left, far_left, near_right, sent_right):
        return (near_left, far_left, near_right, *[swap(values) for values in sent_right])

    def scatter_start(*sources):
        count = len(sources)
        pieces = [len(source) - 3 for source in sources]
        columns = sum(source[2].shape[1] for source in sources) // 2
        ins = [value for source in sources for value in source]
        kept = [array(groups, part, 2 * row_len)] * count + [
            array(groups // 2, part, columns)
        ] * 2
        outs = local_call(
            functools.partial(grad_kernel, pieces),
            56,
            [array(1, width, kind=f32)] * count
            + [array(1, source[2].shape[1], kind=f32) for source in sources]
            + kept,
            scratch(ins)
            + scratch(kept)
            + [
                vmem((count, groups // 2, part, 2 * row_len), bf16),
                dma((len(ins),)),
                dma((len(kept),)),
            ],
            "s" + "h" * len(ins),
            own_bits,
            *ins,
            out_kind="v" * (2 * count) + "h" * len(kept),
        )
        left_sums, right_sums = outs[:count], outs[count : 2 * count]
        rest = list(outs[2 * count : 3 * count])
        rest += [value for source in sources for value in source[2:]]
        return left_sums, right_sums, (pieces, rest), tuple(outs[3 * count :])

    def travel(sent):
        return flip(sent[0], 0), flip(sent[1], 1)

    def scatter_second(started, came, flops=1):
        pieces, rest = started
        count = len(pieces)
        columns = came[0].shape[2]
        ins = [*rest, *came]
        kept = [array(groups // 4, part, columns)] * 2 + [array(groups // 4, part, 2 * columns)]
        sent_a, sent_b, own = local_call(
            functools.partial(second_kernel, pieces),
            56,
            kept,
            scratch(ins)
            + scratch(kept)
            + [
                vmem((count, groups // 2, part, 2 * row_len), bf16),
                dma((len(ins),)),
                dma((3,)),
            ],
            "s" + "h" * len(ins),
            own_bits,
            *ins,
            out_kind="h",
            flops=flops,
        )
        return own, (sent_a, sent_b)

    def scatter_more(bit, own, came):
        rows, _, columns = own.shape
        sent, own = local_call(
            functools.partial(third_kernel, bit),
            56,
            [
                array(rows // 2, part, columns),
                array(rows // 2, part, columns, kind=f32 if bit == bits - 1 else bf16),
            ],
            [],
            "sv" + "v" * len(came),
            own_bits,
            own,
            *came,
        )
        return own, sent

    def scatter_end(begin, own, came):
        for bit in range(begin, bits):
            own, sent = scatter_more(bit, own, came)
            came = (flip(sent, bit),)
        return own[0] + came[0][0].astype(f32)

    grad_out = to_row(after(grads_arrived, act0))
    grad_branch = (mods[1:2] * grad_out.astype(f32)).astype(bf16)
    fc2_left, _, fc2_rest, fc2_sent = scatter_start(
        source(grad_branch, swap(grad_branch), act0, act1)
    )
    h1_far, h2_far, mixed_far = swap(h1), swap(h2), swap(mixed1)
    fc2_came = travel(fc2_sent)

    pre_kept = [array(row_len, hidden)] + [array(row_len, hidden // 2)] * 2
    pre0, *pre1 = local_call(
        hidden_back_kernel,
        56,
        pre_kept,
        scratch(pre_kept)
        + [vmem((2, row_len, hidden), bf16), vmem((2, hidden, width), bf16), dma((8,)), dma((3,))],
        "vhhhh",
        after(grad_branch, fc2_sent, h1_far, h2_far, mixed_far),
        slope0,
        slope1,
        *fc2_w,
        out_kind="h",
    )
    _, fc1_right, fc1_rest, fc1_sent = scatter_start(
        source(h2, h2_far, pre0, pre1)
    )
    fc1_came = travel(fc1_sent)
    def to_target(values):
        return (
            values.reshape(groups, share, 2, half).transpose(0, 2, 1, 3).reshape(-1, share, half)
        )

    fc2_own, fc2_sent = scatter_second(fc2_rest, after(fc2_came, fc1_sent), int(3e9))
    fc2_came = travel(fc2_sent[::-1])[::-1]
    row_ins = [
        after(pre0, fc2_sent),
        fc1_w[0],
        *pre1,
        fc1_w[1],
        middle,
        grad_out,
        attn,
        *proj_w,
        qn,
        kn,
        vn,
        probs,
        rq,
        rk,
    ]
    row_kept = [
        array(row_len, width, kind=f32),
        array(row_len, width),
        array(row_len, 3 * half),
        array(row_len, 3 * half // 2),
        array(row_len, 3 * half // 2),
        array(4, width, kind=f32),
    ]
    middle_grad, attn_grad, qkv_grad0, qkv1a, qkv1b, row_mods = local_call(
        row_back_kernel,
        56,
        row_kept,
        scratch(row_kept)
        + scratch(row_ins)
        + [vmem((row_len, width), f32), vmem((row_len, half), bf16), dma((16,)), dma((6,))],
        "vv" + "h" * 16,
        mods,
        head_mult,
        *row_ins,
        out_kind="h",
    )
    fc1_own, fc1_sent = scatter_second(fc1_rest, after(fc1_came, attn_grad))
    ready = after((qkv1a, qkv1b, attn_grad), fc2_came, fc1_sent)
    fc1_came = travel(fc1_sent[::-1])[::-1]
    qkv_left, qkv_right, qkv_rest, qkv_sent = scatter_start(
        source(h1, h1_far, qkv_grad0, ready[:2]),
        (attn_grad, swap(ready[2]), mixed0, mixed_far),
    )
    qkv_came = travel(qkv_sent)
    fc2_own, fc2_sent = scatter_more(2, fc2_own, after(fc2_came, qkv_sent))
    fc2_came = (flip(fc2_sent, 2),)
    branch_ins = [after(act0, fc1_came, fc2_sent), fc2_w[0], *act1, fc2_w[1], grad_out, middle]
    output, branch_mods = local_call(
        branch_kernel,
        56,
        [array(row_len, width), array(1, width, kind=f32)],
        scratch(branch_ins) + [dma((7,))],
        "vv" + "h" * 7,
        mods,
        fc2_shift[None],
        *branch_ins,
    )
    fc2_own, fc2_sent = scatter_more(3, fc2_own, after(fc2_came, output))
    fc2_came = (flip(fc2_sent, 3),)
    end_ins = [
        after(qkv_grad0, fc2_sent),
        qkv1a,
        qkv1b,
        resident,
        middle_grad,
        *qkv_w,
    ]
    tokens_grad, end_mods = local_call(
        input_back_kernel,
        56,
        [array(row_len, width), array(2, width, kind=f32)],
        scratch(end_ins) + [vmem((row_len, width), f32), dma((11,))],
        "v" + "h" * 11,
        mods,
        *end_ins,
    )

    row_grads = jnp.stack(
        [row_mods[2], branch_mods[0], end_mods[0], row_mods[0], end_mods[1], row_mods[1]]
    ).astype(bf16)
    scale_terms = jnp.sum(row_mods[3].reshape(2, heads, HEAD_DIM), axis=2)
    scale_sum = scale_terms[0] + swap(scale_terms[1])

    def own_half(values):
        return lax.dynamic_slice_in_dim(values, core * half, half, 0)

    bias_sum = jnp.concatenate(
        [
            qkv_right[0][0, :half],
            qkv_right[0][0, 2 * half :],
            own_half(qkv_left[1][0]),
            fc1_right[0][0],
            own_half(fc2_left[0][0]),
            scale_sum,
        ]
    )

    def double(gathered, bias_sum, bit):
        rounded = bias_sum.astype(bf16)
        count = gathered.size
        came = flip(jnp.concatenate([gathered.reshape(-1), rounded]), bit)
        theirs = came[:count].reshape(gathered.shape)
        mine = (here >> bit) & 1
        both = jnp.where(mine == 0, jnp.stack([gathered, theirs]), jnp.stack([theirs, gathered]))
        return both, rounded.astype(f32) + came[count:].astype(f32)

    gathered, bias_sum = double(row_grads.reshape(6 * width), bias_sum, 2)
    returned = exchange(
        jnp.concatenate(
            [to_target(values) for values in after((output, tokens_grad), row_grads)], axis=1
        )
    )
    qkv_own, qkv_sent = scatter_second(
        qkv_rest, after(qkv_came, fc1_came, fc2_came, gathered)
    )
    qkv_came = travel(qkv_sent[::-1])[::-1]
    fc1_own, fc1_sent = scatter_more(2, fc1_own, after(fc1_came, qkv_sent))
    fc1_came = (flip(fc1_sent, 2),)
    gathered = after(gathered, qkv_sent)
    for bit in range(3, bits):
        gathered, bias_sum = double(gathered, bias_sum, bit)
    qkv_own, qkv_sent = scatter_more(2, qkv_own, after(qkv_came, fc1_came, gathered, returned))
    qkv_came = (flip(qkv_sent, 2),)
    fc1_own, fc1_sent = scatter_more(3, fc1_own, after(fc1_came, qkv_sent))
    fc1_came = (flip(fc1_sent, 3),)
    gathered = after(gathered, fc1_sent)
    for bit in range(2):
        gathered, bias_sum = double(gathered, bias_sum, bit)
    gathered = gathered.transpose(*range(2, bits), 0, 1, bits).reshape(groups, 6 * width)
    qkv_own, qkv_sent = scatter_more(3, qkv_own, after(qkv_came, fc1_came, gathered))
    qkv_came = (flip(qkv_sent, 3),)
    gathered = after(gathered, qkv_sent)
    gathered = in_order(gathered, swap(gathered), 0)
    fc2_sum = scatter_end(4, fc2_own, fc2_came)
    fc1_sum = scatter_end(4, fc1_own, fc1_came)
    qkv_sum = scatter_end(4, qkv_own, qkv_came)

    ada_weight_grad = dot_tn(lifted, gathered).reshape(ada_weight.shape)
    ada_bias_grad = jnp.sum(gathered.astype(f32), axis=0).reshape(6, width)
    grad_lifted = dot_nt(gathered, ada_weight.reshape(ada_weight.shape[0], 6 * width))
    _, silu_pull = jax.vjp(jax.nn.silu, condition)
    table_grad = lax.dot_general(
        class_picks.astype(f32),
        silu_pull(grad_lifted)[0],
        (((0,), (0,)), ((), ())),
        precision=lax.Precision.HIGHEST,
    )

    def from_rows(values):
        return values.reshape(groups, 2, share, half).swapaxes(0, 1).reshape(2, row_len, half)

    qkv_cols, proj_cols = 3 * half // 2, half // 2
    turn = qkv_cols + proj_cols
    qkv_own_sum = jnp.concatenate([qkv_sum[:, :qkv_cols], qkv_sum[:, turn : turn + qkv_cols]], 1)
    proj_sum = jnp.concatenate([qkv_sum[:, qkv_cols:turn], qkv_sum[:, turn + qkv_cols :]], 1)
    ends = [half, 2 * half, 3 * half, 3 * half + hidden, 4 * half + hidden]
    return (
        from_rows(returned[:, :share]),
        from_rows(returned[:, share:]),
        table_grad,
        ada_weight_grad,
        ada_bias_grad,
        qkv_own_sum.reshape(-1, 3, half),
        bias_sum[: ends[1]].reshape(2, half),
        bias_sum[ends[4] :],
        proj_sum.T,
        bias_sum[ends[1] : ends[2]],
        fc1_sum,
        bias_sum[ends[2] : ends[3]],
        fc2_sum.T,
        bias_sum[ends[3] : ends[4]],
    )


def solution(mesh):
    placed = (
        P(None, "dp", "mp"),
        P(),
        P(None, "dp", None),
        P(None, "dp", None),
        P(None, "dp"),
        P("dp", None, None),
        P(None, "mp"),
        P(None, None, "mp"),
        P(None, "mp"),
        P("mp"),
        P("mp", None),
        P("mp"),
        P(None, "mp"),
        P("mp"),
        P("mp", None),
        P("mp"),
        P(None, "dp", "mp"),
    )
    return jax.shard_map(
        shards,
        mesh=mesh,
        in_specs=placed,
        out_specs=(
            P(None, "dp", "mp"),
            P(None, "dp", "mp"),
            P(None, "dp"),
            P("dp", None, None),
            P(),
            P("dp", None, "mp"),
            P(None, "mp"),
            P("mp"),
            P("mp", "dp"),
            P("mp"),
            P("dp", "mp"),
            P("mp"),
            P("mp", "dp"),
            P("mp"),
        ),
        check_vma=False,
    )
```

```python
import functools

import jax
import jax.numpy as jnp
from jax import lax
from jax.experimental import pallas as pl
from jax.experimental.pallas import tpu as pltpu
from jax.sharding import PartitionSpec as P

HEAD_DIM = 64
LANES = 128
scale_ends = (1, 5, 14, 30, 55, 91, 155, 255, 424, 680)
norm_eps = 1e-06
unit_eps = 1e-06
bf16 = jnp.bfloat16
f32 = jnp.float32
gelu_c = 0.7978845608028654
gelu_a = 0.044715


def slot_layout(final_row, slots_row):
    ends_table = jnp.asarray(scale_ends, dtype=jnp.int32)
    chosen = final_row[:, None] == jnp.arange(len(scale_ends), dtype=jnp.int32)[None, :]
    lengths = jnp.sum(jnp.where(chosen, ends_table[None, :], 0), axis=1)
    items = final_row.shape[0]
    before = jnp.arange(items)[:, None] <= jnp.arange(items)[None, :]
    item_ends = jnp.sum(jnp.where(before, lengths[:, None], 0), axis=0)
    passed = slots_row[:, None] >= item_ends[None, :]
    segment = jnp.sum(passed.astype(jnp.int32), axis=1)
    item_start = jnp.sum(jnp.where(passed, lengths[None, :], 0), axis=1)
    offset = slots_row - item_start
    level = jnp.sum((offset[:, None] >= ends_table[None, :]).astype(jnp.int32), axis=1)
    return segment, jnp.where(segment == items, 0, level)


def dot(a, b):
    return jnp.dot(a, b, preferred_element_type=f32)


def dot_nt(a, b):
    return lax.dot_general(a, b, (((1,), (1,)), ((), ())), preferred_element_type=f32)


def dot_tn(a, b):
    return lax.dot_general(a, b, (((0,), (0,)), ((), ())), preferred_element_type=f32)


def half_sums(values, first):
    low = jnp.sum(jnp.where(first, values, 0.0), axis=1, keepdims=True)
    high = jnp.sum(jnp.where(first, 0.0, values), axis=1, keepdims=True)
    return jnp.where(first, low, high)


def head_parts(queries, keys, mult, first):
    query_scale = lax.rsqrt(half_sums(queries * queries, first) + unit_eps)
    key_scale = lax.rsqrt(half_sums(keys * keys, first) + unit_eps)
    return queries * query_scale * mult, keys * key_scale, query_scale, key_scale


def start_copies(pairs, sems):
    copies = [pltpu.make_async_copy(src, dst, sems.at[i]) for i, (src, dst) in enumerate(pairs)]
    for copy in copies:
        copy.start()
    return copies


def wait_all(copies):
    for copy in copies:
        copy.wait()


def tiles(size, most):
    tile = min(most, size)
    return [slice(start, start + tile) for start in range(0, size, tile)]


def forward_kernel(
    share, arrived, ada_ref, qkv_bias, mult, mask_ref, proj_bias, fc1_bias, *refs
):
    weights, outs, (x_ref, mods), held, rest = split_refs(refs, [10, 17, 2, 17])
    qkv_w, proj_w, fc1_w, qkv_s, in_sems, out_sems = rest
    copies = start_copies(
        [(weights[i], qkv_w.at[i // 3, i % 3]) for i in range(6)]
        + [(weights[6 + i], proj_w.at[i]) for i in range(2)]
        + [(weights[8 + i], fc1_w.at[i]) for i in range(2)],
        in_sems,
    )
    leaving = []

    def leave(index, *at):
        src, dst = held[index], outs[index]
        if at:
            src, dst = src.at[at], dst.at[at]
        copy = pltpu.make_async_copy(src, dst, out_sems.at[len(leaving)])
        copy.start()
        leaving.append(copy)

    h1, qn_out, kn_out, v_out, rq_out, rk_out, p_out, mixed0, mixed1, attn_out = held[:10]
    middle_out, h2_out, act0, act1a, act1b, slope0, slope1 = held[10:]
    rows, width = x_ref.shape
    half = width // 2
    if share:
        for side in range(2):
            cols = slice(side * half, (side + 1) * half)
            terms = jnp.zeros((8, half), f32)
            for group in range(rows // share):
                block = arrived.at[2 * group + side]
                x_ref[group * share : (group + 1) * share, cols] = block[:share, :]
                terms = terms + block[share : share + 8, :].astype(f32)
            mods[:, cols] = ada_ref[:, cols] + terms[:6]
            mods[2:3, cols] = mods[2:3, cols] + terms[6:7]
            mods[4:5, cols] = mods[4:5, cols] + terms[7:8]
    else:
        x_ref[...] = arrived[...]
        mods[...] = ada_ref[...]
    x = x_ref[...].astype(f32)
    h1[...] = (normalize(x)[0] * (1.0 + mods[2:3, :]) + mods[4:5, :]).astype(bf16)
    leave(0)
    first = lax.broadcasted_iota(jnp.int32, (rows, LANES), 1) < HEAD_DIM
    mask = mask_ref[...]
    heads = half // HEAD_DIM
    for side, mixed_out in enumerate((mixed0, mixed1)):
        for part in range(3):
            copies[3 * side + part].wait()
            at = slice(part * half, (part + 1) * half)
            qkv_s[:, at] = dot(h1[...], qkv_w[side, part]) + qkv_bias[side : side + 1, at]
        for pair in range(half // LANES):
            at = slice(pair * LANES, (pair + 1) * LANES)
            qn, kn, query_scale, key_scale = head_parts(
                qkv_s[:, at],
                qkv_s[:, half + pair * LANES : half + (pair + 1) * LANES],
                mult[side : side + 1, at],
                first,
            )
            q_low, k_low = qn.astype(bf16), kn.astype(bf16)
            v_low = qkv_s[:, 2 * half + pair * LANES : 2 * half + (pair + 1) * LANES].astype(bf16)
            qn_out[side, :, at] = q_low
            kn_out[side, :, at] = k_low
            v_out[side, :, at] = v_low
            rq_out[side, :, at] = query_scale
            rk_out[side, :, at] = key_scale
            mixed = []
            for head in range(2):
                own = first if head == 0 else jnp.logical_not(first)
                scores = dot_nt(jnp.where(own, k_low, jnp.zeros_like(k_low)), q_low)
                raised = jnp.exp(scores) * mask
                weight = raised * (1.0 / jnp.sum(raised, axis=0, keepdims=True))
                p_out[side * heads + 2 * pair + head] = weight
                mixed.append(dot_tn(weight.astype(bf16), v_low))
            mixed_out[:, at] = jnp.where(first, mixed[0], mixed[1]).astype(bf16)
        leave(7 + side)
        for index in range(1, 6):
            leave(index, side)
        leave(6, pl.ds(side * heads, heads))
    copies[6].wait()
    copies[7].wait()
    attn_out[...] = dot(mixed0[...], proj_w[0]) + dot(mixed1[...], proj_w[1]) + proj_bias[...]
    leave(9)
    middle = x + mods[0:1, :] * attn_out[...]
    middle_out[...] = middle
    leave(10)
    h2_out[...] = (normalize(middle)[0] * (1.0 + mods[3:4, :]) + mods[5:6, :]).astype(bf16)
    leave(11)

    def expand(side, act, slope, first_col):
        for to in tiles(act.shape[1], 512):
            at = slice(first_col + to.start, first_col + to.stop)
            pre = dot(h2_out[...], fc1_w[side, :, at]) + fc1_bias[side : side + 1, at]
            value, rise = gelu_parts(pre)
            act[:, to] = value.astype(bf16)
            slope[:, at] = rise.astype(bf16)

    copies[9].wait()
    expand(1, act1a, slope1, 0)
    leave(13)
    expand(1, act1b, slope1, act1a.shape[1])
    leave(14)
    leave(16)
    copies[8].wait()
    expand(0, act0, slope0, 0)
    leave(12)
    leave(15)
    wait_all(leaving)


def hidden_back_kernel(grad_ref, mods, fc2_bias, *refs):
    ins, outs, held, rest = split_refs(refs, [9, 5, 3])
    slope_s, fc2_w, act0, act1a, act1b, grad_out_ref, middle_ref, in_sems, out_sems = rest
    slope0, slope1, fc2_0, fc2_1 = ins[:4]
    pre0, pre1a, pre1b = held
    output, mod_out = outs[3:]
    cut = pre1a.shape[1]
    pairs = []
    for side in (1, 0):
        fc2, slope = (fc2_0, slope0) if side == 0 else (fc2_1, slope1)
        for at in (slice(0, cut), slice(cut, 2 * cut)):
            pairs.append((fc2.at[at, :], fc2_w.at[side, at, :]))
            pairs.append((slope.at[:, at], slope_s.at[side, :, at]))
    pairs += list(zip(ins[4:], (act0, act1a, act1b, grad_out_ref, middle_ref)))
    copies = start_copies(pairs, in_sems)
    leaving = []
    for side, pre, at, first_col in (
        (1, pre1a, slice(0, cut), 0),
        (1, pre1b, slice(cut, 2 * cut), 0),
        (0, pre0, slice(0, cut), 0),
        (0, pre0, slice(cut, 2 * cut), cut),
    ):
        step = 2 * (1 - side) + at.start // cut
        copies[2 * step].wait()
        copies[2 * step + 1].wait()
        for to in tiles(cut, 512):
            cols = slice(at.start + to.start, at.start + to.stop)
            grad = dot_nt(grad_ref[...], fc2_w[side, cols, :])
            pre[:, first_col + to.start : first_col + to.stop] = (
                grad * slope_s[side, :, cols].astype(f32)
            ).astype(bf16)
        if step < 2 or step == 3:
            index = {0: 1, 1: 2, 3: 0}[step]
            leaving += start_copies([(held[index], outs[index])], out_sems.at[pl.ds(index, 1)])
    wait_all(copies[8:])
    for at in tiles(middle_ref.shape[1], 512):
        value = (
            dot(act0[...], fc2_w[0, :, at])
            + dot(act1a[...], fc2_w[1, :cut, at])
            + dot(act1b[...], fc2_w[1, cut:, at])
            + fc2_bias[:, at]
        )
        output[:, at] = (middle_ref[:, at] + mods[1:2, at] * value).astype(bf16)
        mod_out[0:1, at] = jnp.sum(grad_out_ref[:, at].astype(f32) * value, axis=0, keepdims=True)
    wait_all(leaving)


def row_back_kernel(mods, mult, *refs):
    ins, outs, held, got, rest = split_refs(refs, [16, 6, 6, 16])
    h2_s, mixed_s, in_sems, out_sems = rest
    copies = start_copies(list(zip(ins, got)), in_sems)
    leaving = []

    def leave(index):
        copy = pltpu.make_async_copy(held[index], outs[index], out_sems.at[index])
        copy.start()
        leaving.append(copy)

    pre0, fc1_0, pre1a, pre1b, fc1_1, middle_ref, grad_out_ref, attn_ref = got[:8]
    proj_0, proj_1, qn_ref, kn_ref, v_ref, p_ref, rq_ref, rk_ref = got[8:]
    middle_grad, attn_grad, qkv_grad0, qkv1a, qkv1b, small = held
    rows, width = middle_ref.shape
    half = width // 2
    heads = half // HEAD_DIM
    copies[0].wait()
    copies[1].wait()
    for at in tiles(width, 512):
        h2_s[:, at] = dot_nt(pre0[...], fc1_0[at, :])
    wait_all(copies[2:5])
    for at in tiles(width, 512):
        total = h2_s[:, at]
        for index, pre in enumerate((pre1a, pre1b)):
            cut = pre.shape[1]
            total = total + dot_nt(pre[...], fc1_1[at, index * cut : (index + 1) * cut])
        h2_s[:, at] = total
    wait_all(copies[5:8])
    normed, spread = normalize(middle_ref[...])
    grad = h2_s[...]
    small[0:1, :] = jnp.sum(grad * normed, axis=0, keepdims=True)
    small[1:2, :] = jnp.sum(grad, axis=0, keepdims=True)
    total = grad_out_ref[...].astype(f32) + norm_back(
        grad * (1.0 + mods[3:4, :]), normed, spread
    )
    middle_grad[...] = total
    leave(0)
    small[2:3, :] = jnp.sum(total * attn_ref[...], axis=0, keepdims=True)
    attn_grad[...] = (mods[0:1, :] * total).astype(bf16)
    leave(1)
    first = lax.broadcasted_iota(jnp.int32, (rows, LANES), 1) < HEAD_DIM
    cut = qkv1a.shape[1]

    def put(side, start, values):
        if side == 0:
            qkv_grad0[:, start : start + LANES] = values
        else:
            index, to = start // cut, start % cut
            (qkv1a, qkv1b)[index][:, to : to + LANES] = values

    wait_all(copies[8:])
    for side in (1, 0):
        mixed_s[...] = dot_nt(attn_grad[...], (proj_0, proj_1)[side][...]).astype(bf16)
        for pair in range(half // LANES):
            at = slice(pair * LANES, (pair + 1) * LANES)
            mixed = mixed_s[:, at]
            q_low, k_low, v_low = qn_ref[side, :, at], kn_ref[side, :, at], v_ref[side, :, at]
            parts = []
            for head in range(2):
                own = first if head == 0 else jnp.logical_not(first)
                probs = p_ref[side * heads + 2 * pair + head]
                prob_grad = dot_nt(jnp.where(own, v_low, jnp.zeros_like(v_low)), mixed)
                centred = jnp.sum(prob_grad * probs, axis=0, keepdims=True)
                score_grad = (probs * (prob_grad - centred)).astype(bf16)
                parts.append(
                    (dot_tn(score_grad, k_low), dot(score_grad, q_low), dot(probs.astype(bf16), mixed))
                )
            query_grad, key_grad, value_grad = [
                jnp.where(first, low, high).astype(bf16) for low, high in zip(*parts)
            ]
            scaled = mult[side : side + 1, at]
            query_unit = q_low.astype(f32) * (1.0 / scaled)
            key_unit = k_low.astype(f32)
            unit_grad = query_grad.astype(f32) * scaled
            key_grad = key_grad.astype(f32)
            cross = unit_grad * query_unit
            small[3:4, side * half + pair * LANES : side * half + (pair + 1) * LANES] = jnp.sum(
                cross, axis=0, keepdims=True
            )
            query_pre = rq_ref[side, :, at] * (unit_grad - query_unit * half_sums(cross, first))
            key_pre = rk_ref[side, :, at] * (
                key_grad - key_unit * half_sums(key_grad * key_unit, first)
            )
            put(side, pair * LANES, query_pre.astype(bf16))
            put(side, half + pair * LANES, key_pre.astype(bf16))
            put(side, 2 * half + pair * LANES, value_grad)
        for index in (3, 4) if side == 1 else (2, 5):
            leave(index)
    wait_all(leaving)


def input_back_kernel(mods, *refs):
    ins, outs, got, rest = split_refs(refs, [11, 2, 11])
    tokens_grad, mod_out = outs
    sum_s, in_sems = rest
    copies = start_copies(list(zip(ins, got)), in_sems)
    qkv_grad0, qkv1a, qkv1b, x_ref, middle_grad = got[:5]
    weights = got[5:]
    width = x_ref.shape[1]
    half, cut = width // 2, qkv1a.shape[1]
    wait_all(copies[:4])
    normed, spread = normalize(x_ref[...].astype(f32))
    wait_all(copies[4:])
    for at in tiles(width, 512):
        total = jnp.zeros((x_ref.shape[0], at.stop - at.start), f32)
        for part in range(3):
            total = total + dot_nt(
                qkv_grad0[:, part * half : (part + 1) * half], weights[part][at, :]
            )
        for start in range(0, 3 * half, half // 2):
            piece = (qkv1a, qkv1b)[start // cut][:, start % cut : start % cut + half // 2]
            inner = start % half
            total = total + dot_nt(piece, weights[3 + start // half][at, inner : inner + half // 2])
        sum_s[:, at] = total
    grad = sum_s[...]
    mod_out[0:1, :] = jnp.sum(grad * normed, axis=0, keepdims=True)
    mod_out[1:2, :] = jnp.sum(grad, axis=0, keepdims=True)
    tokens_grad[...] = (
        middle_grad[...] + norm_back(grad * (1.0 + mods[2:3, :]), normed, spread)
    ).astype(bf16)


def column_tiles(rights, flow):
    start = 0
    for source, (near, *pieces) in enumerate(rights):
        quarter, cut = near.shape[1] // 4, pieces[0].shape[1]
        for step in range(2):
            at = (2 * flow + step) * quarter
            to = start + step * quarter
            far = pieces[at // cut][:, at % cut : at % cut + quarter]
            both = jnp.concatenate([near[:, at : at + quarter], far], axis=0)
            yield source, both, slice(at, at + quarter), slice(to, to + quarter)
        start += 2 * quarter


def split_refs(refs, counts):
    out = []
    for count in counts:
        out.append(refs[:count])
        refs = refs[count:]
    return out + [refs]


def grad_kernel(pieces, bit_ref, *refs):
    sources = len(pieces)
    count = sum(pieces) + 3 * sources
    far, outs, got, held, rest = split_refs(refs, [count, 3 * sources + 2, count, sources + 2])
    *ins, _ = split_refs(got, [3 + count for count in pieces])
    picked, in_sems, out_sems = rest
    copies = start_copies(list(zip(far, got)), in_sems)
    waits = []
    for piece in pieces:
        waits.append(copies[: 3 + piece])
        copies = copies[3 + piece :]
    left_sums, right_sums = outs[:sources], outs[sources : 2 * sources]
    left_t, (sent_a, sent_b) = held[:sources], held[sources:]
    leaving = []

    def leave(index):
        copy = pltpu.make_async_copy(held[index], outs[2 * sources + index], out_sems.at[index])
        copy.start()
        leaving.append(copy)

    moved, part, columns = sent_a.shape
    tokens, half = ins[0][0].shape[0], ins[0][0].shape[1] // 2
    depth = 2 * tokens
    ones = jnp.ones((8, depth), bf16)
    for source in range(sources):
        wait_all(waits[source][:2])
        for side in range(2):
            cols = slice(side * half, (side + 1) * half)
            near, far = ins[source][0][:, cols], ins[source][1][:, cols]
            rows = slice(side * moved, (side + 1) * moved)
            left_sums[source][:, cols] = dot(ones, jnp.concatenate([near, far], axis=0))[0:1]
            left_t[source][rows, :, :tokens] = near.T.reshape(moved, part, tokens)
            left_t[source][rows, :, tokens:] = far.T.reshape(moved, part, tokens)
        leave(source)
    rights = [refs[2:] for refs in ins]
    for source in range(sources):
        wait_all(waits[source][2:])
    for flow, sent in enumerate((sent_a, sent_b)):
        away = 1 - bit_ref[flow]
        for source in range(sources):
            for row in range(moved):
                at = 2 * row + away if flow == 0 else (row // 2) * 4 + row % 2 + 2 * away
                picked[source, row] = left_t[source][at]
        for source, right, at, to in column_tiles(rights, flow):
            left = picked[source].reshape(moved * part, depth)
            sent[:, :, to] = dot(left, right).astype(bf16).reshape(moved, part, -1)
            right_sums[source][:, at] = dot(ones, right)[0:1]
        leave(sources + flow)
    wait_all(leaving)


def second_kernel(pieces, bit_ref, *refs):
    sources = len(pieces)
    count = 2 * sources + sum(pieces) + 2
    far, outs, got, held, rest = split_refs(refs, [count, 3, count, 3])
    left_t, *rights, (came_a, came_b) = split_refs(got, [sources] + [1 + count for count in pieces])
    sent_a, sent_b, own = held
    picked, in_sems, out_sems = rest
    copies = start_copies(list(zip(far, got)), in_sems)
    wait_all(copies[:-2])
    leaving = []
    moved, part, columns = sent_a.shape
    depth = left_t[0].shape[2]
    for flow, (came, sent) in enumerate(((came_a, sent_a), (came_b, sent_b))):
        copies[flow - 2].wait()
        mine, away = bit_ref[flow], 1 - bit_ref[1 - flow]
        for source in range(sources):
            for row in range(moved):
                if flow == 0:
                    base, other = 4 * row + mine, 2
                else:
                    base, other = 4 * row + 2 * mine, 1
                picked[source, row] = left_t[source][base + other * away]
                picked[source, moved + row] = left_t[source][base + other * (1 - away)]
        for source, right, at, to in column_tiles(rights, flow):
            left = picked[source].reshape(2 * moved * part, depth)
            block = dot(left, right).reshape(2 * moved, part, -1)
            kept = slice(flow * columns + to.start, flow * columns + to.stop)
            for row in range(moved):
                sent[row, :, to] = (block[row] + came[2 * row + away, :, to].astype(f32)).astype(
                    bf16
                )
                own[row, :, kept] = (
                    block[moved + row] + came[2 * row + 1 - away, :, to].astype(f32)
                ).astype(bf16)
        leaving += start_copies([(held[flow], outs[flow])], out_sems.at[pl.ds(flow, 1)])
    leaving += start_copies([(own, outs[2])], out_sems.at[pl.ds(2, 1)])
    wait_all(leaving)


def third_kernel(bit, bit_ref, own, *refs):
    came, (sent, kept) = refs[:-2], refs[-2:]
    mine = bit_ref[bit]
    start = 0
    for part in came:
        to = slice(start, start + part.shape[2])
        start += part.shape[2]
        for row in range(sent.shape[0]):
            away, near = 2 * row + 1 - mine, 2 * row + mine
            sent[row, :, to] = (own[away, :, to].astype(f32) + part[away].astype(f32)).astype(bf16)
            kept[row, :, to] = (own[near, :, to].astype(f32) + part[near].astype(f32)).astype(kept.dtype)


def local_call(kernel, limit, outs, scratch, kinds, *values, out_kind="v", flops=1):
    places = {
        "s": pl.BlockSpec(memory_space=pltpu.SMEM),
        "v": pl.BlockSpec(memory_space=pltpu.VMEM),
        "h": pl.BlockSpec(memory_space=pl.ANY),
    }
    return pl.pallas_call(
        kernel,
        out_shape=outs,
        in_specs=[places[kind] for kind in kinds],
        out_specs=[places[kind] for kind in (out_kind if len(out_kind) > 1 else out_kind * len(outs))],
        scratch_shapes=scratch,
        compiler_params=pltpu.CompilerParams(vmem_limit_bytes=limit * 2**20),
        cost_estimate=pl.CostEstimate(flops=flops, bytes_accessed=1, transcendentals=0),
    )(*values)


def normalize(values):
    mean = jnp.mean(values, axis=1, keepdims=True)
    spread = jnp.mean(values * values, axis=1, keepdims=True) - mean * mean
    scale = lax.rsqrt(spread + norm_eps)
    return (values - mean) * scale, scale


def norm_back(grad, normed, scale):
    return scale * (
        grad
        - jnp.mean(grad, axis=1, keepdims=True)
        - normed * jnp.mean(grad * normed, axis=1, keepdims=True)
    )


def gelu_parts(pre):
    square = pre * pre
    tanh = jnp.tanh(pre * (gelu_c + gelu_c * gelu_a * square))
    gate = 0.5 + 0.5 * tanh
    slope = gate + pre * (0.5 - 0.5 * tanh * tanh) * (gelu_c + 3.0 * gelu_c * gelu_a * square)
    return pre * gate, slope


def shards(
    tokens,
    class_ids,
    final_scale,
    row_slots,
    class_table,
    ada_weight,
    ada_bias,
    qkv_weight,
    qv_bias,
    log_scale,
    proj_weight,
    proj_bias,
    fc1_weight,
    fc1_bias,
    fc2_weight,
    fc2_bias,
    out_grad,
):
    groups = lax.axis_size("dp")
    bits = groups.bit_length() - 1
    here = lax.axis_index("dp")
    core = lax.axis_index("mp")
    micro, row_len, half = tokens.shape
    width = 2 * half
    share = row_len // groups
    heads = log_scale.shape[0]
    hidden = fc1_weight.shape[1]

    def swap(values):
        return lax.ppermute(values, "mp", [(0, 1), (1, 0)])

    def flip(values, bit):
        return lax.ppermute(values, "dp", [(i, i ^ (1 << bit)) for i in range(groups)])

    def in_order(own, other, axis):
        return jnp.where(
            core == 0,
            jnp.concatenate([own, other], axis),
            jnp.concatenate([other, own], axis),
        )

    class_picks = (
        class_ids.reshape(-1)[:, None] == jnp.arange(class_table.shape[0], dtype=jnp.int32)[None, :]
    )
    condition = dot(class_picks.astype(bf16), class_table)
    lifted = jax.nn.silu(condition).astype(bf16)
    ada_half = lax.dynamic_slice_in_dim(ada_weight, core * half, half, 2)
    ada_terms = dot(lifted, ada_half.reshape(ada_half.shape[0], 6 * half))
    ada_terms = ada_terms.reshape(micro, groups, 6, half)
    ada_round = lax.reduce_precision(ada_terms, 8, 7)
    ada_rest = jnp.stack([ada_terms[:, :, c] - ada_round[:, :, c] for c in (2, 4)], axis=2)
    ada_sent = jnp.concatenate([ada_round, ada_rest], axis=2).astype(bf16)

    def by_target(values):
        return values.reshape(micro, groups, -1, half).swapaxes(0, 1).reshape(2 * groups, -1, half)

    def exchange(values):
        return lax.all_to_all(values, ("dp", "mp"), split_axis=0, concat_axis=0, tiled=True)

    def to_row(values):
        return (
            values.reshape(groups, 2, share, half).transpose(0, 2, 1, 3).reshape(row_len, width)
        )

    first_message = jnp.concatenate([by_target(tokens), by_target(ada_sent)], axis=1)
    arrived = exchange(first_message)

    def after(values, *earlier):
        return lax.optimization_barrier((values, earlier))[0]

    small = jnp.concatenate(
        [ada_bias.reshape(-1), qv_bias.reshape(-1), log_scale, proj_bias, fc1_bias, fc2_bias]
    )
    small_sizes = [6 * half, 2 * half, heads, half, hidden, half]

    def unpack(flat):
        starts = [sum(small_sizes[:i]) for i in range(7)]
        return [flat[starts[i] : starts[i + 1]] for i in range(6)]

    own_small, oth_small = unpack(small), unpack(swap(small))
    qkv_w = [qkv_weight[:, part] for part in range(3)]
    qkv_w += [swap(weight) for weight in qkv_w]
    proj_w = (proj_weight, swap(proj_weight))
    fc1_w = (fc1_weight, swap(fc1_weight))
    fc2_w = (fc2_weight, swap(fc2_weight))
    ada_shift = in_order(own_small[0].reshape(6, half), oth_small[0].reshape(6, half), 1)
    proj_shift = in_order(own_small[3], oth_small[3], 0)
    fc2_shift = in_order(own_small[5], oth_small[5], 0)
    fc1_shift = jnp.stack([own_small[4], oth_small[4]])
    qkv_shift = jnp.stack(
        [
            jnp.concatenate([part[1][:half], jnp.zeros((half,), f32), part[1][half:]])
            for part in (own_small, oth_small)
        ]
    )
    head_mult = jnp.stack([jnp.repeat(jnp.exp(part[2]), HEAD_DIM) for part in (own_small, oth_small)])

    segments, levels = slot_layout(
        lax.dynamic_index_in_dim(final_scale[:, 0], core, 0, keepdims=False),
        lax.dynamic_index_in_dim(row_slots[:, 0], core, 0, keepdims=False),
    )
    mask = (
        (segments[:, None] == segments[None, :]) & (levels[:, None] <= levels[None, :])
    ).astype(f32)

    grads_arrived = exchange(
        after(by_target(out_grad), arrived, qkv_shift, head_mult, mask, proj_shift, fc1_shift, fc2_shift)
    )

    def array(*dims, kind=bf16):
        return jax.ShapeDtypeStruct(dims, kind)

    vmem, dma = pltpu.VMEM, pltpu.SemaphoreType.DMA

    def scratch(arrays):
        return [vmem(value.shape, value.dtype) for value in arrays]

    wide = array(2, row_len, half)
    wide32 = array(2, row_len, half, kind=f32)
    whole_tiles = share % 16 == 0
    if whole_tiles:
        row_in, ada_in = arrived, ada_shift
    else:
        row_in = to_row(arrived[:, :share])
        terms = jnp.sum(arrived[:, share:].reshape(groups, 2, 8, half).astype(f32), axis=0)
        terms = terms.transpose(1, 0, 2).reshape(8, width)
        ada_in = (ada_shift + terms[:6]).at[2].add(terms[6]).at[4].add(terms[7])
    kept = [
        array(row_len, width),
        wide,
        wide,
        wide,
        wide32,
        wide32,
        array(2 * heads, row_len, row_len, kind=f32),
        array(row_len, half),
        array(row_len, half),
        array(row_len, width, kind=f32),
        array(row_len, width, kind=f32),
        array(row_len, width),
        array(row_len, hidden),
        array(row_len, hidden // 2),
        array(row_len, hidden // 2),
        array(row_len, hidden),
        array(row_len, hidden),
    ]
    h1, qn, kn, vn, rq, rk, probs, mixed0, mixed1, attn, middle, h2, act0, *more = local_call(
        functools.partial(forward_kernel, share if whole_tiles else 0),
        56,
        kept + [array(row_len, width), array(6, width, kind=f32)],
        scratch(kept)
        + [
            vmem((2, 3, width, half), bf16),
            vmem((2, half, width), bf16),
            vmem((2, width, hidden), bf16),
            vmem((row_len, 3 * half), f32),
            dma((10,)),
            dma((23,)),
        ],
        "vvvvvvv" + "h" * 10,
        row_in,
        ada_in,
        qkv_shift,
        head_mult,
        mask,
        proj_shift[None],
        fc1_shift,
        *qkv_w,
        *proj_w,
        *fc1_w,
        out_kind="h" * len(kept) + "vv",
    )
    act1, (slope0, slope1, resident, mods) = more[:2], more[2:]

    own_bits = jnp.stack([(here >> bit) & 1 for bit in range(bits)])
    part = width // groups

    def source(near_left, far_left, near_right, sent_right):
        return (near_left, far_left, near_right, *[swap(values) for values in sent_right])

    def scatter_start(*sources):
        count = len(sources)
        pieces = [len(source) - 3 for source in sources]
        columns = sum(source[2].shape[1] for source in sources) // 2
        ins = [value for source in sources for value in source]
        kept = [array(groups, part, 2 * row_len)] * count + [
            array(groups // 2, part, columns)
        ] * 2
        outs = local_call(
            functools.partial(grad_kernel, pieces),
            56,
            [array(1, width, kind=f32)] * count
            + [array(1, source[2].shape[1], kind=f32) for source in sources]
            + kept,
            scratch(ins)
            + scratch(kept)
            + [
                vmem((count, groups // 2, part, 2 * row_len), bf16),
                dma((len(ins),)),
                dma((len(kept),)),
            ],
            "s" + "h" * len(ins),
            own_bits,
            *ins,
            out_kind="v" * (2 * count) + "h" * len(kept),
        )
        left_sums, right_sums = outs[:count], outs[count : 2 * count]
        rest = list(outs[2 * count : 3 * count])
        rest += [value for source in sources for value in source[2:]]
        return left_sums, right_sums, (pieces, rest), tuple(outs[3 * count :])

    def travel(sent):
        return flip(sent[0], 0), flip(sent[1], 1)

    def scatter_second(started, came, flops=1):
        pieces, rest = started
        count = len(pieces)
        columns = came[0].shape[2]
        ins = [*rest, *came]
        kept = [array(groups // 4, part, columns)] * 2 + [array(groups // 4, part, 2 * columns)]
        sent_a, sent_b, own = local_call(
            functools.partial(second_kernel, pieces),
            56,
            kept,
            scratch(ins)
            + scratch(kept)
            + [
                vmem((count, groups // 2, part, 2 * row_len), bf16),
                dma((len(ins),)),
                dma((3,)),
            ],
            "s" + "h" * len(ins),
            own_bits,
            *ins,
            out_kind="h",
            flops=flops,
        )
        return own, (sent_a, sent_b)

    def scatter_more(bit, own, came):
        rows, _, columns = own.shape
        sent, own = local_call(
            functools.partial(third_kernel, bit),
            56,
            [
                array(rows // 2, part, columns),
                array(rows // 2, part, columns, kind=f32 if bit == bits - 1 else bf16),
            ],
            [],
            "sv" + "v" * len(came),
            own_bits,
            own,
            *came,
        )
        return own, sent

    def scatter_end(begin, own, came):
        for bit in range(begin, bits):
            own, sent = scatter_more(bit, own, came)
            came = (flip(sent, bit),)
        return own[0] + came[0][0].astype(f32)

    grad_out = to_row(after(grads_arrived, act0))
    grad_branch = (mods[1:2] * grad_out.astype(f32)).astype(bf16)
    fc2_left, _, fc2_rest, fc2_sent = scatter_start(
        source(grad_branch, swap(grad_branch), act0, act1)
    )
    h1_far, h2_far, mixed_far = swap(h1), swap(h2), swap(mixed1)
    fc2_came = travel(fc2_sent)

    pre_kept = [array(row_len, hidden)] + [array(row_len, hidden // 2)] * 2
    branch_ins = [act0, *act1, grad_out, middle]
    pre0, *pre1, output, branch_mods = local_call(
        hidden_back_kernel,
        56,
        pre_kept + [array(row_len, width), array(1, width, kind=f32)],
        scratch(pre_kept)
        + [vmem((2, row_len, hidden), bf16), vmem((2, hidden, width), bf16)]
        + scratch(branch_ins)
        + [dma((13,)), dma((3,))],
        "vvv" + "h" * 9,
        after(grad_branch, fc2_sent, h1_far, h2_far, mixed_far),
        mods,
        fc2_shift[None],
        slope0,
        slope1,
        *fc2_w,
        *branch_ins,
        out_kind="hhhvv",
    )
    _, fc1_right, fc1_rest, fc1_sent = scatter_start(
        source(h2, h2_far, pre0, pre1)
    )
    fc1_came = travel(fc1_sent)
    def to_target(values):
        return (
            values.reshape(groups, share, 2, half).transpose(0, 2, 1, 3).reshape(-1, share, half)
        )

    fc2_own, fc2_sent = scatter_second(fc2_rest, after(fc2_came, fc1_sent), int(3e9))
    fc2_came = travel(fc2_sent[::-1])[::-1]
    row_ins = [
        after(pre0, fc2_sent),
        fc1_w[0],
        *pre1,
        fc1_w[1],
        middle,
        grad_out,
        attn,
        *proj_w,
        qn,
        kn,
        vn,
        probs,
        rq,
        rk,
    ]
    row_kept = [
        array(row_len, width, kind=f32),
        array(row_len, width),
        array(row_len, 3 * half),
        array(row_len, 3 * half // 2),
        array(row_len, 3 * half // 2),
        array(4, width, kind=f32),
    ]
    middle_grad, attn_grad, qkv_grad0, qkv1a, qkv1b, row_mods = local_call(
        row_back_kernel,
        56,
        row_kept,
        scratch(row_kept)
        + scratch(row_ins)
        + [vmem((row_len, width), f32), vmem((row_len, half), bf16), dma((16,)), dma((6,))],
        "vv" + "h" * 16,
        mods,
        head_mult,
        *row_ins,
        out_kind="h",
    )
    fc1_own, fc1_sent = scatter_second(fc1_rest, after(fc1_came, attn_grad))
    ready = after((qkv1a, qkv1b, attn_grad), fc2_came, fc1_sent)
    fc1_came = travel(fc1_sent[::-1])[::-1]
    fc2_own, fc2_sent = scatter_more(2, fc2_own, fc2_came)
    fc2_came = (flip(fc2_sent, 2),)
    qkv_left, qkv_right, qkv_rest, qkv_sent = scatter_start(
        after(source(h1, h1_far, qkv_grad0, ready[:2]), fc2_sent),
        (attn_grad, swap(ready[2]), mixed0, mixed_far),
    )
    qkv_came = travel(qkv_sent)
    fc2_own, fc2_sent = scatter_more(3, fc2_own, after(fc2_came, qkv_sent))
    fc2_came = (flip(fc2_sent, 3),)
    end_ins = [
        after(qkv_grad0, fc1_came, fc2_sent),
        qkv1a,
        qkv1b,
        resident,
        middle_grad,
        *qkv_w,
    ]
    tokens_grad, end_mods = local_call(
        input_back_kernel,
        56,
        [array(row_len, width), array(2, width, kind=f32)],
        scratch(end_ins) + [vmem((row_len, width), f32), dma((11,))],
        "v" + "h" * 11,
        mods,
        *end_ins,
    )

    row_grads = jnp.stack(
        [row_mods[2], branch_mods[0], end_mods[0], row_mods[0], end_mods[1], row_mods[1]]
    ).astype(bf16)
    scale_terms = jnp.sum(row_mods[3].reshape(2, heads, HEAD_DIM), axis=2)
    scale_sum = scale_terms[0] + swap(scale_terms[1])

    def own_half(values):
        return lax.dynamic_slice_in_dim(values, core * half, half, 0)

    bias_sum = jnp.concatenate(
        [
            qkv_right[0][0, :half],
            qkv_right[0][0, 2 * half :],
            own_half(qkv_left[1][0]),
            fc1_right[0][0],
            own_half(fc2_left[0][0]),
            scale_sum,
        ]
    )

    def double(gathered, bias_sum, bit):
        rounded = bias_sum.astype(bf16)
        count = gathered.size
        came = flip(jnp.concatenate([gathered.reshape(-1), rounded]), bit)
        theirs = came[:count].reshape(gathered.shape)
        mine = (here >> bit) & 1
        both = jnp.where(mine == 0, jnp.stack([gathered, theirs]), jnp.stack([theirs, gathered]))
        return both, rounded.astype(f32) + came[count:].astype(f32)

    gathered, bias_sum = double(row_grads.reshape(6 * width), bias_sum, 2)
    returned = exchange(
        jnp.concatenate(
            [to_target(values) for values in after((output, tokens_grad))], axis=1
        )
    )
    qkv_own, qkv_sent = scatter_second(
        qkv_rest, after(qkv_came, fc1_came, fc2_came, gathered)
    )
    qkv_came = travel(qkv_sent[::-1])[::-1]
    fc1_own, fc1_sent = scatter_more(2, fc1_own, after(fc1_came, qkv_sent))
    fc1_came = (flip(fc1_sent, 2),)
    gathered = after(gathered, qkv_sent)
    for bit in range(3, bits):
        gathered, bias_sum = double(gathered, bias_sum, bit)
    qkv_own, qkv_sent = scatter_more(2, qkv_own, after(qkv_came, fc1_came, gathered, returned))
    qkv_came = (flip(qkv_sent, 2),)
    fc1_own, fc1_sent = scatter_more(3, fc1_own, after(fc1_came, qkv_sent))
    fc1_came = (flip(fc1_sent, 3),)
    gathered = after(gathered, fc1_sent)
    for bit in range(2):
        gathered, bias_sum = double(gathered, bias_sum, bit)
    gathered = gathered.transpose(*range(2, bits), 0, 1, bits).reshape(groups, 6 * width)
    qkv_own, qkv_sent = scatter_more(3, qkv_own, after(qkv_came, fc1_came, gathered))
    qkv_came = (flip(qkv_sent, 3),)
    gathered = after(gathered, qkv_sent)
    gathered = in_order(gathered, swap(gathered), 0)
    fc2_sum = scatter_end(4, fc2_own, fc2_came)
    fc1_sum = scatter_end(4, fc1_own, fc1_came)
    qkv_sum = scatter_end(4, qkv_own, qkv_came)

    ada_weight_grad = dot_tn(lifted, gathered).reshape(ada_weight.shape)
    ada_bias_grad = jnp.sum(gathered.astype(f32), axis=0).reshape(6, width)
    grad_lifted = dot_nt(gathered, ada_weight.reshape(ada_weight.shape[0], 6 * width))
    _, silu_pull = jax.vjp(jax.nn.silu, condition)
    table_grad = lax.dot_general(
        class_picks.astype(f32),
        silu_pull(grad_lifted)[0],
        (((0,), (0,)), ((), ())),
        precision=lax.Precision.HIGHEST,
    )

    def from_rows(values):
        return values.reshape(groups, 2, share, half).swapaxes(0, 1).reshape(2, row_len, half)

    qkv_cols, proj_cols = 3 * half // 2, half // 2
    turn = qkv_cols + proj_cols
    qkv_own_sum = jnp.concatenate([qkv_sum[:, :qkv_cols], qkv_sum[:, turn : turn + qkv_cols]], 1)
    proj_sum = jnp.concatenate([qkv_sum[:, qkv_cols:turn], qkv_sum[:, turn + qkv_cols :]], 1)
    ends = [half, 2 * half, 3 * half, 3 * half + hidden, 4 * half + hidden]
    return (
        from_rows(returned[:, :share]),
        from_rows(returned[:, share:]),
        table_grad,
        ada_weight_grad,
        ada_bias_grad,
        qkv_own_sum.reshape(-1, 3, half),
        bias_sum[: ends[1]].reshape(2, half),
        bias_sum[ends[4] :],
        proj_sum.T,
        bias_sum[ends[1] : ends[2]],
        fc1_sum,
        bias_sum[ends[2] : ends[3]],
        fc2_sum.T,
        bias_sum[ends[3] : ends[4]],
    )


def solution(mesh):
    placed = (
        P(None, "dp", "mp"),
        P(),
        P(None, "dp", None),
        P(None, "dp", None),
        P(None, "dp"),
        P("dp", None, None),
        P(None, "mp"),
        P(None, None, "mp"),
        P(None, "mp"),
        P("mp"),
        P("mp", None),
        P("mp"),
        P(None, "mp"),
        P("mp"),
        P("mp", None),
        P("mp"),
        P(None, "dp", "mp"),
    )
    return jax.shard_map(
        shards,
        mesh=mesh,
        in_specs=placed,
        out_specs=(
            P(None, "dp", "mp"),
            P(None, "dp", "mp"),
            P(None, "dp"),
            P("dp", None, None),
            P(),
            P("dp", None, "mp"),
            P(None, "mp"),
            P("mp"),
            P("mp", "dp"),
            P("mp"),
            P("dp", "mp"),
            P("mp"),
            P("mp", "dp"),
            P("mp"),
        ),
        check_vma=False,
    )
```

```python
import functools

import jax
import jax.numpy as jnp
from jax import lax
from jax.experimental import pallas as pl
from jax.experimental.pallas import tpu as pltpu
from jax.sharding import PartitionSpec as P

HEAD_DIM = 64
LANES = 128
scale_ends = (1, 5, 14, 30, 55, 91, 155, 255, 424, 680)
norm_eps = 1e-06
unit_eps = 1e-06
bf16 = jnp.bfloat16
f32 = jnp.float32
gelu_c = 0.7978845608028654
gelu_a = 0.044715


def slot_layout(final_row, slots_row):
    ends_table = jnp.asarray(scale_ends, dtype=jnp.int32)
    chosen = final_row[:, None] == jnp.arange(len(scale_ends), dtype=jnp.int32)[None, :]
    lengths = jnp.sum(jnp.where(chosen, ends_table[None, :], 0), axis=1)
    items = final_row.shape[0]
    before = jnp.arange(items)[:, None] <= jnp.arange(items)[None, :]
    item_ends = jnp.sum(jnp.where(before, lengths[:, None], 0), axis=0)
    passed = slots_row[:, None] >= item_ends[None, :]
    segment = jnp.sum(passed.astype(jnp.int32), axis=1)
    item_start = jnp.sum(jnp.where(passed, lengths[None, :], 0), axis=1)
    offset = slots_row - item_start
    level = jnp.sum((offset[:, None] >= ends_table[None, :]).astype(jnp.int32), axis=1)
    return segment, jnp.where(segment == items, 0, level)


def dot(a, b):
    return jnp.dot(a, b, preferred_element_type=f32)


def dot_nt(a, b):
    return lax.dot_general(a, b, (((1,), (1,)), ((), ())), preferred_element_type=f32)


def dot_tn(a, b):
    return lax.dot_general(a, b, (((0,), (0,)), ((), ())), preferred_element_type=f32)


def half_sums(values, first):
    low = jnp.sum(jnp.where(first, values, 0.0), axis=1, keepdims=True)
    high = jnp.sum(jnp.where(first, 0.0, values), axis=1, keepdims=True)
    return jnp.where(first, low, high)


def head_parts(queries, keys, mult, first):
    query_scale = lax.rsqrt(half_sums(queries * queries, first) + unit_eps)
    key_scale = lax.rsqrt(half_sums(keys * keys, first) + unit_eps)
    return queries * query_scale * mult, keys * key_scale, query_scale, key_scale


def start_copies(pairs, sems):
    copies = [pltpu.make_async_copy(src, dst, sems.at[i]) for i, (src, dst) in enumerate(pairs)]
    for copy in copies:
        copy.start()
    return copies


def wait_all(copies):
    for copy in copies:
        copy.wait()


def tiles(size, most):
    tile = min(most, size)
    return [slice(start, start + tile) for start in range(0, size, tile)]


def forward_kernel(
    share, arrived, ada_ref, qkv_bias, mult, mask_ref, proj_bias, fc1_bias, *refs
):
    weights, outs, (x_ref, mods), held, rest = split_refs(refs, [10, 17, 2, 17])
    qkv_w, proj_w, fc1_w, qkv_s, in_sems, out_sems = rest
    copies = start_copies(
        [(weights[i], qkv_w.at[i // 3, i % 3]) for i in range(6)]
        + [(weights[6 + i], proj_w.at[i]) for i in range(2)]
        + [(weights[8 + i], fc1_w.at[i]) for i in range(2)],
        in_sems,
    )
    leaving = []

    def leave(index, *at):
        src, dst = held[index], outs[index]
        if at:
            src, dst = src.at[at], dst.at[at]
        copy = pltpu.make_async_copy(src, dst, out_sems.at[len(leaving)])
        copy.start()
        leaving.append(copy)

    h1, qn_out, kn_out, v_out, rq_out, rk_out, p_out, mixed0, mixed1, attn_out = held[:10]
    middle_out, h2_out, act0, act1a, act1b, slope0, slope1 = held[10:]
    rows, width = x_ref.shape
    half = width // 2
    if share:
        for side in range(2):
            cols = slice(side * half, (side + 1) * half)
            terms = jnp.zeros((8, half), f32)
            for group in range(rows // share):
                block = arrived.at[2 * group + side]
                x_ref[group * share : (group + 1) * share, cols] = block[:share, :]
                terms = terms + block[share : share + 8, :].astype(f32)
            mods[:, cols] = ada_ref[:, cols] + terms[:6]
            mods[2:3, cols] = mods[2:3, cols] + terms[6:7]
            mods[4:5, cols] = mods[4:5, cols] + terms[7:8]
    else:
        x_ref[...] = arrived[...]
        mods[...] = ada_ref[...]
    x = x_ref[...].astype(f32)
    h1[...] = (normalize(x)[0] * (1.0 + mods[2:3, :]) + mods[4:5, :]).astype(bf16)
    leave(0)
    first = lax.broadcasted_iota(jnp.int32, (rows, LANES), 1) < HEAD_DIM
    mask = mask_ref[...]
    heads = half // HEAD_DIM
    for side, mixed_out in enumerate((mixed0, mixed1)):
        for part in range(3):
            copies[3 * side + part].wait()
            at = slice(part * half, (part + 1) * half)
            qkv_s[:, at] = dot(h1[...], qkv_w[side, part]) + qkv_bias[side : side + 1, at]
        for pair in range(half // LANES):
            at = slice(pair * LANES, (pair + 1) * LANES)
            qn, kn, query_scale, key_scale = head_parts(
                qkv_s[:, at],
                qkv_s[:, half + pair * LANES : half + (pair + 1) * LANES],
                mult[side : side + 1, at],
                first,
            )
            q_low, k_low = qn.astype(bf16), kn.astype(bf16)
            v_low = qkv_s[:, 2 * half + pair * LANES : 2 * half + (pair + 1) * LANES].astype(bf16)
            qn_out[side, :, at] = q_low
            kn_out[side, :, at] = k_low
            v_out[side, :, at] = v_low
            rq_out[side, :, at] = query_scale
            rk_out[side, :, at] = key_scale
            mixed = []
            for head in range(2):
                own = first if head == 0 else jnp.logical_not(first)
                scores = dot_nt(jnp.where(own, k_low, jnp.zeros_like(k_low)), q_low)
                raised = jnp.exp(scores) * mask
                weight = raised * (1.0 / jnp.sum(raised, axis=0, keepdims=True))
                p_out[side * heads + 2 * pair + head] = weight
                mixed.append(dot_tn(weight.astype(bf16), v_low))
            mixed_out[:, at] = jnp.where(first, mixed[0], mixed[1]).astype(bf16)
        leave(7 + side)
        for index in range(1, 6):
            leave(index, side)
        leave(6, pl.ds(side * heads, heads))
    copies[6].wait()
    copies[7].wait()
    attn_out[...] = dot(mixed0[...], proj_w[0]) + dot(mixed1[...], proj_w[1]) + proj_bias[...]
    leave(9)
    middle = x + mods[0:1, :] * attn_out[...]
    middle_out[...] = middle
    leave(10)
    h2_out[...] = (normalize(middle)[0] * (1.0 + mods[3:4, :]) + mods[5:6, :]).astype(bf16)
    leave(11)

    def expand(side, act, slope, first_col):
        for to in tiles(act.shape[1], 512):
            at = slice(first_col + to.start, first_col + to.stop)
            pre = dot(h2_out[...], fc1_w[side, :, at]) + fc1_bias[side : side + 1, at]
            value, rise = gelu_parts(pre)
            act[:, to] = value.astype(bf16)
            slope[:, at] = rise.astype(bf16)

    copies[9].wait()
    expand(1, act1a, slope1, 0)
    leave(13)
    expand(1, act1b, slope1, act1a.shape[1])
    leave(14)
    leave(16)
    copies[8].wait()
    expand(0, act0, slope0, 0)
    leave(12)
    leave(15)
    wait_all(leaving)


def hidden_back_kernel(grad_ref, mods, fc2_bias, *refs):
    ins, outs, held, rest = split_refs(refs, [9, 5, 3])
    slope_s, fc2_w, act0, act1a, act1b, grad_out_ref, middle_ref, in_sems, out_sems = rest
    slope0, slope1, fc2_0, fc2_1 = ins[:4]
    pre0, pre1a, pre1b = held
    output, mod_out = outs[3:]
    cut = pre1a.shape[1]
    pairs = []
    for side in (1, 0):
        fc2, slope = (fc2_0, slope0) if side == 0 else (fc2_1, slope1)
        for at in (slice(0, cut), slice(cut, 2 * cut)):
            pairs.append((fc2.at[at, :], fc2_w.at[side, at, :]))
            pairs.append((slope.at[:, at], slope_s.at[side, :, at]))
    pairs += list(zip(ins[4:], (act0, act1a, act1b, grad_out_ref, middle_ref)))
    copies = start_copies(pairs, in_sems)
    leaving = []
    for side, pre, at, first_col in (
        (1, pre1a, slice(0, cut), 0),
        (1, pre1b, slice(cut, 2 * cut), 0),
        (0, pre0, slice(0, cut), 0),
        (0, pre0, slice(cut, 2 * cut), cut),
    ):
        step = 2 * (1 - side) + at.start // cut
        copies[2 * step].wait()
        copies[2 * step + 1].wait()
        for to in tiles(cut, 512):
            cols = slice(at.start + to.start, at.start + to.stop)
            grad = dot_nt(grad_ref[...], fc2_w[side, cols, :])
            pre[:, first_col + to.start : first_col + to.stop] = (
                grad * slope_s[side, :, cols].astype(f32)
            ).astype(bf16)
        if step < 2 or step == 3:
            index = {0: 1, 1: 2, 3: 0}[step]
            leaving += start_copies([(held[index], outs[index])], out_sems.at[pl.ds(index, 1)])
    wait_all(copies[8:])
    for at in tiles(middle_ref.shape[1], 512):
        value = (
            dot(act0[...], fc2_w[0, :, at])
            + dot(act1a[...], fc2_w[1, :cut, at])
            + dot(act1b[...], fc2_w[1, cut:, at])
            + fc2_bias[:, at]
        )
        output[:, at] = (middle_ref[:, at] + mods[1:2, at] * value).astype(bf16)
        mod_out[0:1, at] = jnp.sum(grad_out_ref[:, at].astype(f32) * value, axis=0, keepdims=True)
    wait_all(leaving)


def row_back_kernel(mods, mult, *refs):
    ins, outs, held, got, rest = split_refs(refs, [16, 6, 6, 16])
    h2_s, mixed_s, in_sems, out_sems = rest
    copies = start_copies(list(zip(ins, got)), in_sems)
    leaving = []

    def leave(index):
        copy = pltpu.make_async_copy(held[index], outs[index], out_sems.at[index])
        copy.start()
        leaving.append(copy)

    pre0, fc1_0, pre1a, pre1b, fc1_1, middle_ref, grad_out_ref, attn_ref = got[:8]
    proj_0, proj_1, qn_ref, kn_ref, v_ref, p_ref, rq_ref, rk_ref = got[8:]
    middle_grad, attn_grad, qkv_grad0, qkv1a, qkv1b, small = held
    rows, width = middle_ref.shape
    half = width // 2
    heads = half // HEAD_DIM
    copies[0].wait()
    copies[1].wait()
    for at in tiles(width, 512):
        h2_s[:, at] = dot_nt(pre0[...], fc1_0[at, :])
    wait_all(copies[2:5])
    for at in tiles(width, 512):
        total = h2_s[:, at]
        for index, pre in enumerate((pre1a, pre1b)):
            cut = pre.shape[1]
            total = total + dot_nt(pre[...], fc1_1[at, index * cut : (index + 1) * cut])
        h2_s[:, at] = total
    wait_all(copies[5:8])
    normed, spread = normalize(middle_ref[...])
    grad = h2_s[...]
    small[0:1, :] = jnp.sum(grad * normed, axis=0, keepdims=True)
    small[1:2, :] = jnp.sum(grad, axis=0, keepdims=True)
    total = grad_out_ref[...].astype(f32) + norm_back(
        grad * (1.0 + mods[3:4, :]), normed, spread
    )
    middle_grad[...] = total
    leave(0)
    small[2:3, :] = jnp.sum(total * attn_ref[...], axis=0, keepdims=True)
    attn_grad[...] = (mods[0:1, :] * total).astype(bf16)
    leave(1)
    first = lax.broadcasted_iota(jnp.int32, (rows, LANES), 1) < HEAD_DIM
    cut = qkv1a.shape[1]

    def put(side, start, values):
        if side == 0:
            qkv_grad0[:, start : start + LANES] = values
        else:
            index, to = start // cut, start % cut
            (qkv1a, qkv1b)[index][:, to : to + LANES] = values

    wait_all(copies[8:])
    for side in (1, 0):
        mixed_s[...] = dot_nt(attn_grad[...], (proj_0, proj_1)[side][...]).astype(bf16)
        for pair in range(half // LANES):
            at = slice(pair * LANES, (pair + 1) * LANES)
            mixed = mixed_s[:, at]
            q_low, k_low, v_low = qn_ref[side, :, at], kn_ref[side, :, at], v_ref[side, :, at]
            parts = []
            for head in range(2):
                own = first if head == 0 else jnp.logical_not(first)
                probs = p_ref[side * heads + 2 * pair + head]
                prob_grad = dot_nt(jnp.where(own, v_low, jnp.zeros_like(v_low)), mixed)
                centred = jnp.sum(prob_grad * probs, axis=0, keepdims=True)
                score_grad = (probs * (prob_grad - centred)).astype(bf16)
                parts.append(
                    (dot_tn(score_grad, k_low), dot(score_grad, q_low), dot(probs.astype(bf16), mixed))
                )
            query_grad, key_grad, value_grad = [
                jnp.where(first, low, high).astype(bf16) for low, high in zip(*parts)
            ]
            scaled = mult[side : side + 1, at]
            query_unit = q_low.astype(f32) * (1.0 / scaled)
            key_unit = k_low.astype(f32)
            unit_grad = query_grad.astype(f32) * scaled
            key_grad = key_grad.astype(f32)
            cross = unit_grad * query_unit
            small[3:4, side * half + pair * LANES : side * half + (pair + 1) * LANES] = jnp.sum(
                cross, axis=0, keepdims=True
            )
            query_pre = rq_ref[side, :, at] * (unit_grad - query_unit * half_sums(cross, first))
            key_pre = rk_ref[side, :, at] * (
                key_grad - key_unit * half_sums(key_grad * key_unit, first)
            )
            put(side, pair * LANES, query_pre.astype(bf16))
            put(side, half + pair * LANES, key_pre.astype(bf16))
            put(side, 2 * half + pair * LANES, value_grad)
        for index in (3, 4) if side == 1 else (2, 5):
            leave(index)
    wait_all(leaving)


def input_back_kernel(mods, *refs):
    ins, outs, got, rest = split_refs(refs, [11, 2, 11])
    tokens_grad, mod_out = outs
    sum_s, in_sems = rest
    copies = start_copies(list(zip(ins, got)), in_sems)
    qkv_grad0, qkv1a, qkv1b, x_ref, middle_grad = got[:5]
    weights = got[5:]
    width = x_ref.shape[1]
    half, cut = width // 2, qkv1a.shape[1]
    wait_all(copies[:4])
    normed, spread = normalize(x_ref[...].astype(f32))
    wait_all(copies[4:])
    for at in tiles(width, 512):
        total = jnp.zeros((x_ref.shape[0], at.stop - at.start), f32)
        for part in range(3):
            total = total + dot_nt(
                qkv_grad0[:, part * half : (part + 1) * half], weights[part][at, :]
            )
        for start in range(0, 3 * half, half // 2):
            piece = (qkv1a, qkv1b)[start // cut][:, start % cut : start % cut + half // 2]
            inner = start % half
            total = total + dot_nt(piece, weights[3 + start // half][at, inner : inner + half // 2])
        sum_s[:, at] = total
    grad = sum_s[...]
    mod_out[0:1, :] = jnp.sum(grad * normed, axis=0, keepdims=True)
    mod_out[1:2, :] = jnp.sum(grad, axis=0, keepdims=True)
    tokens_grad[...] = (
        middle_grad[...] + norm_back(grad * (1.0 + mods[2:3, :]), normed, spread)
    ).astype(bf16)


def column_tiles(rights, flow):
    start = 0
    for source, (near, *pieces) in enumerate(rights):
        quarter, cut = near.shape[1] // 4, pieces[0].shape[1]
        for step in range(2):
            at = (2 * flow + step) * quarter
            to = start + step * quarter
            far = pieces[at // cut][:, at % cut : at % cut + quarter]
            both = jnp.concatenate([near[:, at : at + quarter], far], axis=0)
            yield source, both, slice(at, at + quarter), slice(to, to + quarter)
        start += 2 * quarter


def split_refs(refs, counts):
    out = []
    for count in counts:
        out.append(refs[:count])
        refs = refs[count:]
    return out + [refs]


def grad_kernel(pieces, bit_ref, *refs):
    sources = len(pieces)
    count = sum(pieces) + 3 * sources
    far, outs, got, held, rest = split_refs(refs, [count, 3 * sources + 2, count, sources + 2])
    *ins, _ = split_refs(got, [3 + count for count in pieces])
    picked, in_sems, out_sems = rest
    copies = start_copies(list(zip(far, got)), in_sems)
    waits = []
    for piece in pieces:
        waits.append(copies[: 3 + piece])
        copies = copies[3 + piece :]
    left_sums, right_sums = outs[:sources], outs[sources : 2 * sources]
    left_t, (sent_a, sent_b) = held[:sources], held[sources:]
    leaving = []

    def leave(index):
        copy = pltpu.make_async_copy(held[index], outs[2 * sources + index], out_sems.at[index])
        copy.start()
        leaving.append(copy)

    moved, part, columns = sent_a.shape
    tokens, half = ins[0][0].shape[0], ins[0][0].shape[1] // 2
    depth = 2 * tokens
    ones = jnp.ones((8, depth), bf16)
    for source in range(sources):
        wait_all(waits[source][:2])
        for side in range(2):
            cols = slice(side * half, (side + 1) * half)
            near, far = ins[source][0][:, cols], ins[source][1][:, cols]
            rows = slice(side * moved, (side + 1) * moved)
            left_sums[source][:, cols] = dot(ones, jnp.concatenate([near, far], axis=0))[0:1]
            left_t[source][rows, :, :tokens] = near.T.reshape(moved, part, tokens)
            left_t[source][rows, :, tokens:] = far.T.reshape(moved, part, tokens)
        leave(source)
    rights = [refs[2:] for refs in ins]
    for source in range(sources):
        wait_all(waits[source][2:])
    for flow, sent in enumerate((sent_a, sent_b)):
        away = 1 - bit_ref[flow]
        for source in range(sources):
            for row in range(moved):
                at = 2 * row + away if flow == 0 else (row // 2) * 4 + row % 2 + 2 * away
                picked[source, row] = left_t[source][at]
        for source, right, at, to in column_tiles(rights, flow):
            left = picked[source].reshape(moved * part, depth)
            sent[:, :, to] = dot(left, right).astype(bf16).reshape(moved, part, -1)
            right_sums[source][:, at] = dot(ones, right)[0:1]
        leave(sources + flow)
    wait_all(leaving)


def second_kernel(pieces, bit_ref, *refs):
    sources = len(pieces)
    count = 2 * sources + sum(pieces) + 2
    far, outs, got, held, rest = split_refs(refs, [count, 3, count, 3])
    left_t, *rights, (came_a, came_b) = split_refs(got, [sources] + [1 + count for count in pieces])
    sent_a, sent_b, own = held
    picked, in_sems, out_sems = rest
    copies = start_copies(list(zip(far, got)), in_sems)
    wait_all(copies[:-2])
    leaving = []
    moved, part, columns = sent_a.shape
    depth = left_t[0].shape[2]
    for flow, (came, sent) in enumerate(((came_a, sent_a), (came_b, sent_b))):
        copies[flow - 2].wait()
        mine, away = bit_ref[flow], 1 - bit_ref[1 - flow]
        for source in range(sources):
            for row in range(moved):
                if flow == 0:
                    base, other = 4 * row + mine, 2
                else:
                    base, other = 4 * row + 2 * mine, 1
                picked[source, row] = left_t[source][base + other * away]
                picked[source, moved + row] = left_t[source][base + other * (1 - away)]
        for source, right, at, to in column_tiles(rights, flow):
            left = picked[source].reshape(2 * moved * part, depth)
            block = dot(left, right).reshape(2 * moved, part, -1)
            kept = slice(flow * columns + to.start, flow * columns + to.stop)
            for row in range(moved):
                sent[row, :, to] = (block[row] + came[2 * row + away, :, to].astype(f32)).astype(
                    bf16
                )
                own[row, :, kept] = (
                    block[moved + row] + came[2 * row + 1 - away, :, to].astype(f32)
                ).astype(bf16)
        leaving += start_copies([(held[flow], outs[flow])], out_sems.at[pl.ds(flow, 1)])
    leaving += start_copies([(own, outs[2])], out_sems.at[pl.ds(2, 1)])
    wait_all(leaving)


def third_kernel(bit, bit_ref, own, *refs):
    came, (sent, kept) = refs[:-2], refs[-2:]
    mine = bit_ref[bit]
    start = 0
    for part in came:
        to = slice(start, start + part.shape[2])
        start += part.shape[2]
        for row in range(sent.shape[0]):
            away, near = 2 * row + 1 - mine, 2 * row + mine
            sent[row, :, to] = (own[away, :, to].astype(f32) + part[away].astype(f32)).astype(bf16)
            kept[row, :, to] = (own[near, :, to].astype(f32) + part[near].astype(f32)).astype(kept.dtype)


def local_call(kernel, limit, outs, scratch, kinds, *values, out_kind="v", flops=1):
    places = {
        "s": pl.BlockSpec(memory_space=pltpu.SMEM),
        "v": pl.BlockSpec(memory_space=pltpu.VMEM),
        "h": pl.BlockSpec(memory_space=pl.ANY),
    }
    return pl.pallas_call(
        kernel,
        out_shape=outs,
        in_specs=[places[kind] for kind in kinds],
        out_specs=[places[kind] for kind in (out_kind if len(out_kind) > 1 else out_kind * len(outs))],
        scratch_shapes=scratch,
        compiler_params=pltpu.CompilerParams(vmem_limit_bytes=limit * 2**20),
        cost_estimate=pl.CostEstimate(flops=flops, bytes_accessed=1, transcendentals=0),
    )(*values)


def normalize(values):
    mean = jnp.mean(values, axis=1, keepdims=True)
    spread = jnp.mean(values * values, axis=1, keepdims=True) - mean * mean
    scale = lax.rsqrt(spread + norm_eps)
    return (values - mean) * scale, scale


def norm_back(grad, normed, scale):
    return scale * (
        grad
        - jnp.mean(grad, axis=1, keepdims=True)
        - normed * jnp.mean(grad * normed, axis=1, keepdims=True)
    )


def gelu_parts(pre):
    square = pre * pre
    tanh = jnp.tanh(pre * (gelu_c + gelu_c * gelu_a * square))
    gate = 0.5 + 0.5 * tanh
    slope = gate + pre * (0.5 - 0.5 * tanh * tanh) * (gelu_c + 3.0 * gelu_c * gelu_a * square)
    return pre * gate, slope


def shards(
    tokens,
    class_ids,
    final_scale,
    row_slots,
    class_table,
    ada_weight,
    ada_bias,
    qkv_weight,
    qv_bias,
    log_scale,
    proj_weight,
    proj_bias,
    fc1_weight,
    fc1_bias,
    fc2_weight,
    fc2_bias,
    out_grad,
):
    groups = lax.axis_size("dp")
    bits = groups.bit_length() - 1
    here = lax.axis_index("dp")
    core = lax.axis_index("mp")
    micro, row_len, half = tokens.shape
    width = 2 * half
    share = row_len // groups
    heads = log_scale.shape[0]
    hidden = fc1_weight.shape[1]

    def swap(values):
        return lax.ppermute(values, "mp", [(0, 1), (1, 0)])

    def flip(values, bit):
        return lax.ppermute(values, "dp", [(i, i ^ (1 << bit)) for i in range(groups)])

    def in_order(own, other, axis):
        return jnp.where(
            core == 0,
            jnp.concatenate([own, other], axis),
            jnp.concatenate([other, own], axis),
        )

    class_picks = (
        class_ids.reshape(-1)[:, None] == jnp.arange(class_table.shape[0], dtype=jnp.int32)[None, :]
    )
    condition = dot(class_picks.astype(bf16), class_table)
    lifted = jax.nn.silu(condition).astype(bf16)
    ada_half = lax.dynamic_slice_in_dim(ada_weight, core * half, half, 2)
    ada_terms = dot(lifted, ada_half.reshape(ada_half.shape[0], 6 * half))
    ada_terms = ada_terms.reshape(micro, groups, 6, half)
    ada_round = lax.reduce_precision(ada_terms, 8, 7)
    ada_rest = jnp.stack([ada_terms[:, :, c] - ada_round[:, :, c] for c in (2, 4)], axis=2)
    ada_sent = jnp.concatenate([ada_round, ada_rest], axis=2).astype(bf16)

    def by_target(values):
        return values.reshape(micro, groups, -1, half).swapaxes(0, 1).reshape(2 * groups, -1, half)

    def exchange(values):
        return lax.all_to_all(values, ("dp", "mp"), split_axis=0, concat_axis=0, tiled=True)

    def to_row(values):
        return (
            values.reshape(groups, 2, share, half).transpose(0, 2, 1, 3).reshape(row_len, width)
        )

    first_message = jnp.concatenate([by_target(tokens), by_target(ada_sent)], axis=1)
    arrived = exchange(first_message)

    def after(values, *earlier):
        return lax.optimization_barrier((values, earlier))[0]

    small = jnp.concatenate(
        [ada_bias.reshape(-1), qv_bias.reshape(-1), log_scale, proj_bias, fc1_bias, fc2_bias]
    )
    small_sizes = [6 * half, 2 * half, heads, half, hidden, half]

    def unpack(flat):
        starts = [sum(small_sizes[:i]) for i in range(7)]
        return [flat[starts[i] : starts[i + 1]] for i in range(6)]

    own_small, oth_small = unpack(small), unpack(swap(small))
    qkv_w = [qkv_weight[:, part] for part in range(3)]
    qkv_w += [swap(weight) for weight in qkv_w]
    proj_w = (proj_weight, swap(proj_weight))
    fc1_w = (fc1_weight, swap(fc1_weight))
    fc2_w = (fc2_weight, swap(fc2_weight))
    ada_shift = in_order(own_small[0].reshape(6, half), oth_small[0].reshape(6, half), 1)
    proj_shift = in_order(own_small[3], oth_small[3], 0)
    fc2_shift = in_order(own_small[5], oth_small[5], 0)
    fc1_shift = jnp.stack([own_small[4], oth_small[4]])
    qkv_shift = jnp.stack(
        [
            jnp.concatenate([part[1][:half], jnp.zeros((half,), f32), part[1][half:]])
            for part in (own_small, oth_small)
        ]
    )
    head_mult = jnp.stack([jnp.repeat(jnp.exp(part[2]), HEAD_DIM) for part in (own_small, oth_small)])

    segments, levels = slot_layout(
        lax.dynamic_index_in_dim(final_scale[:, 0], core, 0, keepdims=False),
        lax.dynamic_index_in_dim(row_slots[:, 0], core, 0, keepdims=False),
    )
    mask = (
        (segments[:, None] == segments[None, :]) & (levels[:, None] <= levels[None, :])
    ).astype(f32)

    grads_arrived = exchange(
        after(by_target(out_grad), arrived, qkv_shift, head_mult, mask, proj_shift, fc1_shift, fc2_shift)
    )

    def array(*dims, kind=bf16):
        return jax.ShapeDtypeStruct(dims, kind)

    vmem, dma = pltpu.VMEM, pltpu.SemaphoreType.DMA

    def scratch(arrays):
        return [vmem(value.shape, value.dtype) for value in arrays]

    wide = array(2, row_len, half)
    wide32 = array(2, row_len, half, kind=f32)
    whole_tiles = share % 16 == 0
    if whole_tiles:
        row_in, ada_in = arrived, ada_shift
    else:
        row_in = to_row(arrived[:, :share])
        terms = jnp.sum(arrived[:, share:].reshape(groups, 2, 8, half).astype(f32), axis=0)
        terms = terms.transpose(1, 0, 2).reshape(8, width)
        ada_in = (ada_shift + terms[:6]).at[2].add(terms[6]).at[4].add(terms[7])
    kept = [
        array(row_len, width),
        wide,
        wide,
        wide,
        wide32,
        wide32,
        array(2 * heads, row_len, row_len, kind=f32),
        array(row_len, half),
        array(row_len, half),
        array(row_len, width, kind=f32),
        array(row_len, width, kind=f32),
        array(row_len, width),
        array(row_len, hidden),
        array(row_len, hidden // 2),
        array(row_len, hidden // 2),
        array(row_len, hidden),
        array(row_len, hidden),
    ]
    h1, qn, kn, vn, rq, rk, probs, mixed0, mixed1, attn, middle, h2, act0, *more = local_call(
        functools.partial(forward_kernel, share if whole_tiles else 0),
        56,
        kept + [array(row_len, width), array(6, width, kind=f32)],
        scratch(kept)
        + [
            vmem((2, 3, width, half), bf16),
            vmem((2, half, width), bf16),
            vmem((2, width, hidden), bf16),
            vmem((row_len, 3 * half), f32),
            dma((10,)),
            dma((23,)),
        ],
        "vvvvvvv" + "h" * 10,
        row_in,
        ada_in,
        qkv_shift,
        head_mult,
        mask,
        proj_shift[None],
        fc1_shift,
        *qkv_w,
        *proj_w,
        *fc1_w,
        out_kind="h" * len(kept) + "vv",
    )
    act1, (slope0, slope1, resident, mods) = more[:2], more[2:]

    own_bits = jnp.stack([(here >> bit) & 1 for bit in range(bits)])
    part = width // groups

    def source(near_left, far_left, near_right, sent_right):
        return (near_left, far_left, near_right, *[swap(values) for values in sent_right])

    def scatter_start(*sources):
        count = len(sources)
        pieces = [len(source) - 3 for source in sources]
        columns = sum(source[2].shape[1] for source in sources) // 2
        ins = [value for source in sources for value in source]
        kept = [array(groups, part, 2 * row_len)] * count + [
            array(groups // 2, part, columns)
        ] * 2
        outs = local_call(
            functools.partial(grad_kernel, pieces),
            56,
            [array(1, width, kind=f32)] * count
            + [array(1, source[2].shape[1], kind=f32) for source in sources]
            + kept,
            scratch(ins)
            + scratch(kept)
            + [
                vmem((count, groups // 2, part, 2 * row_len), bf16),
                dma((len(ins),)),
                dma((len(kept),)),
            ],
            "s" + "h" * len(ins),
            own_bits,
            *ins,
            out_kind="v" * (2 * count) + "h" * len(kept),
        )
        left_sums, right_sums = outs[:count], outs[count : 2 * count]
        rest = list(outs[2 * count : 3 * count])
        rest += [value for source in sources for value in source[2:]]
        return left_sums, right_sums, (pieces, rest), tuple(outs[3 * count :])

    def travel(sent):
        return flip(sent[0], 0), flip(sent[1], 1)

    def scatter_second(started, came, flops=1):
        pieces, rest = started
        count = len(pieces)
        columns = came[0].shape[2]
        ins = [*rest, *came]
        kept = [array(groups // 4, part, columns)] * 2 + [array(groups // 4, part, 2 * columns)]
        sent_a, sent_b, own = local_call(
            functools.partial(second_kernel, pieces),
            56,
            kept,
            scratch(ins)
            + scratch(kept)
            + [
                vmem((count, groups // 2, part, 2 * row_len), bf16),
                dma((len(ins),)),
                dma((3,)),
            ],
            "s" + "h" * len(ins),
            own_bits,
            *ins,
            out_kind="h",
            flops=flops,
        )
        return own, (sent_a, sent_b)

    def scatter_more(bit, own, came):
        rows, _, columns = own.shape
        sent, own = local_call(
            functools.partial(third_kernel, bit),
            56,
            [
                array(rows // 2, part, columns),
                array(rows // 2, part, columns, kind=f32 if bit == bits - 1 else bf16),
            ],
            [],
            "sv" + "v" * len(came),
            own_bits,
            own,
            *came,
        )
        return own, sent

    def scatter_end(begin, own, came):
        for bit in range(begin, bits):
            own, sent = scatter_more(bit, own, came)
            came = (flip(sent, bit),)
        return own[0] + came[0][0].astype(f32)

    grad_out = to_row(after(grads_arrived, act0))
    grad_branch = (mods[1:2] * grad_out.astype(f32)).astype(bf16)
    fc2_left, _, fc2_rest, fc2_sent = scatter_start(
        source(grad_branch, swap(grad_branch), act0, act1)
    )
    h1_far, h2_far, mixed_far = swap(h1), swap(h2), swap(mixed1)
    fc2_came = travel(fc2_sent)

    pre_kept = [array(row_len, hidden)] + [array(row_len, hidden // 2)] * 2
    branch_ins = [act0, *act1, grad_out, middle]
    pre0, *pre1, output, branch_mods = local_call(
        hidden_back_kernel,
        56,
        pre_kept + [array(row_len, width), array(1, width, kind=f32)],
        scratch(pre_kept)
        + [vmem((2, row_len, hidden), bf16), vmem((2, hidden, width), bf16)]
        + scratch(branch_ins)
        + [dma((13,)), dma((3,))],
        "vvv" + "h" * 9,
        after(grad_branch, fc2_sent, h1_far, h2_far, mixed_far),
        mods,
        fc2_shift[None],
        slope0,
        slope1,
        *fc2_w,
        *branch_ins,
        out_kind="hhhvv",
    )
    _, fc1_right, fc1_rest, fc1_sent = scatter_start(
        source(h2, h2_far, pre0, pre1)
    )
    fc1_came = travel(fc1_sent)
    def to_target(values):
        return (
            values.reshape(groups, share, 2, half).transpose(0, 2, 1, 3).reshape(-1, share, half)
        )

    fc2_own, fc2_sent = scatter_second(fc2_rest, after(fc2_came, fc1_sent), int(3e9))
    fc2_came = travel(fc2_sent[::-1])[::-1]
    row_ins = [
        after(pre0, fc2_sent),
        fc1_w[0],
        *pre1,
        fc1_w[1],
        middle,
        grad_out,
        attn,
        *proj_w,
        qn,
        kn,
        vn,
        probs,
        rq,
        rk,
    ]
    row_kept = [
        array(row_len, width, kind=f32),
        array(row_len, width),
        array(row_len, 3 * half),
        array(row_len, 3 * half // 2),
        array(row_len, 3 * half // 2),
        array(4, width, kind=f32),
    ]
    middle_grad, attn_grad, qkv_grad0, qkv1a, qkv1b, row_mods = local_call(
        row_back_kernel,
        56,
        row_kept,
        scratch(row_kept)
        + scratch(row_ins)
        + [vmem((row_len, width), f32), vmem((row_len, half), bf16), dma((16,)), dma((6,))],
        "vv" + "h" * 16,
        mods,
        head_mult,
        *row_ins,
        out_kind="h",
    )
    fc1_own, fc1_sent = scatter_second(fc1_rest, after(fc1_came, attn_grad))
    ready = after((qkv1a, qkv1b, attn_grad), fc2_came, fc1_sent)
    fc1_came = travel(fc1_sent[::-1])[::-1]
    fc2_own, fc2_sent = scatter_more(2, fc2_own, fc2_came)
    fc2_came = (flip(fc2_sent, 2),)
    qkv_left, qkv_right, qkv_rest, qkv_sent = scatter_start(
        after(source(h1, h1_far, qkv_grad0, ready[:2]), fc2_sent),
        (attn_grad, swap(ready[2]), mixed0, mixed_far),
    )
    qkv_came = travel(qkv_sent)
    fc2_own, fc2_sent = scatter_more(3, fc2_own, after(fc2_came, qkv_sent))
    fc2_came = (flip(fc2_sent, 3),)
    end_ins = [
        after(qkv_grad0, fc1_came, fc2_sent),
        qkv1a,
        qkv1b,
        resident,
        middle_grad,
        *qkv_w,
    ]
    tokens_grad, end_mods = local_call(
        input_back_kernel,
        56,
        [array(row_len, width), array(2, width, kind=f32)],
        scratch(end_ins) + [vmem((row_len, width), f32), dma((11,))],
        "v" + "h" * 11,
        mods,
        *end_ins,
        flops=int(2e9),
    )

    row_grads = jnp.stack(
        [row_mods[2], branch_mods[0], end_mods[0], row_mods[0], end_mods[1], row_mods[1]]
    ).astype(bf16)
    scale_terms = jnp.sum(row_mods[3].reshape(2, heads, HEAD_DIM), axis=2)
    scale_sum = scale_terms[0] + swap(scale_terms[1])

    def own_half(values):
        return lax.dynamic_slice_in_dim(values, core * half, half, 0)

    bias_sum = jnp.concatenate(
        [
            qkv_right[0][0, :half],
            qkv_right[0][0, 2 * half :],
            own_half(qkv_left[1][0]),
            fc1_right[0][0],
            own_half(fc2_left[0][0]),
            scale_sum,
        ]
    )

    def double(gathered, bias_sum, bit):
        rounded = bias_sum.astype(bf16)
        count = gathered.size
        came = flip(jnp.concatenate([gathered.reshape(-1), rounded]), bit)
        theirs = came[:count].reshape(gathered.shape)
        mine = (here >> bit) & 1
        both = jnp.where(mine == 0, jnp.stack([gathered, theirs]), jnp.stack([theirs, gathered]))
        return both, rounded.astype(f32) + came[count:].astype(f32)

    returned = exchange(
        jnp.concatenate([to_target(values) for values in (output, tokens_grad)], axis=1)
    )
    qkv_own, qkv_sent = scatter_second(qkv_rest, after(qkv_came, fc1_came, fc2_came, tokens_grad))
    qkv_came = travel(qkv_sent[::-1])[::-1]
    fc1_own, fc1_sent = scatter_more(2, fc1_own, after(fc1_came, qkv_sent))
    fc1_came = (flip(fc1_sent, 2),)
    gathered = after(row_grads, qkv_sent).reshape(6 * width)
    for bit in (2, 0):
        gathered, bias_sum = double(gathered, bias_sum, bit)
    qkv_own, qkv_sent = scatter_more(2, qkv_own, after(qkv_came, fc1_came, gathered, returned))
    qkv_came = (flip(qkv_sent, 2),)
    fc1_own, fc1_sent = scatter_more(3, fc1_own, after(fc1_came, qkv_sent))
    fc1_came = (flip(fc1_sent, 3),)
    gathered = after(gathered, fc1_sent)
    for bit in [1] + list(range(3, bits)):
        gathered, bias_sum = double(gathered, bias_sum, bit)
    order = list(range(bits - 1, 2, -1)) + [1, 0, 2]
    gathered = gathered.transpose(
        *[order.index(bit) for bit in range(bits - 1, -1, -1)], bits
    ).reshape(groups, 6 * width)
    qkv_own, qkv_sent = scatter_more(3, qkv_own, after(qkv_came, fc1_came, gathered))
    qkv_came = (flip(qkv_sent, 3),)
    gathered = after(gathered, qkv_sent)
    gathered = in_order(gathered, swap(gathered), 0)
    fc2_sum = scatter_end(4, fc2_own, fc2_came)
    fc1_sum = scatter_end(4, fc1_own, fc1_came)
    qkv_sum = scatter_end(4, qkv_own, qkv_came)

    ada_weight_grad = dot_tn(lifted, gathered).reshape(ada_weight.shape)
    ada_bias_grad = jnp.sum(gathered.astype(f32), axis=0).reshape(6, width)
    grad_lifted = dot_nt(gathered, ada_weight.reshape(ada_weight.shape[0], 6 * width))
    _, silu_pull = jax.vjp(jax.nn.silu, condition)
    table_grad = lax.dot_general(
        class_picks.astype(f32),
        silu_pull(grad_lifted)[0],
        (((0,), (0,)), ((), ())),
        precision=lax.Precision.HIGHEST,
    )

    def from_rows(values):
        return values.reshape(groups, 2, share, half).swapaxes(0, 1).reshape(2, row_len, half)

    qkv_cols, proj_cols = 3 * half // 2, half // 2
    turn = qkv_cols + proj_cols
    qkv_own_sum = jnp.concatenate([qkv_sum[:, :qkv_cols], qkv_sum[:, turn : turn + qkv_cols]], 1)
    proj_sum = jnp.concatenate([qkv_sum[:, qkv_cols:turn], qkv_sum[:, turn + qkv_cols :]], 1)
    ends = [half, 2 * half, 3 * half, 3 * half + hidden, 4 * half + hidden]
    return (
        from_rows(returned[:, :share]),
        from_rows(returned[:, share:]),
        table_grad,
        ada_weight_grad,
        ada_bias_grad,
        qkv_own_sum.reshape(-1, 3, half),
        bias_sum[: ends[1]].reshape(2, half),
        bias_sum[ends[4] :],
        proj_sum.T,
        bias_sum[ends[1] : ends[2]],
        fc1_sum,
        bias_sum[ends[2] : ends[3]],
        fc2_sum.T,
        bias_sum[ends[3] : ends[4]],
    )


def solution(mesh):
    placed = (
        P(None, "dp", "mp"),
        P(),
        P(None, "dp", None),
        P(None, "dp", None),
        P(None, "dp"),
        P("dp", None, None),
        P(None, "mp"),
        P(None, None, "mp"),
        P(None, "mp"),
        P("mp"),
        P("mp", None),
        P("mp"),
        P(None, "mp"),
        P("mp"),
        P("mp", None),
        P("mp"),
        P(None, "dp", "mp"),
    )
    return jax.shard_map(
        shards,
        mesh=mesh,
        in_specs=placed,
        out_specs=(
            P(None, "dp", "mp"),
            P(None, "dp", "mp"),
            P(None, "dp"),
            P("dp", None, None),
            P(),
            P("dp", None, "mp"),
            P(None, "mp"),
            P("mp"),
            P("mp", "dp"),
            P("mp"),
            P("dp", "mp"),
            P("mp"),
            P("mp", "dp"),
            P("mp"),
        ),
        check_vma=False,
    )
```

```python
import functools

import jax
import jax.numpy as jnp
from jax import lax
from jax.experimental import pallas as pl
from jax.experimental.pallas import tpu as pltpu
from jax.sharding import PartitionSpec as P

HEAD_DIM = 64
LANES = 128
scale_ends = (1, 5, 14, 30, 55, 91, 155, 255, 424, 680)
norm_eps = 1e-06
unit_eps = 1e-06
bf16 = jnp.bfloat16
f32 = jnp.float32
gelu_c = 0.7978845608028654
gelu_a = 0.044715


def slot_layout(final_row, slots_row):
    ends_table = jnp.asarray(scale_ends, dtype=jnp.int32)
    chosen = final_row[:, None] == jnp.arange(len(scale_ends), dtype=jnp.int32)[None, :]
    lengths = jnp.sum(jnp.where(chosen, ends_table[None, :], 0), axis=1)
    items = final_row.shape[0]
    before = jnp.arange(items)[:, None] <= jnp.arange(items)[None, :]
    item_ends = jnp.sum(jnp.where(before, lengths[:, None], 0), axis=0)
    passed = slots_row[:, None] >= item_ends[None, :]
    segment = jnp.sum(passed.astype(jnp.int32), axis=1)
    item_start = jnp.sum(jnp.where(passed, lengths[None, :], 0), axis=1)
    offset = slots_row - item_start
    level = jnp.sum((offset[:, None] >= ends_table[None, :]).astype(jnp.int32), axis=1)
    return segment, jnp.where(segment == items, 0, level)


def dot(a, b):
    return jnp.dot(a, b, preferred_element_type=f32)


def dot_nt(a, b):
    return lax.dot_general(a, b, (((1,), (1,)), ((), ())), preferred_element_type=f32)


def dot_tn(a, b):
    return lax.dot_general(a, b, (((0,), (0,)), ((), ())), preferred_element_type=f32)


def half_sums(values, first):
    low = jnp.sum(jnp.where(first, values, 0.0), axis=1, keepdims=True)
    high = jnp.sum(jnp.where(first, 0.0, values), axis=1, keepdims=True)
    return jnp.where(first, low, high)


def head_parts(queries, keys, mult, first):
    query_scale = lax.rsqrt(half_sums(queries * queries, first) + unit_eps)
    key_scale = lax.rsqrt(half_sums(keys * keys, first) + unit_eps)
    return queries * query_scale * mult, keys * key_scale, query_scale, key_scale


def start_copies(pairs, sems):
    copies = [pltpu.make_async_copy(src, dst, sems.at[i]) for i, (src, dst) in enumerate(pairs)]
    for copy in copies:
        copy.start()
    return copies


def wait_all(copies):
    for copy in copies:
        copy.wait()


def tiles(size, most):
    tile = min(most, size)
    return [slice(start, start + tile) for start in range(0, size, tile)]


def forward_kernel(
    share, arrived, ada_ref, qkv_bias, mult, mask_ref, proj_bias, fc1_bias, *refs
):
    weights, outs, (x_ref, mods), held, rest = split_refs(refs, [10, 17, 2, 17])
    qkv_w, proj_w, fc1_w, qkv_s, in_sems, out_sems = rest
    copies = start_copies(
        [(weights[i], qkv_w.at[i // 3, i % 3]) for i in range(6)]
        + [(weights[6 + i], proj_w.at[i]) for i in range(2)]
        + [(weights[8 + i], fc1_w.at[i]) for i in range(2)],
        in_sems,
    )
    leaving = []

    def leave(index, *at):
        src, dst = held[index], outs[index]
        if at:
            src, dst = src.at[at], dst.at[at]
        copy = pltpu.make_async_copy(src, dst, out_sems.at[len(leaving)])
        copy.start()
        leaving.append(copy)

    h1, qn_out, kn_out, v_out, rq_out, rk_out, p_out, mixed0, mixed1, attn_out = held[:10]
    middle_out, h2_out, act0, act1a, act1b, slope0, slope1 = held[10:]
    rows, width = x_ref.shape
    half = width // 2
    if share:
        for side in range(2):
            cols = slice(side * half, (side + 1) * half)
            terms = jnp.zeros((8, half), f32)
            for group in range(rows // share):
                block = arrived.at[2 * group + side]
                x_ref[group * share : (group + 1) * share, cols] = block[:share, :]
                terms = terms + block[share : share + 8, :].astype(f32)
            mods[:, cols] = ada_ref[:, cols] + terms[:6]
            mods[2:3, cols] = mods[2:3, cols] + terms[6:7]
            mods[4:5, cols] = mods[4:5, cols] + terms[7:8]
    else:
        x_ref[...] = arrived[...]
        mods[...] = ada_ref[...]
    x = x_ref[...].astype(f32)
    h1[...] = (normalize(x)[0] * (1.0 + mods[2:3, :]) + mods[4:5, :]).astype(bf16)
    leave(0)
    first = lax.broadcasted_iota(jnp.int32, (rows, LANES), 1) < HEAD_DIM
    mask = mask_ref[...]
    heads = half // HEAD_DIM
    for side, mixed_out in enumerate((mixed0, mixed1)):
        for part in range(3):
            copies[3 * side + part].wait()
            at = slice(part * half, (part + 1) * half)
            qkv_s[:, at] = dot(h1[...], qkv_w[side, part]) + qkv_bias[side : side + 1, at]
        for pair in range(half // LANES):
            at = slice(pair * LANES, (pair + 1) * LANES)
            qn, kn, query_scale, key_scale = head_parts(
                qkv_s[:, at],
                qkv_s[:, half + pair * LANES : half + (pair + 1) * LANES],
                mult[side : side + 1, at],
                first,
            )
            q_low, k_low = qn.astype(bf16), kn.astype(bf16)
            v_low = qkv_s[:, 2 * half + pair * LANES : 2 * half + (pair + 1) * LANES].astype(bf16)
            qn_out[side, :, at] = q_low
            kn_out[side, :, at] = k_low
            v_out[side, :, at] = v_low
            rq_out[side, :, at] = query_scale
            rk_out[side, :, at] = key_scale
            mixed = []
            for head in range(2):
                own = first if head == 0 else jnp.logical_not(first)
                scores = dot_nt(jnp.where(own, k_low, jnp.zeros_like(k_low)), q_low)
                raised = jnp.exp(scores) * mask
                weight = raised * (1.0 / jnp.sum(raised, axis=0, keepdims=True))
                p_out[side * heads + 2 * pair + head] = weight
                mixed.append(dot_tn(weight.astype(bf16), v_low))
            mixed_out[:, at] = jnp.where(first, mixed[0], mixed[1]).astype(bf16)
        leave(7 + side)
        for index in range(1, 6):
            leave(index, side)
        leave(6, pl.ds(side * heads, heads))
    copies[6].wait()
    copies[7].wait()
    attn_out[...] = dot(mixed0[...], proj_w[0]) + dot(mixed1[...], proj_w[1]) + proj_bias[...]
    leave(9)
    middle = x + mods[0:1, :] * attn_out[...]
    middle_out[...] = middle
    leave(10)
    h2_out[...] = (normalize(middle)[0] * (1.0 + mods[3:4, :]) + mods[5:6, :]).astype(bf16)
    leave(11)

    def expand(side, act, slope, first_col):
        for to in tiles(act.shape[1], 512):
            at = slice(first_col + to.start, first_col + to.stop)
            pre = dot(h2_out[...], fc1_w[side, :, at]) + fc1_bias[side : side + 1, at]
            value, rise = gelu_parts(pre)
            act[:, to] = value.astype(bf16)
            slope[:, at] = rise.astype(bf16)

    copies[9].wait()
    expand(1, act1a, slope1, 0)
    leave(13)
    expand(1, act1b, slope1, act1a.shape[1])
    leave(14)
    leave(16)
    copies[8].wait()
    expand(0, act0, slope0, 0)
    leave(12)
    leave(15)
    wait_all(leaving)


def hidden_back_kernel(grad_ref, mods, fc2_bias, *refs):
    ins, outs, held, rest = split_refs(refs, [9, 5, 3])
    slope_s, fc2_w, act0, act1a, act1b, grad_out_ref, middle_ref, in_sems, out_sems = rest
    slope0, slope1, fc2_0, fc2_1 = ins[:4]
    pre0, pre1a, pre1b = held
    output, mod_out = outs[3:]
    cut = pre1a.shape[1]
    pairs = []
    for side in (1, 0):
        fc2, slope = (fc2_0, slope0) if side == 0 else (fc2_1, slope1)
        for at in (slice(0, cut), slice(cut, 2 * cut)):
            pairs.append((fc2.at[at, :], fc2_w.at[side, at, :]))
            pairs.append((slope.at[:, at], slope_s.at[side, :, at]))
    pairs += list(zip(ins[4:], (act0, act1a, act1b, grad_out_ref, middle_ref)))
    copies = start_copies(pairs, in_sems)
    leaving = []
    for side, pre, at, first_col in (
        (1, pre1a, slice(0, cut), 0),
        (1, pre1b, slice(cut, 2 * cut), 0),
        (0, pre0, slice(0, cut), 0),
        (0, pre0, slice(cut, 2 * cut), cut),
    ):
        step = 2 * (1 - side) + at.start // cut
        copies[2 * step].wait()
        copies[2 * step + 1].wait()
        for to in tiles(cut, 512):
            cols = slice(at.start + to.start, at.start + to.stop)
            grad = dot_nt(grad_ref[...], fc2_w[side, cols, :])
            pre[:, first_col + to.start : first_col + to.stop] = (
                grad * slope_s[side, :, cols].astype(f32)
            ).astype(bf16)
        if step < 2 or step == 3:
            index = {0: 1, 1: 2, 3: 0}[step]
            leaving += start_copies([(held[index], outs[index])], out_sems.at[pl.ds(index, 1)])
    wait_all(copies[8:])
    for at in tiles(middle_ref.shape[1], 512):
        value = (
            dot(act0[...], fc2_w[0, :, at])
            + dot(act1a[...], fc2_w[1, :cut, at])
            + dot(act1b[...], fc2_w[1, cut:, at])
            + fc2_bias[:, at]
        )
        output[:, at] = (middle_ref[:, at] + mods[1:2, at] * value).astype(bf16)
        mod_out[0:1, at] = jnp.sum(grad_out_ref[:, at].astype(f32) * value, axis=0, keepdims=True)
    wait_all(leaving)


def row_back_kernel(mods, mult, *refs):
    ins, outs, held, got, rest = split_refs(refs, [16, 6, 6, 16])
    h2_s, mixed_s, in_sems, out_sems = rest
    copies = start_copies(list(zip(ins, got)), in_sems)
    leaving = []

    def leave(index):
        copy = pltpu.make_async_copy(held[index], outs[index], out_sems.at[index])
        copy.start()
        leaving.append(copy)

    pre0, fc1_0, pre1a, pre1b, fc1_1, middle_ref, grad_out_ref, attn_ref = got[:8]
    proj_0, proj_1, qn_ref, kn_ref, v_ref, p_ref, rq_ref, rk_ref = got[8:]
    middle_grad, attn_grad, qkv_grad0, qkv1a, qkv1b, small = held
    rows, width = middle_ref.shape
    half = width // 2
    heads = half // HEAD_DIM
    copies[0].wait()
    copies[1].wait()
    for at in tiles(width, 512):
        h2_s[:, at] = dot_nt(pre0[...], fc1_0[at, :])
    wait_all(copies[2:5])
    for at in tiles(width, 512):
        total = h2_s[:, at]
        for index, pre in enumerate((pre1a, pre1b)):
            cut = pre.shape[1]
            total = total + dot_nt(pre[...], fc1_1[at, index * cut : (index + 1) * cut])
        h2_s[:, at] = total
    wait_all(copies[5:8])
    normed, spread = normalize(middle_ref[...])
    grad = h2_s[...]
    small[0:1, :] = jnp.sum(grad * normed, axis=0, keepdims=True)
    small[1:2, :] = jnp.sum(grad, axis=0, keepdims=True)
    total = grad_out_ref[...].astype(f32) + norm_back(
        grad * (1.0 + mods[3:4, :]), normed, spread
    )
    middle_grad[...] = total
    leave(0)
    small[2:3, :] = jnp.sum(total * attn_ref[...], axis=0, keepdims=True)
    attn_grad[...] = (mods[0:1, :] * total).astype(bf16)
    leave(1)
    first = lax.broadcasted_iota(jnp.int32, (rows, LANES), 1) < HEAD_DIM
    cut = qkv1a.shape[1]

    def put(side, start, values):
        if side == 0:
            qkv_grad0[:, start : start + LANES] = values
        else:
            index, to = start // cut, start % cut
            (qkv1a, qkv1b)[index][:, to : to + LANES] = values

    wait_all(copies[8:])
    for side in (1, 0):
        mixed_s[...] = dot_nt(attn_grad[...], (proj_0, proj_1)[side][...]).astype(bf16)
        for pair in range(half // LANES):
            at = slice(pair * LANES, (pair + 1) * LANES)
            mixed = mixed_s[:, at]
            q_low, k_low, v_low = qn_ref[side, :, at], kn_ref[side, :, at], v_ref[side, :, at]
            parts = []
            for head in range(2):
                own = first if head == 0 else jnp.logical_not(first)
                probs = p_ref[side * heads + 2 * pair + head]
                prob_grad = dot_nt(jnp.where(own, v_low, jnp.zeros_like(v_low)), mixed)
                centred = jnp.sum(prob_grad * probs, axis=0, keepdims=True)
                score_grad = (probs * (prob_grad - centred)).astype(bf16)
                parts.append(
                    (dot_tn(score_grad, k_low), dot(score_grad, q_low), dot(probs.astype(bf16), mixed))
                )
            query_grad, key_grad, value_grad = [
                jnp.where(first, low, high).astype(bf16) for low, high in zip(*parts)
            ]
            scaled = mult[side : side + 1, at]
            query_unit = q_low.astype(f32) * (1.0 / scaled)
            key_unit = k_low.astype(f32)
            unit_grad = query_grad.astype(f32) * scaled
            key_grad = key_grad.astype(f32)
            cross = unit_grad * query_unit
            small[3:4, side * half + pair * LANES : side * half + (pair + 1) * LANES] = jnp.sum(
                cross, axis=0, keepdims=True
            )
            query_pre = rq_ref[side, :, at] * (unit_grad - query_unit * half_sums(cross, first))
            key_pre = rk_ref[side, :, at] * (
                key_grad - key_unit * half_sums(key_grad * key_unit, first)
            )
            put(side, pair * LANES, query_pre.astype(bf16))
            put(side, half + pair * LANES, key_pre.astype(bf16))
            put(side, 2 * half + pair * LANES, value_grad)
        for index in (3, 4) if side == 1 else (2, 5):
            leave(index)
    wait_all(leaving)


def input_back_kernel(mods, *refs):
    ins, outs, got, rest = split_refs(refs, [11, 2, 11])
    tokens_grad, mod_out = outs
    sum_s, in_sems = rest
    copies = start_copies(list(zip(ins, got)), in_sems)
    qkv_grad0, qkv1a, qkv1b, x_ref, middle_grad = got[:5]
    weights = got[5:]
    width = x_ref.shape[1]
    half, cut = width // 2, qkv1a.shape[1]
    wait_all(copies[:4])
    normed, spread = normalize(x_ref[...].astype(f32))
    wait_all(copies[4:])
    for at in tiles(width, 512):
        total = jnp.zeros((x_ref.shape[0], at.stop - at.start), f32)
        for part in range(3):
            total = total + dot_nt(
                qkv_grad0[:, part * half : (part + 1) * half], weights[part][at, :]
            )
        for start in range(0, 3 * half, half // 2):
            piece = (qkv1a, qkv1b)[start // cut][:, start % cut : start % cut + half // 2]
            inner = start % half
            total = total + dot_nt(piece, weights[3 + start // half][at, inner : inner + half // 2])
        sum_s[:, at] = total
    grad = sum_s[...]
    mod_out[0:1, :] = jnp.sum(grad * normed, axis=0, keepdims=True)
    mod_out[1:2, :] = jnp.sum(grad, axis=0, keepdims=True)
    tokens_grad[...] = (
        middle_grad[...] + norm_back(grad * (1.0 + mods[2:3, :]), normed, spread)
    ).astype(bf16)


def column_tiles(rights, flow):
    start = 0
    for source, (near, *pieces) in enumerate(rights):
        quarter, cut = near.shape[1] // 4, pieces[0].shape[1]
        for step in range(2):
            at = (2 * flow + step) * quarter
            to = start + step * quarter
            far = pieces[at // cut][:, at % cut : at % cut + quarter]
            both = jnp.concatenate([near[:, at : at + quarter], far], axis=0)
            yield source, both, slice(at, at + quarter), slice(to, to + quarter)
        start += 2 * quarter


def split_refs(refs, counts):
    out = []
    for count in counts:
        out.append(refs[:count])
        refs = refs[count:]
    return out + [refs]


def grad_kernel(pieces, bit_ref, *refs):
    sources = len(pieces)
    count = sum(pieces) + 3 * sources
    far, outs, got, held, rest = split_refs(refs, [count, 3 * sources + 2, count, sources + 2])
    *ins, _ = split_refs(got, [3 + count for count in pieces])
    picked, in_sems, out_sems = rest
    copies = start_copies(list(zip(far, got)), in_sems)
    waits = []
    for piece in pieces:
        waits.append(copies[: 3 + piece])
        copies = copies[3 + piece :]
    left_sums, right_sums = outs[:sources], outs[sources : 2 * sources]
    left_t, (sent_a, sent_b) = held[:sources], held[sources:]
    leaving = []

    def leave(index):
        copy = pltpu.make_async_copy(held[index], outs[2 * sources + index], out_sems.at[index])
        copy.start()
        leaving.append(copy)

    moved, part, columns = sent_a.shape
    tokens, half = ins[0][0].shape[0], ins[0][0].shape[1] // 2
    depth = 2 * tokens
    ones = jnp.ones((8, depth), bf16)
    for source in range(sources):
        wait_all(waits[source][:2])
        for side in range(2):
            cols = slice(side * half, (side + 1) * half)
            near, far = ins[source][0][:, cols], ins[source][1][:, cols]
            rows = slice(side * moved, (side + 1) * moved)
            left_sums[source][:, cols] = dot(ones, jnp.concatenate([near, far], axis=0))[0:1]
            left_t[source][rows, :, :tokens] = near.T.reshape(moved, part, tokens)
            left_t[source][rows, :, tokens:] = far.T.reshape(moved, part, tokens)
        leave(source)
    rights = [refs[2:] for refs in ins]
    for source in range(sources):
        wait_all(waits[source][2:])
    for flow, sent in enumerate((sent_a, sent_b)):
        away = 1 - bit_ref[flow]
        for source in range(sources):
            for row in range(moved):
                at = 2 * row + away if flow == 0 else (row // 2) * 4 + row % 2 + 2 * away
                picked[source, row] = left_t[source][at]
        for source, right, at, to in column_tiles(rights, flow):
            left = picked[source].reshape(moved * part, depth)
            sent[:, :, to] = dot(left, right).astype(bf16).reshape(moved, part, -1)
            right_sums[source][:, at] = dot(ones, right)[0:1]
        leave(sources + flow)
    wait_all(leaving)


def second_kernel(pieces, bit_ref, *refs):
    sources = len(pieces)
    count = 2 * sources + sum(pieces) + 2
    far, outs, got, held, rest = split_refs(refs, [count, 3, count, 3])
    left_t, *rights, (came_a, came_b) = split_refs(got, [sources] + [1 + count for count in pieces])
    sent_a, sent_b, own = held
    picked, in_sems, out_sems = rest
    copies = start_copies(list(zip(far, got)), in_sems)
    wait_all(copies[:-2])
    leaving = []
    moved, part, columns = sent_a.shape
    depth = left_t[0].shape[2]
    for flow, (came, sent) in enumerate(((came_a, sent_a), (came_b, sent_b))):
        copies[flow - 2].wait()
        mine, away = bit_ref[flow], 1 - bit_ref[1 - flow]
        for source in range(sources):
            for row in range(moved):
                if flow == 0:
                    base, other = 4 * row + mine, 2
                else:
                    base, other = 4 * row + 2 * mine, 1
                picked[source, row] = left_t[source][base + other * away]
                picked[source, moved + row] = left_t[source][base + other * (1 - away)]
        for source, right, at, to in column_tiles(rights, flow):
            left = picked[source].reshape(2 * moved * part, depth)
            block = dot(left, right).reshape(2 * moved, part, -1)
            kept = slice(flow * columns + to.start, flow * columns + to.stop)
            for row in range(moved):
                sent[row, :, to] = (block[row] + came[2 * row + away, :, to].astype(f32)).astype(
                    bf16
                )
                own[row, :, kept] = (
                    block[moved + row] + came[2 * row + 1 - away, :, to].astype(f32)
                ).astype(bf16)
        leaving += start_copies([(held[flow], outs[flow])], out_sems.at[pl.ds(flow, 1)])
    leaving += start_copies([(own, outs[2])], out_sems.at[pl.ds(2, 1)])
    wait_all(leaving)


def third_kernel(bit, bit_ref, own, *refs):
    came, (sent, kept) = refs[:-2], refs[-2:]
    mine = bit_ref[bit]
    start = 0
    for part in came:
        to = slice(start, start + part.shape[2])
        start += part.shape[2]
        for row in range(sent.shape[0]):
            away, near = 2 * row + 1 - mine, 2 * row + mine
            sent[row, :, to] = (own[away, :, to].astype(f32) + part[away].astype(f32)).astype(bf16)
            kept[row, :, to] = (own[near, :, to].astype(f32) + part[near].astype(f32)).astype(kept.dtype)


def local_call(kernel, limit, outs, scratch, kinds, *values, out_kind="v", flops=1):
    places = {
        "s": pl.BlockSpec(memory_space=pltpu.SMEM),
        "v": pl.BlockSpec(memory_space=pltpu.VMEM),
        "h": pl.BlockSpec(memory_space=pl.ANY),
    }
    return pl.pallas_call(
        kernel,
        out_shape=outs,
        in_specs=[places[kind] for kind in kinds],
        out_specs=[places[kind] for kind in (out_kind if len(out_kind) > 1 else out_kind * len(outs))],
        scratch_shapes=scratch,
        compiler_params=pltpu.CompilerParams(vmem_limit_bytes=limit * 2**20),
        cost_estimate=pl.CostEstimate(flops=flops, bytes_accessed=1, transcendentals=0),
    )(*values)


def normalize(values):
    mean = jnp.mean(values, axis=1, keepdims=True)
    spread = jnp.mean(values * values, axis=1, keepdims=True) - mean * mean
    scale = lax.rsqrt(spread + norm_eps)
    return (values - mean) * scale, scale


def norm_back(grad, normed, scale):
    return scale * (
        grad
        - jnp.mean(grad, axis=1, keepdims=True)
        - normed * jnp.mean(grad * normed, axis=1, keepdims=True)
    )


def gelu_parts(pre):
    square = pre * pre
    tanh = jnp.tanh(pre * (gelu_c + gelu_c * gelu_a * square))
    gate = 0.5 + 0.5 * tanh
    slope = gate + pre * (0.5 - 0.5 * tanh * tanh) * (gelu_c + 3.0 * gelu_c * gelu_a * square)
    return pre * gate, slope


def shards(
    tokens,
    class_ids,
    final_scale,
    row_slots,
    class_table,
    ada_weight,
    ada_bias,
    qkv_weight,
    qv_bias,
    log_scale,
    proj_weight,
    proj_bias,
    fc1_weight,
    fc1_bias,
    fc2_weight,
    fc2_bias,
    out_grad,
):
    groups = lax.axis_size("dp")
    bits = groups.bit_length() - 1
    here = lax.axis_index("dp")
    core = lax.axis_index("mp")
    micro, row_len, half = tokens.shape
    width = 2 * half
    share = row_len // groups
    heads = log_scale.shape[0]
    hidden = fc1_weight.shape[1]

    def swap(values):
        return lax.ppermute(values, "mp", [(0, 1), (1, 0)])

    def flip(values, bit):
        return lax.ppermute(values, "dp", [(i, i ^ (1 << bit)) for i in range(groups)])

    def in_order(own, other, axis):
        return jnp.where(
            core == 0,
            jnp.concatenate([own, other], axis),
            jnp.concatenate([other, own], axis),
        )

    class_picks = (
        class_ids.reshape(-1)[:, None] == jnp.arange(class_table.shape[0], dtype=jnp.int32)[None, :]
    )
    condition = dot(class_picks.astype(bf16), class_table)
    lifted = jax.nn.silu(condition).astype(bf16)
    ada_half = lax.dynamic_slice_in_dim(ada_weight, core * half, half, 2)
    ada_terms = dot(lifted, ada_half.reshape(ada_half.shape[0], 6 * half))
    ada_terms = ada_terms.reshape(micro, groups, 6, half)
    ada_round = lax.reduce_precision(ada_terms, 8, 7)
    ada_rest = jnp.stack([ada_terms[:, :, c] - ada_round[:, :, c] for c in (2, 4)], axis=2)
    ada_sent = jnp.concatenate([ada_round, ada_rest], axis=2).astype(bf16)

    def by_target(values):
        return values.reshape(micro, groups, -1, half).swapaxes(0, 1).reshape(2 * groups, -1, half)

    def exchange(values):
        return lax.all_to_all(values, ("dp", "mp"), split_axis=0, concat_axis=0, tiled=True)

    def to_row(values):
        return (
            values.reshape(groups, 2, share, half).transpose(0, 2, 1, 3).reshape(row_len, width)
        )

    first_message = jnp.concatenate([by_target(tokens), by_target(ada_sent)], axis=1)
    arrived = exchange(first_message)

    def after(values, *earlier):
        return lax.optimization_barrier((values, earlier))[0]

    small = jnp.concatenate(
        [ada_bias.reshape(-1), qv_bias.reshape(-1), log_scale, proj_bias, fc1_bias, fc2_bias]
    )
    small_sizes = [6 * half, 2 * half, heads, half, hidden, half]

    def unpack(flat):
        starts = [sum(small_sizes[:i]) for i in range(7)]
        return [flat[starts[i] : starts[i + 1]] for i in range(6)]

    own_small, oth_small = unpack(small), unpack(swap(small))
    qkv_w = [qkv_weight[:, part] for part in range(3)]
    qkv_w += [swap(weight) for weight in qkv_w]
    proj_w = (proj_weight, swap(proj_weight))
    fc1_w = (fc1_weight, swap(fc1_weight))
    fc2_w = (fc2_weight, swap(fc2_weight))
    ada_shift = in_order(own_small[0].reshape(6, half), oth_small[0].reshape(6, half), 1)
    proj_shift = in_order(own_small[3], oth_small[3], 0)
    fc2_shift = in_order(own_small[5], oth_small[5], 0)
    fc1_shift = jnp.stack([own_small[4], oth_small[4]])
    qkv_shift = jnp.stack(
        [
            jnp.concatenate([part[1][:half], jnp.zeros((half,), f32), part[1][half:]])
            for part in (own_small, oth_small)
        ]
    )
    head_mult = jnp.stack([jnp.repeat(jnp.exp(part[2]), HEAD_DIM) for part in (own_small, oth_small)])

    segments, levels = slot_layout(
        lax.dynamic_index_in_dim(final_scale[:, 0], core, 0, keepdims=False),
        lax.dynamic_index_in_dim(row_slots[:, 0], core, 0, keepdims=False),
    )
    mask = (
        (segments[:, None] == segments[None, :]) & (levels[:, None] <= levels[None, :])
    ).astype(f32)

    grads_arrived = exchange(
        after(by_target(out_grad), arrived, qkv_shift, head_mult, mask, proj_shift, fc1_shift, fc2_shift)
    )

    def array(*dims, kind=bf16):
        return jax.ShapeDtypeStruct(dims, kind)

    vmem, dma = pltpu.VMEM, pltpu.SemaphoreType.DMA

    def scratch(arrays):
        return [vmem(value.shape, value.dtype) for value in arrays]

    wide = array(2, row_len, half)
    wide32 = array(2, row_len, half, kind=f32)
    whole_tiles = share % 16 == 0
    if whole_tiles:
        row_in, ada_in = arrived, ada_shift
    else:
        row_in = to_row(arrived[:, :share])
        terms = jnp.sum(arrived[:, share:].reshape(groups, 2, 8, half).astype(f32), axis=0)
        terms = terms.transpose(1, 0, 2).reshape(8, width)
        ada_in = (ada_shift + terms[:6]).at[2].add(terms[6]).at[4].add(terms[7])
    kept = [
        array(row_len, width),
        wide,
        wide,
        wide,
        wide32,
        wide32,
        array(2 * heads, row_len, row_len, kind=f32),
        array(row_len, half),
        array(row_len, half),
        array(row_len, width, kind=f32),
        array(row_len, width, kind=f32),
        array(row_len, width),
        array(row_len, hidden),
        array(row_len, hidden // 2),
        array(row_len, hidden // 2),
        array(row_len, hidden),
        array(row_len, hidden),
    ]
    h1, qn, kn, vn, rq, rk, probs, mixed0, mixed1, attn, middle, h2, act0, *more = local_call(
        functools.partial(forward_kernel, share if whole_tiles else 0),
        61,
        kept + [array(row_len, width), array(6, width, kind=f32)],
        scratch(kept)
        + [
            vmem((2, 3, width, half), bf16),
            vmem((2, half, width), bf16),
            vmem((2, width, hidden), bf16),
            vmem((row_len, 3 * half), f32),
            dma((10,)),
            dma((23,)),
        ],
        "vvvvvvv" + "h" * 10,
        row_in,
        ada_in,
        qkv_shift,
        head_mult,
        mask,
        proj_shift[None],
        fc1_shift,
        *qkv_w,
        *proj_w,
        *fc1_w,
        out_kind="h" * len(kept) + "vv",
    )
    act1, (slope0, slope1, resident, mods) = more[:2], more[2:]

    own_bits = jnp.stack([(here >> bit) & 1 for bit in range(bits)])
    part = width // groups

    def source(near_left, far_left, near_right, sent_right):
        return (near_left, far_left, near_right, *[swap(values) for values in sent_right])

    def scatter_start(*sources):
        count = len(sources)
        pieces = [len(source) - 3 for source in sources]
        columns = sum(source[2].shape[1] for source in sources) // 2
        ins = [value for source in sources for value in source]
        kept = [array(groups, part, 2 * row_len)] * count + [
            array(groups // 2, part, columns)
        ] * 2
        outs = local_call(
            functools.partial(grad_kernel, pieces),
            61,
            [array(1, width, kind=f32)] * count
            + [array(1, source[2].shape[1], kind=f32) for source in sources]
            + kept,
            scratch(ins)
            + scratch(kept)
            + [
                vmem((count, groups // 2, part, 2 * row_len), bf16),
                dma((len(ins),)),
                dma((len(kept),)),
            ],
            "s" + "h" * len(ins),
            own_bits,
            *ins,
            out_kind="v" * (2 * count) + "h" * len(kept),
        )
        left_sums, right_sums = outs[:count], outs[count : 2 * count]
        rest = list(outs[2 * count : 3 * count])
        rest += [value for source in sources for value in source[2:]]
        return left_sums, right_sums, (pieces, rest), tuple(outs[3 * count :])

    def travel(sent):
        return flip(sent[0], 0), flip(sent[1], 1)

    def scatter_second(started, came, flops=1):
        pieces, rest = started
        count = len(pieces)
        columns = came[0].shape[2]
        ins = [*rest, *came]
        kept = [array(groups // 4, part, columns)] * 2 + [array(groups // 4, part, 2 * columns)]
        sent_a, sent_b, own = local_call(
            functools.partial(second_kernel, pieces),
            61,
            kept,
            scratch(ins)
            + scratch(kept)
            + [
                vmem((count, groups // 2, part, 2 * row_len), bf16),
                dma((len(ins),)),
                dma((3,)),
            ],
            "s" + "h" * len(ins),
            own_bits,
            *ins,
            out_kind="h",
            flops=flops,
        )
        return own, (sent_a, sent_b)

    def scatter_more(bit, own, came):
        rows, _, columns = own.shape
        sent, own = local_call(
            functools.partial(third_kernel, bit),
            61,
            [
                array(rows // 2, part, columns),
                array(rows // 2, part, columns, kind=f32 if bit == bits - 1 else bf16),
            ],
            [],
            "sv" + "v" * len(came),
            own_bits,
            own,
            *came,
        )
        return own, sent

    def scatter_end(begin, own, came):
        for bit in range(begin, bits):
            own, sent = scatter_more(bit, own, came)
            came = (flip(sent, bit),)
        return own[0] + came[0][0].astype(f32)

    grad_out = to_row(after(grads_arrived, act0))
    grad_branch = (mods[1:2] * grad_out.astype(f32)).astype(bf16)
    fc2_left, _, fc2_rest, fc2_sent = scatter_start(
        source(grad_branch, swap(grad_branch), act0, act1)
    )
    h1_far, h2_far, mixed_far = swap(h1), swap(h2), swap(mixed1)
    fc2_came = travel(fc2_sent)

    pre_kept = [array(row_len, hidden)] + [array(row_len, hidden // 2)] * 2
    branch_ins = [act0, *act1, grad_out, middle]
    pre0, *pre1, output, branch_mods = local_call(
        hidden_back_kernel,
        61,
        pre_kept + [array(row_len, width), array(1, width, kind=f32)],
        scratch(pre_kept)
        + [vmem((2, row_len, hidden), bf16), vmem((2, hidden, width), bf16)]
        + scratch(branch_ins)
        + [dma((13,)), dma((3,))],
        "vvv" + "h" * 9,
        after(grad_branch, fc2_sent, h1_far, h2_far, mixed_far),
        mods,
        fc2_shift[None],
        slope0,
        slope1,
        *fc2_w,
        *branch_ins,
        out_kind="hhhvv",
    )
    _, fc1_right, fc1_rest, fc1_sent = scatter_start(
        source(h2, h2_far, pre0, pre1)
    )
    fc1_came = travel(fc1_sent)
    def to_target(values):
        return (
            values.reshape(groups, share, 2, half).transpose(0, 2, 1, 3).reshape(-1, share, half)
        )

    fc2_own, fc2_sent = scatter_second(fc2_rest, after(fc2_came, fc1_sent), int(3e9))
    fc2_came = travel(fc2_sent[::-1])[::-1]
    row_ins = [
        after(pre0, fc2_sent),
        fc1_w[0],
        *pre1,
        fc1_w[1],
        middle,
        grad_out,
        attn,
        *proj_w,
        qn,
        kn,
        vn,
        probs,
        rq,
        rk,
    ]
    row_kept = [
        array(row_len, width, kind=f32),
        array(row_len, width),
        array(row_len, 3 * half),
        array(row_len, 3 * half // 2),
        array(row_len, 3 * half // 2),
        array(4, width, kind=f32),
    ]
    middle_grad, attn_grad, qkv_grad0, qkv1a, qkv1b, row_mods = local_call(
        row_back_kernel,
        61,
        row_kept,
        scratch(row_kept)
        + scratch(row_ins)
        + [vmem((row_len, width), f32), vmem((row_len, half), bf16), dma((16,)), dma((6,))],
        "vv" + "h" * 16,
        mods,
        head_mult,
        *row_ins,
        out_kind="h",
    )
    fc1_own, fc1_sent = scatter_second(fc1_rest, after(fc1_came, attn_grad))
    ready = after((qkv1a, qkv1b, attn_grad), fc2_came, fc1_sent)
    fc1_came = travel(fc1_sent[::-1])[::-1]
    fc2_own, fc2_sent = scatter_more(2, fc2_own, fc2_came)
    fc2_came = (flip(fc2_sent, 2),)
    qkv_left, qkv_right, qkv_rest, qkv_sent = scatter_start(
        after(source(h1, h1_far, qkv_grad0, ready[:2]), fc2_sent),
        (attn_grad, swap(ready[2]), mixed0, mixed_far),
    )
    qkv_came = travel(qkv_sent)
    fc2_own, fc2_sent = scatter_more(3, fc2_own, after(fc2_came, qkv_sent))
    fc2_came = (flip(fc2_sent, 3),)
    end_ins = [
        after(qkv_grad0, fc1_came, fc2_sent),
        qkv1a,
        qkv1b,
        resident,
        middle_grad,
        *qkv_w,
    ]
    tokens_grad, end_mods = local_call(
        input_back_kernel,
        61,
        [array(row_len, width), array(2, width, kind=f32)],
        scratch(end_ins) + [vmem((row_len, width), f32), dma((11,))],
        "v" + "h" * 11,
        mods,
        *end_ins,
        flops=int(2e9),
    )

    row_grads = jnp.stack(
        [row_mods[2], branch_mods[0], end_mods[0], row_mods[0], end_mods[1], row_mods[1]]
    ).astype(bf16)
    scale_terms = jnp.sum(row_mods[3].reshape(2, heads, HEAD_DIM), axis=2)
    scale_sum = scale_terms[0] + swap(scale_terms[1])

    def own_half(values):
        return lax.dynamic_slice_in_dim(values, core * half, half, 0)

    bias_sum = jnp.concatenate(
        [
            qkv_right[0][0, :half],
            qkv_right[0][0, 2 * half :],
            own_half(qkv_left[1][0]),
            fc1_right[0][0],
            own_half(fc2_left[0][0]),
            scale_sum,
        ]
    )

    def double(gathered, bias_sum, bit):
        rounded = bias_sum.astype(bf16)
        count = gathered.size
        came = flip(jnp.concatenate([gathered.reshape(-1), rounded]), bit)
        theirs = came[:count].reshape(gathered.shape)
        mine = (here >> bit) & 1
        both = jnp.where(mine == 0, jnp.stack([gathered, theirs]), jnp.stack([theirs, gathered]))
        return both, rounded.astype(f32) + came[count:].astype(f32)

    returned = exchange(
        jnp.concatenate([to_target(values) for values in (output, tokens_grad)], axis=1)
    )
    qkv_own, qkv_sent = scatter_second(qkv_rest, after(qkv_came, fc1_came, fc2_came, tokens_grad))
    qkv_came = travel(qkv_sent[::-1])[::-1]
    fc1_own, fc1_sent = scatter_more(2, fc1_own, after(fc1_came, qkv_sent))
    fc1_came = (flip(fc1_sent, 2),)
    gathered = after(row_grads, qkv_sent).reshape(6 * width)
    for bit in (2, 0):
        gathered, bias_sum = double(gathered, bias_sum, bit)
    qkv_own, qkv_sent = scatter_more(2, qkv_own, after(qkv_came, fc1_came, gathered, returned))
    qkv_came = (flip(qkv_sent, 2),)
    fc1_own, fc1_sent = scatter_more(3, fc1_own, after(fc1_came, qkv_sent))
    fc1_came = (flip(fc1_sent, 3),)
    gathered = after(gathered, fc1_sent)
    for bit in [1] + list(range(3, bits)):
        gathered, bias_sum = double(gathered, bias_sum, bit)
    order = list(range(bits - 1, 2, -1)) + [1, 0, 2]
    gathered = gathered.transpose(
        *[order.index(bit) for bit in range(bits - 1, -1, -1)], bits
    ).reshape(groups, 6 * width)
    qkv_own, qkv_sent = scatter_more(3, qkv_own, after(qkv_came, fc1_came, gathered))
    qkv_came = (flip(qkv_sent, 3),)
    gathered = after(gathered, qkv_sent)
    gathered = in_order(gathered, swap(gathered), 0)
    fc2_sum = scatter_end(4, fc2_own, fc2_came)
    fc1_sum = scatter_end(4, fc1_own, fc1_came)
    qkv_sum = scatter_end(4, qkv_own, qkv_came)

    ada_weight_grad = dot_tn(lifted, gathered).reshape(ada_weight.shape)
    ada_bias_grad = jnp.sum(gathered.astype(f32), axis=0).reshape(6, width)
    grad_lifted = dot_nt(gathered, ada_weight.reshape(ada_weight.shape[0], 6 * width))
    _, silu_pull = jax.vjp(jax.nn.silu, condition)
    table_grad = lax.dot_general(
        class_picks.astype(f32),
        silu_pull(grad_lifted)[0],
        (((0,), (0,)), ((), ())),
        precision=lax.Precision.HIGHEST,
    )

    def from_rows(values):
        return values.reshape(groups, 2, share, half).swapaxes(0, 1).reshape(2, row_len, half)

    qkv_cols, proj_cols = 3 * half // 2, half // 2
    turn = qkv_cols + proj_cols
    qkv_own_sum = jnp.concatenate([qkv_sum[:, :qkv_cols], qkv_sum[:, turn : turn + qkv_cols]], 1)
    proj_sum = jnp.concatenate([qkv_sum[:, qkv_cols:turn], qkv_sum[:, turn + qkv_cols :]], 1)
    ends = [half, 2 * half, 3 * half, 3 * half + hidden, 4 * half + hidden]
    return (
        from_rows(returned[:, :share]),
        from_rows(returned[:, share:]),
        table_grad,
        ada_weight_grad,
        ada_bias_grad,
        qkv_own_sum.reshape(-1, 3, half),
        bias_sum[: ends[1]].reshape(2, half),
        bias_sum[ends[4] :],
        proj_sum.T,
        bias_sum[ends[1] : ends[2]],
        fc1_sum,
        bias_sum[ends[2] : ends[3]],
        fc2_sum.T,
        bias_sum[ends[3] : ends[4]],
    )


def solution(mesh):
    placed = (
        P(None, "dp", "mp"),
        P(),
        P(None, "dp", None),
        P(None, "dp", None),
        P(None, "dp"),
        P("dp", None, None),
        P(None, "mp"),
        P(None, None, "mp"),
        P(None, "mp"),
        P("mp"),
        P("mp", None),
        P("mp"),
        P(None, "mp"),
        P("mp"),
        P("mp", None),
        P("mp"),
        P(None, "dp", "mp"),
    )
    return jax.shard_map(
        shards,
        mesh=mesh,
        in_specs=placed,
        out_specs=(
            P(None, "dp", "mp"),
            P(None, "dp", "mp"),
            P(None, "dp"),
            P("dp", None, None),
            P(),
            P("dp", None, "mp"),
            P(None, "mp"),
            P("mp"),
            P("mp", "dp"),
            P("mp"),
            P("dp", "mp"),
            P("mp"),
            P("mp", "dp"),
            P("mp"),
        ),
        check_vma=False,
    )
```
